32 devices in a mesh: dp: 16 (over z, x, core), tensor: 2 (over y).
Axes of the slice: x: 2, y: 2, z: 4, core: 2. Of those that a mesh axis runs over, the one named last changes fastest.
Arguments:
- tokens: bfloat16 [12288, 1152], P(('dp', 'tensor')), may hold values from -6 to 6
- conditions: bfloat16 [48, 1152], P('dp'), may hold values from -6 to 6
- item_grids: int32 [48, 2], P('dp'), may hold values from 8 to 32, as said below
- mod_weight: bfloat16 [1152, 6912], P('dp'), may hold values from -0.25 to 0.25
- query_weight: bfloat16 [1152, 1152], P(None, 'tensor'), may hold values from -0.1875 to 0.1875
- key_weight: bfloat16 [1152, 1152], P(None, 'tensor'), may hold values from -0.1875 to 0.1875
- value_weight: bfloat16 [1152, 1152], P(None, 'tensor'), may hold values from -0.1875 to 0.1875
- proj_weight: bfloat16 [1152, 1152], P('tensor'), may hold values from -0.75 to 0.75
- query_gain: float32 [72], replicated, may hold values from 0.8 to 2
- key_gain: float32 [72], replicated, may hold values from 0.8 to 2
- gate_weight: bfloat16 [1152, 3072], P(None, 'tensor'), may hold values from -0.1875 to 0.1875
- up_weight: bfloat16 [1152, 3072], P(None, 'tensor'), may hold values from -0.1875 to 0.1875
- down_weight: bfloat16 [3072, 1152], P('tensor'), may hold values from -0.21875 to 0.21875
- out_grad: bfloat16 [12288, 1152], P(('dp', 'tensor')), may hold values from -6 to 6
Outputs:
- block_out: bfloat16 [12288, 1152], P(('dp', 'tensor'))
- grad_tokens: bfloat16 [12288, 1152], P(('dp', 'tensor'))
- grad_conditions: float32 [48, 1152], P('dp')
- grad_mod_weight: float32 [1152, 6912], P('dp')
- grad_query_weight: float32 [1152, 1152], P('dp', 'tensor')
- grad_key_weight: float32 [1152, 1152], P('dp', 'tensor')
- grad_value_weight: float32 [1152, 1152], P('dp', 'tensor')
- grad_proj_weight: float32 [1152, 1152], P('tensor', 'dp')
- grad_query_gain: float32 [72], replicated
- grad_key_gain: float32 [72], replicated
- grad_gate_weight: float32 [1152, 3072], P('dp', 'tensor')
- grad_up_weight: float32 [1152, 3072], P('dp', 'tensor')
- grad_down_weight: float32 [3072, 1152], P('tensor', 'dp')
The draws below stay inside these ranges and needn't reach their ends.
Inputs may be any that keep to these rules, and one draw needn't show every extreme that they name: `item_grids`: every item is (12, 20), (16, 16) or (8, 32) patches; each packed row holds exactly 3 items laid end to end from its first token in order, and the rest of the row is padding.
All inputs are finite; a program needn't handle non-finite values.
Results may differ from the reference program's by a relative error of at most 0.02.
Values may be sent and summed in bfloat16 or wider, within the bound.
A program may use at most 256 MiB of HBM per device.

```python
import jax
import jax.numpy as jnp
from jax import lax

D = 1152
HEADS = 16
HD = 72
FF = 3072
SIDE = 16
SEGS = 3
ROW = 768
TOKENS = 12288
ITEMS = 48


def draw_item_grids(key, part):
    key = jax.random.fold_in(key, 7)
    item_kinds = jax.random.randint(key, (ITEMS,), 0, 3)
    chosen = jax.random.randint(jax.random.fold_in(key, 1), (), 0, ITEMS)
    item_kinds = jnp.where(jnp.arange(ITEMS) == chosen, 2, item_kinds)
    heights = jnp.where(item_kinds == 0, 3 * SIDE // 4, jnp.where(item_kinds == 1, SIDE, SIDE // 2))
    widths = jnp.where(item_kinds == 0, 5 * SIDE // 4, jnp.where(item_kinds == 1, SIDE, 2 * SIDE))
    return jnp.stack([heights, widths], axis=1).astype(jnp.int32)


def raised(array, own_key, source, target, shards_of, factor):
    def block_of(position):
        return (jnp.arange(array.shape[position]) // (array.shape[position] // shards_of)).reshape((-1,) + (1,) * (array.ndim - 1 - position))

    first = jax.random.permutation(own_key, shards_of)[block_of(target)]
    far = (block_of(target) + shards_of // 2) % shards_of
    return jnp.where((block_of(source) == first) | (block_of(source) == far), factor * array, array)


def block_scale(own_key, dims, cuts, low, high):
    def one(dim, shards_of):
        draws = jax.random.uniform(jax.random.fold_in(jax.random.fold_in(own_key, 6), dim), (shards_of,), jnp.float32, low / len(cuts), high / len(cuts))
        return jnp.repeat(jnp.exp(draws), dims[dim] // shards_of).reshape((-1,) + (1,) * (len(dims) - dim - 1))

    factor_of = one(*cuts[0])
    for cut in cuts[1:]:
        factor_of = factor_of * one(*cut)
    return factor_of


def normal_values(own_key, extent, width, reach, shards=(), kind=jnp.bfloat16):
    result = jax.random.normal(own_key, extent, jnp.float32) * width
    if len(shards) > 0:
        result = block_scale(own_key, extent, shards, -0.22, 0.18) * result
    return jnp.clip(result, min=-reach, max=reach).astype(kind)


def gaussian_with(rng, extent, deviation, limit, cuts, heavy, kind=jnp.bfloat16):
    entries = deviation * jax.random.normal(rng, extent, jnp.float32)
    if cuts:
        entries = entries * block_scale(rng, extent, cuts, -0.22, 0.18)
    return jnp.clip(raised(entries, jax.random.fold_in(rng, 3), *heavy), -limit, limit).astype(kind)


def setup_inputs(seed: int = 0) -> dict:
    splits = jax.random.split(jax.random.key(seed), 15)
    tokens = gaussian_with(splits[0], (TOKENS, D), 1.0, 6.0, ((0, 32),), (0, 1, 32, 2.75))
    conditions = gaussian_with(splits[1], (ITEMS, D), 1.0, 6.0, ((0, 16),), (0, 1, 16, 2.0))
    item_grids = draw_item_grids(jax.random.fold_in(splits[14], 71), 0)
    mod_weight = normal_values(splits[3], (D, 6 * D), (D // 2) ** -0.5, 0.25, ((0, 16),))
    query_weight = normal_values(splits[4], (D, D), D ** -0.5, 0.1875, ((1, 2),))
    key_weight = normal_values(splits[5], (D, D), D ** -0.5, 0.1875, ((1, 2),))
    value_weight = normal_values(splits[6], (D, D), D ** -0.5, 0.1875, ((1, 2),))
    proj_weight = normal_values(splits[7], (D, D), (D // 16) ** -0.5, 0.75, ((0, 2),))
    query_gain = jnp.clip(jax.random.uniform(splits[8], (HD,), jnp.float32, 0.8, 2.0), 0.8, 2.0)
    key_gain = jnp.clip(jax.random.uniform(splits[9], (HD,), jnp.float32, 0.8, 2.0), 0.8, 2.0)
    gate_weight = normal_values(splits[10], (D, FF), D ** -0.5, 0.1875, ((1, 2),))
    up_weight = normal_values(splits[11], (D, FF), D ** -0.5, 0.1875, ((1, 2),))
    down_weight = normal_values(splits[12], (FF, D), (FF // 4) ** -0.5, 0.21875, ((0, 2),))
    out_grad = gaussian_with(splits[13], (TOKENS, D), 1.0, 6.0, ((0, 32),), (0, 1, 32, 2.75))
    return dict(tokens=tokens, conditions=conditions, item_grids=item_grids, mod_weight=mod_weight, query_weight=query_weight, key_weight=key_weight, value_weight=value_weight, proj_weight=proj_weight, query_gain=query_gain, key_gain=key_gain, gate_weight=gate_weight, up_weight=up_weight, down_weight=down_weight, out_grad=out_grad)


EPSILON = 1e-06
HIGH = lax.Precision.HIGHEST

@jax.custom_vjp
def low(v):
    return lax.optimization_barrier(v.astype(jnp.bfloat16)).astype(jnp.float32)

@jax.custom_vjp
def low_back(v):
    return v

def low_keep(v):
    return (low(v), None)

def low_pass(kept, grad):
    return (grad,)

def back_keep(v):
    return (v, None)

def back_low(kept, grad):
    return (low(grad),)
low.defvjp(low_keep, low_pass)
low_back.defvjp(back_keep, back_low)

def matmul(left, right):
    return jnp.dot(left, right, precision=HIGH, preferred_element_type=jnp.float32)

def geometry(row_grids, length):
    heights = row_grids[:, 0]
    widths = row_grids[:, 1]
    item_sizes = (heights * widths).astype(jnp.int32)
    item_ends = jnp.cumsum(item_sizes).astype(jnp.int32)
    starts = (item_ends - item_sizes).astype(jnp.int32)
    positions = jnp.arange(length, dtype=jnp.int32)
    member = (positions[:, None] >= starts[None, :]) & (positions[:, None] < item_ends[None, :])
    member_int = member.astype(jnp.int32)
    item_count = row_grids.shape[0]
    valid_tok = lax.optimization_barrier(jnp.sum(member_int, axis=1)).astype(jnp.int32) > 0
    item_index = lax.optimization_barrier(jnp.sum(member_int * jnp.arange(item_count, dtype=jnp.int32)[None, :], axis=1)).astype(jnp.int32)
    segment = jnp.where(valid_tok, item_index, item_count)
    local_index = (positions - lax.optimization_barrier(jnp.sum(member_int * starts[None, :], axis=1))).astype(jnp.int32)
    width_tok = jnp.maximum(lax.optimization_barrier(jnp.sum(member_int * widths[None, :], axis=1)).astype(jnp.int32), 1)
    row_pos = (local_index // width_tok).astype(jnp.int32)
    col_pos = (local_index % width_tok).astype(jnp.int32)
    allowed = (segment[:, None] == segment[None, :]) & valid_tok[None, :] | (positions[:, None] == positions[None, :])
    return (member.astype(jnp.float32), allowed, row_pos, col_pos)

def rope_tables(row_pos, col_pos, head_dim):
    quarter = head_dim // 4
    frequency = 10000.0 ** (-jnp.arange(quarter, dtype=jnp.float32) / quarter)
    along_rows = row_pos.astype(jnp.float32)[:, None] * frequency[None, :]
    along_cols = col_pos.astype(jnp.float32)[:, None] * frequency[None, :]
    angles = jnp.concatenate([along_rows, along_rows, along_cols, along_cols], axis=1)
    return (jnp.cos(angles)[:, None, :], jnp.sin(angles)[:, None, :])

def rotate(values):
    dims_in = values.shape
    quarter = dims_in[2] // 4
    halves_view = values.reshape(dims_in[0], dims_in[1], 2, 2, quarter)
    turned = jnp.concatenate([-halves_view[:, :, :, 1:2], halves_view[:, :, :, 0:1]], axis=3)
    return turned.reshape(dims_in)

def layer_norm(values):
    centred = values - lax.optimization_barrier(jnp.mean(values, axis=1, keepdims=True))
    return centred * lax.rsqrt(lax.optimization_barrier(jnp.mean(centred * centred, axis=1, keepdims=True)) + EPSILON)

def norm_rotate(projected, gain, cosine, sine):
    length = projected.shape[0]
    shaped = projected.reshape(length, HEADS, HD)
    normed = shaped * lax.rsqrt(lax.optimization_barrier(jnp.mean(shaped * shaped, axis=2, keepdims=True)) + EPSILON) * gain
    turned = normed * cosine + rotate(normed) * sine
    return turned.reshape(length, HEADS * HD)

def attention(queries, keys, values, allowed):
    length = queries.shape[0]
    shaped = (length, HEADS, HD)
    scores = jnp.einsum('qhd,khd->hqk', queries.reshape(shaped), keys.reshape(shaped), precision=HIGH) * HD ** (-0.5)
    scores = low_back(scores)
    scores = jnp.where(allowed[None], scores, -1e+30)
    attn_probs = low(jax.nn.softmax(scores, axis=-1))
    head_out = jnp.einsum('hqk,khd->qhd', attn_probs, values.reshape(shaped), precision=HIGH)
    return head_out.reshape(length, HEADS * HD)

def row_forward(row_tokens, row_cond, row_grids, weights):
    mod_weight, query_weight, key_weight, value_weight, proj_weight, query_gain, key_gain, gate_weight, up_weight, down_weight = weights
    member, allowed, row_pos, col_pos = geometry(row_grids, ROW)
    cosine, sine = rope_tables(row_pos, col_pos, HD)
    modulation = low_back(matmul(low(jax.nn.silu(row_cond)), mod_weight))
    per_token = matmul(member, modulation)
    shift_one, scale_one, gate_one, shift_two, scale_two, gate_two = jnp.split(per_token, 6, axis=1)
    attn_in = low(layer_norm(row_tokens) * (1.0 + scale_one) + shift_one)
    query_pre = low_back(matmul(attn_in, query_weight))
    key_pre = low_back(matmul(attn_in, key_weight))
    value_pre = low_back(matmul(attn_in, value_weight))
    queries = low(norm_rotate(query_pre, query_gain, cosine, sine))
    keys = low(norm_rotate(key_pre, key_gain, cosine, sine))
    values = low(value_pre)
    heads_out = low(low_back(attention(queries, keys, values, allowed)))
    attn_out = low_back(matmul(heads_out, proj_weight))
    resid = row_tokens + gate_one * attn_out
    mlp_in = low(layer_norm(resid) * (1.0 + scale_two) + shift_two)
    gate_pre = low_back(matmul(mlp_in, gate_weight))
    up_pre = low_back(matmul(mlp_in, up_weight))
    hidden = low(jax.nn.silu(gate_pre) * up_pre)
    mlp_out = low_back(matmul(hidden, down_weight))
    return resid + gate_two * mlp_out

def reference(tokens, conditions, item_grids, mod_weight, query_weight, key_weight, value_weight, proj_weight, query_gain, key_gain, gate_weight, up_weight, down_weight, out_grad):
    weights = tuple((weight.astype(jnp.float32) for weight in (mod_weight, query_weight, key_weight, value_weight, proj_weight, query_gain, key_gain, gate_weight, up_weight, down_weight)))
    rows_count = tokens.shape[0] // ROW
    tokens_rows = tokens.astype(jnp.float32).reshape(rows_count, ROW, D)
    cond_rows = conditions.astype(jnp.float32).reshape(rows_count, SEGS, D)
    grid_rows = item_grids.reshape(rows_count, SEGS, 2)

    def forward(tokens_in, cond_in, weights_in):

        def one_row(carry, inputs):
            row_tokens, row_cond, row_grids = inputs
            return (carry, jax.checkpoint(row_forward)(row_tokens, row_cond, row_grids, weights_in))
        carry, rows_out = lax.scan(one_row, jnp.zeros((), jnp.float32), (tokens_in, cond_in, grid_rows))
        return rows_out
    rows_out, pull_back = jax.vjp(forward, tokens_rows, cond_rows, weights)
    grad_rows, grad_cond, grad_weights = pull_back(out_grad.astype(jnp.float32).reshape(rows_count, ROW, D))
    block_out = rows_out.reshape(rows_count * ROW, D).astype(jnp.bfloat16)
    grad_tokens = grad_rows.reshape(rows_count * ROW, D).astype(jnp.bfloat16)
    grad_conditions = grad_cond.reshape(rows_count * SEGS, D)
    return (block_out, grad_tokens, grad_conditions, grad_weights[0], grad_weights[1], grad_weights[2], grad_weights[3], grad_weights[4], grad_weights[5], grad_weights[6], grad_weights[7], grad_weights[8], grad_weights[9])
```

```python
import functools

import jax
import jax.numpy as jnp
from jax import lax
from jax.experimental import pallas as pl
from jax.experimental.pallas import tpu as pltpu
from jax.sharding import PartitionSpec as P

HD = 72
QUARTER = HD // 4
LANES = 128
SPAN = 256
TILE = 256
EPSILON = 1e-06
F32 = jnp.float32
BF16 = jnp.bfloat16
HIGH = lax.Precision.HIGHEST


def silu_grad(values):
    sigma = jax.nn.sigmoid(values)
    return sigma * (1.0 + values * (1.0 - sigma))


def dot(left, right):
    return jnp.dot(left, right, preferred_element_type=F32)


def dot_t(left, right):
    return lax.dot_general(left, right, (((1,), (1,)), ((), ())), preferred_element_type=F32)


def t_dot(left, right):
    return lax.dot_general(left, right, (((0,), (0,)), ((), ())), preferred_element_type=F32)


def geometry(row_grids, length):
    heights = row_grids[:, 0]
    widths = row_grids[:, 1]
    count = row_grids.shape[0]
    sizes = heights * widths
    ends = [sizes[0]]
    for item in range(1, count):
        ends.append(ends[-1] + sizes[item])
    starts = [ends[item] - sizes[item] for item in range(count)]
    positions = jnp.arange(length, dtype=jnp.int32)
    member = jnp.stack(
        [(positions >= starts[item]) & (positions < ends[item]) for item in range(count)], axis=1
    )
    origin = sum(jnp.where(member[:, item], starts[item], 0) for item in range(count))
    width = jnp.maximum(
        sum(jnp.where(member[:, item], widths[item], 0) for item in range(count)), 1
    )
    local = positions - origin
    spans = jnp.stack([jnp.stack(starts), sizes])
    return member.astype(F32), local // width, local % width, spans


def rope_tables(row_pos, col_pos):
    lane = jnp.arange(LANES)
    frequency = 10000.0 ** (-(lane % QUARTER).astype(F32) / QUARTER)
    along = jnp.where(lane[None, :] < 2 * QUARTER, row_pos[:, None], col_pos[:, None])
    angles = along.astype(F32) * frequency[None, :]
    valid = lane[None, :] < HD
    return jnp.where(valid, jnp.cos(angles), 0.0), jnp.where(valid, jnp.sin(angles), 0.0)


def turn(values):
    lane = lax.broadcasted_iota(jnp.int32, values.shape, 1)
    return jnp.where(
        lane % (2 * QUARTER) < QUARTER,
        -pltpu.roll(values, LANES - QUARTER, 1),
        pltpu.roll(values, QUARTER, 1),
    )


def only_head(values):
    lane = lax.broadcasted_iota(jnp.int32, values.shape, 1)
    return jnp.where(lane < HD, values, jnp.zeros_like(values))


def split_heads(wide, store, heads):
    rows = wide.shape[0]
    wide = jnp.concatenate([wide, jnp.zeros((rows, LANES), wide.dtype)], axis=1)
    for head in range(heads):
        store(head, only_head(wide[:, head * HD : head * HD + LANES]))


def attend_kernel(
    heads,
    items,
    spans,
    x_ref,
    wq_ref,
    wk_ref,
    wv_ref,
    gq_ref,
    gk_ref,
    cos_ref,
    sin_ref,
    out_ref,
    qpre_ref,
    kpre_ref,
    q_ref,
    k_ref,
    v_ref,
    probs_ref,
    qraw,
    kraw,
    vraw,
    oraw,
    wide,
):
    length = x_ref.shape[0]
    head = pl.program_id(0)

    @pl.when(head == 0)
    def _():
        for first in range(0, length, TILE):
            rows = pl.ds(first, TILE)
            x = x_ref[rows, :]
            for w_ref, raw in ((wq_ref, qraw), (wk_ref, kraw), (wv_ref, vraw)):

                def store(h, part, raw=raw):
                    raw[h, rows, :] = part.astype(raw.dtype)

                split_heads(dot(x, w_ref[...]), store, heads)

    for raw, pre_ref, low_ref, gain_ref in (
        (qraw, qpre_ref, q_ref, gq_ref),
        (kraw, kpre_ref, k_ref, gk_ref),
    ):
        for first in range(0, length, TILE):
            rows = pl.ds(first, TILE)
            pre = raw[head, rows, :]
            pre_ref[0, rows, :] = pre
            inv = lax.rsqrt(jnp.sum(pre * pre, axis=1, keepdims=True) / HD + EPSILON)
            normed = pre * inv * gain_ref[...]
            low_ref[0, rows, :] = (
                normed * cos_ref[rows, :] + turn(normed) * sin_ref[rows, :]
            ).astype(BF16)
    v_ref[0] = vraw[head]
    oraw[head] = vraw[head].astype(F32)
    row = lax.broadcasted_iota(jnp.int32, (SPAN, SPAN), 0)
    col = lax.broadcasted_iota(jnp.int32, (SPAN, SPAN), 1)
    row_out = lax.broadcasted_iota(jnp.int32, (SPAN, LANES), 0)
    for item in range(items):
        start = pl.multiple_of(spans[0, item], 16)
        size = spans[1, item]
        rows = pl.ds(start, SPAN)
        scores = dot_t(q_ref[0, rows, :], k_ref[0, rows, :]) * HD**-0.5
        scores = jnp.where(col < size, scores, -1e30)
        top = jnp.max(scores, axis=1, keepdims=True)
        weights = jnp.exp(scores - top)
        total = jnp.sum(weights, axis=1, keepdims=True)
        probs = jnp.where(row < size, weights / total, 0.0).astype(BF16)
        probs_ref[0, item] = probs
        mixed = dot(probs, v_ref[0, rows, :])
        oraw[head, rows, :] = jnp.where(row_out < size, mixed, oraw[head, rows, :])

    @pl.when(head == heads - 1)
    def _():
        for h in range(heads):
            wide[:, h * HD : h * HD + HD] = oraw[h][:, :HD]
        out_ref[...] = wide[...].astype(BF16)


def attend_back_kernel(
    heads,
    items,
    spans,
    grad_ref,
    qpre_ref,
    kpre_ref,
    q_ref,
    k_ref,
    v_ref,
    probs_ref,
    gq_ref,
    gk_ref,
    cos_ref,
    sin_ref,
    dq_ref,
    dk_ref,
    dv_ref,
    gain_ref,
    graw,
    dqraw,
    dkraw,
    dvraw,
    wide,
):
    length = grad_ref.shape[0]
    head = pl.program_id(0)

    @pl.when(head == 0)
    def _():
        gain_ref[...] = jnp.zeros_like(gain_ref)
        for first in range(0, length, TILE):
            rows = pl.ds(first, TILE)

            def store(h, part):
                graw[h, rows, :] = part.astype(BF16)

            split_heads(grad_ref[rows, :].astype(F32), store, heads)

    dqraw[head] = jnp.zeros((length, LANES), F32)
    dkraw[head] = jnp.zeros((length, LANES), F32)
    row_all = lax.broadcasted_iota(jnp.int32, (length, LANES), 0)
    used = spans[0, items - 1] + spans[1, items - 1]
    dvraw[head] = jnp.where(row_all >= used, graw[head].astype(F32), 0.0)
    for item in range(items):
        start = pl.multiple_of(spans[0, item], 16)
        rows = pl.ds(start, SPAN)
        probs_low = probs_ref[0, item]
        probs = probs_low.astype(F32)
        grad = graw[head, rows, :]
        grad_probs = dot_t(grad, v_ref[0, rows, :])
        inner = jnp.sum(probs * grad_probs, axis=1, keepdims=True) / jnp.maximum(
            jnp.sum(probs, axis=1, keepdims=True), 0.5
        )
        grad_scores = (probs * (grad_probs - inner)).astype(BF16)
        dqraw[head, rows, :] += dot(grad_scores, k_ref[0, rows, :])
        dkraw[head, rows, :] += t_dot(grad_scores, q_ref[0, rows, :])
        dvraw[head, rows, :] += t_dot(probs_low, grad)

    for raw, pre_ref, g_ref, which in (
        (dqraw, qpre_ref, gq_ref, 0),
        (dkraw, kpre_ref, gk_ref, 1),
    ):
        for first in range(0, length, TILE):
            rows = pl.ds(first, TILE)
            turned = raw[head, rows, :] * HD**-0.5
            normed = turned * cos_ref[rows, :] - turn(turned * sin_ref[rows, :])
            pre = pre_ref[0, rows, :]
            inv = lax.rsqrt(jnp.sum(pre * pre, axis=1, keepdims=True) / HD + EPSILON)
            unit = pre * inv
            gain_ref[which : which + 1, :] += jnp.sum(normed * unit, axis=0, keepdims=True)
            scaled = normed * g_ref[...]
            along = jnp.sum(scaled * unit, axis=1, keepdims=True) / HD
            raw[head, rows, :] = inv * (scaled - unit * along)

    @pl.when(head == heads - 1)
    def _():
        for raw, o_ref in ((dqraw, dq_ref), (dkraw, dk_ref), (dvraw, dv_ref)):
            for h in range(heads):
                wide[:, h * HD : h * HD + HD] = raw[h][:, :HD]
            o_ref[...] = wide[...].astype(BF16)


def whole(shape):
    return pl.BlockSpec(shape, lambda h, spans: (0,) * len(shape))


def per_head(shape):
    return pl.BlockSpec((1,) + shape, lambda h, spans: (h,) + (0,) * len(shape))


def attend(spans, x, wq, wk, wv, gain_q, gain_k, cosine, sine):
    length, width = x.shape
    heads = wq.shape[1] // HD
    items = spans.shape[1]
    head_f32 = jax.ShapeDtypeStruct((heads, length, LANES), F32)
    head_low = jax.ShapeDtypeStruct((heads, length, LANES), BF16)
    return pl.pallas_call(
        functools.partial(attend_kernel, heads, items),
        grid_spec=pltpu.PrefetchScalarGridSpec(
            num_scalar_prefetch=1,
            grid=(heads,),
            in_specs=[
                whole(x.shape),
                whole(wq.shape),
                whole(wk.shape),
                whole(wv.shape),
                whole((1, LANES)),
                whole((1, LANES)),
                whole((length, LANES)),
                whole((length, LANES)),
            ],
            out_specs=[
                whole((length, heads * HD)),
                per_head((length, LANES)),
                per_head((length, LANES)),
                per_head((length, LANES)),
                per_head((length, LANES)),
                per_head((length, LANES)),
                per_head((items, SPAN, SPAN)),
            ],
            scratch_shapes=[
                pltpu.VMEM((heads, length, LANES), F32),
                pltpu.VMEM((heads, length, LANES), F32),
                pltpu.VMEM((heads, length, LANES), BF16),
                pltpu.VMEM((heads, length, LANES), F32),
                pltpu.VMEM((length, heads * HD), F32),
            ],
        ),
        out_shape=[
            jax.ShapeDtypeStruct((length, heads * HD), BF16),
            head_f32,
            head_f32,
            head_low,
            head_low,
            head_low,
            jax.ShapeDtypeStruct((heads, items, SPAN, SPAN), BF16),
        ],
        compiler_params=pltpu.CompilerParams(vmem_limit_bytes=56 * 2**20),
        cost_estimate=pl.CostEstimate(
            flops=2 * length * width * heads * HD * 3 + 4 * heads * items * SPAN * SPAN * LANES,
            bytes_accessed=24 * 2**20,
            transcendentals=heads * items * SPAN * SPAN,
        ),
        name="attend",
    )(spans, x, wq, wk, wv, gain_q, gain_k, cosine, sine)


def attend_back(spans, grad, saved, gain_q, gain_k, cosine, sine):
    length, width = grad.shape
    heads = width // HD
    items = spans.shape[1]
    out = jax.ShapeDtypeStruct((length, width), BF16)
    return pl.pallas_call(
        functools.partial(attend_back_kernel, heads, items),
        grid_spec=pltpu.PrefetchScalarGridSpec(
            num_scalar_prefetch=1,
            grid=(heads,),
            in_specs=[
                whole(grad.shape),
                per_head((length, LANES)),
                per_head((length, LANES)),
                per_head((length, LANES)),
                per_head((length, LANES)),
                per_head((length, LANES)),
                per_head((items, SPAN, SPAN)),
                whole((1, LANES)),
                whole((1, LANES)),
                whole((length, LANES)),
                whole((length, LANES)),
            ],
            out_specs=[
                whole((length, width)),
                whole((length, width)),
                whole((length, width)),
                whole((8, LANES)),
            ],
            scratch_shapes=[
                pltpu.VMEM((heads, length, LANES), BF16),
                pltpu.VMEM((heads, length, LANES), F32),
                pltpu.VMEM((heads, length, LANES), F32),
                pltpu.VMEM((heads, length, LANES), F32),
                pltpu.VMEM((length, width), F32),
            ],
        ),
        out_shape=[out, out, out, jax.ShapeDtypeStruct((8, LANES), F32)],
        compiler_params=pltpu.CompilerParams(vmem_limit_bytes=56 * 2**20),
        cost_estimate=pl.CostEstimate(
            flops=8 * heads * items * SPAN * SPAN * LANES,
            bytes_accessed=24 * 2**20,
            transcendentals=0,
        ),
        name="attend_back",
    )(spans, grad, *saved, gain_q, gain_k, cosine, sine)


def layer_norm(values):
    centred = values - jnp.mean(values, axis=1, keepdims=True)
    inv_std = lax.rsqrt(jnp.mean(centred * centred, axis=1, keepdims=True) + EPSILON)
    return (centred * inv_std, inv_std)


def norm_back(grad_norm, normed, inv_std):
    return inv_std * (
        grad_norm
        - jnp.mean(grad_norm, axis=1, keepdims=True)
        - normed * jnp.mean(grad_norm * normed, axis=1, keepdims=True)
    )


def per_token(member, rows):
    return sum(member[:, item, None] * rows[item][None, :] for item in range(rows.shape[0]))


def per_item(member, values):
    return jnp.stack(
        [jnp.sum(member[:, item, None] * values, axis=0) for item in range(member.shape[1])]
    )


def swap(values):
    return lax.ppermute(values, "tensor", [(0, 1), (1, 0)])


def in_order(own, other, second):
    return jnp.concatenate([jnp.where(second, other, own), jnp.where(second, own, other)])


def halving_rows(values, bits):
    dp = 2**bits
    depth = values.shape[1] // dp
    blocks = values.T.reshape((2,) * bits + (depth, values.shape[0]))
    me = lax.axis_index("dp")
    for bit in range(bits):
        axis = bits - 1 - bit
        blocks = jnp.where((me >> bit) & 1 == 1, jnp.flip(blocks, axis), blocks)
    blocks = blocks.transpose(tuple(range(bits - 1, -1, -1)) + (bits, bits + 1))
    return blocks.reshape(dp * depth, values.shape[0])


def first_halving(rows, grads):
    half = rows.shape[0] // 2
    sent = lax.ppermute(dot(rows[half:], grads).astype(BF16), "dp", partners(0))
    return (dot(rows[:half], grads) + sent.astype(F32)).astype(BF16)


def partners(bit):
    return [(i, i ^ (1 << bit)) for i in range(lax.axis_size("dp"))]


def rest_of_halving(part, bits):
    for bit in range(1, bits):
        half = part.shape[0] // 2
        sent = lax.ppermute(part[half:], "dp", partners(bit))
        part = part[:half].astype(F32) + sent.astype(F32)
        if bit < bits - 1:
            part = part.astype(BF16)
    return part.astype(F32)


def shards(
    tokens,
    conditions,
    item_grids,
    mod_weight,
    query_weight,
    key_weight,
    value_weight,
    proj_weight,
    query_gain,
    key_gain,
    gate_weight,
    up_weight,
    down_weight,
    out_grad,
):
    half, width = tokens.shape
    length = 2 * half
    dp = lax.axis_size("dp")
    bits = dp.bit_length() - 1
    me = lax.axis_index("dp")
    second = lax.axis_index("tensor") == 1
    own_first = lax.axis_index("tensor") * half
    other_first = half - own_first
    items = conditions.shape[0]
    owned = mod_weight.shape[0]

    tokens_other = swap(tokens)
    out_grad_other = swap(out_grad)

    member, row_pos, col_pos, spans = geometry(item_grids, length)
    cosine, sine = rope_tables(row_pos, col_pos)
    gain_q = jnp.pad(query_gain, (0, LANES - HD))[None, :]
    gain_k = jnp.pad(key_gain, (0, LANES - HD))[None, :]
    member_own = lax.dynamic_slice_in_dim(member, own_first, half, 0)
    member_other = lax.dynamic_slice_in_dim(member, other_first, half, 0)

    cond_all = lax.all_gather(conditions, "dp", axis=0, tiled=True)
    mod_in_all = jax.nn.silu(cond_all.astype(F32)).astype(BF16)
    mod_in_own = lax.dynamic_slice_in_dim(mod_in_all, me * owned, owned, 1)
    mod_part = dot(mod_in_own, mod_weight)
    mod_parts = lax.all_to_all(
        mod_part.reshape(dp, items, 6 * width), "dp", split_axis=0, concat_axis=0, tiled=True
    )
    modulation = jnp.sum(mod_parts.astype(F32), axis=0)
    shift_one, scale_one, gate_one, shift_two, scale_two, gate_two = jnp.split(
        modulation, 6, axis=1
    )

    tokens_float = tokens.astype(F32)
    tokens_all = in_order(tokens, tokens_other, second).astype(F32)
    norm_all, _ = layer_norm(tokens_all)
    attn_in = (
        norm_all * (1.0 + per_token(member, scale_one)) + per_token(member, shift_one)
    ).astype(BF16)

    heads_out, *saved = attend(
        spans, attn_in, query_weight, key_weight, value_weight, gain_q, gain_k, cosine, sine
    )
    heads_other = lax.dynamic_slice_in_dim(heads_out, other_first, half, 0)
    heads_own = lax.dynamic_slice_in_dim(heads_out, own_first, half, 0)
    attn_recv = swap(dot(heads_other, proj_weight).astype(BF16))
    attn_out = dot(heads_own, proj_weight) + attn_recv.astype(F32)

    gate_one_own = per_token(member_own, gate_one)
    scale_two_own = per_token(member_own, scale_two)
    resid = tokens_float + gate_one_own * attn_out
    norm_two, inv_two = layer_norm(resid)
    mlp_in = (norm_two * (1.0 + scale_two_own) + per_token(member_own, shift_two)).astype(BF16)
    mlp_in_all = jnp.concatenate([mlp_in, swap(mlp_in)])

    grad_out = out_grad.astype(F32)
    gate_two_own = per_token(member_own, gate_two)
    grad_mlp_all = jnp.concatenate(
        [
            (gate_two_own * grad_out).astype(BF16),
            (per_token(member_other, gate_two) * out_grad_other.astype(F32)).astype(BF16),
        ]
    )
    grad_hidden = dot_t(grad_mlp_all, down_weight)

    gate_pre = dot(mlp_in_all, gate_weight)
    up_pre = dot(mlp_in_all, up_weight)
    silu_gate = jax.nn.silu(gate_pre)
    hidden = (silu_gate * up_pre).astype(BF16)
    grad_gate_pre = (grad_hidden * up_pre * silu_grad(gate_pre)).astype(BF16)
    grad_up_pre = (grad_hidden * silu_gate).astype(BF16)

    back_other = dot_t(grad_gate_pre[half:], gate_weight) + dot_t(grad_up_pre[half:], up_weight)
    back_recv = swap(back_other.astype(BF16))
    mlp_recv = swap(dot(hidden[half:], down_weight).astype(BF16))
    grad_mlp_in = (
        dot_t(grad_gate_pre[:half], gate_weight)
        + dot_t(grad_up_pre[:half], up_weight)
        + back_recv.astype(F32)
    )

    grad_mlp_rows = halving_rows(grad_mlp_all, bits)
    mlp_in_rows = halving_rows(mlp_in_all, bits)
    down_part = first_halving(grad_mlp_rows, hidden)
    gate_part = first_halving(mlp_in_rows, grad_gate_pre)
    up_part = first_halving(mlp_in_rows, grad_up_pre)

    mlp_out = dot(hidden[:half], down_weight) + mlp_recv.astype(F32)
    block_out = (resid + gate_two_own * mlp_out).astype(BF16)

    grad_resid = grad_out + norm_back(grad_mlp_in * (1.0 + scale_two_own), norm_two, inv_two)
    grad_attn = (gate_one_own * grad_resid).astype(BF16)
    grad_attn_all = in_order(grad_attn, swap(grad_attn), second)
    grad_heads = dot_t(grad_attn_all, proj_weight).astype(BF16)
    dq, dk, dv, gain_parts = attend_back(spans, grad_heads, saved, gain_q, gain_k, cosine, sine)

    def attn_back(first):
        def rows(array):
            return lax.dynamic_slice_in_dim(array, first, half, 0)

        return (
            dot_t(rows(dq), query_weight)
            + dot_t(rows(dk), key_weight)
            + dot_t(rows(dv), value_weight)
        )

    attn_back_recv = swap(attn_back(other_first).astype(BF16))
    grad_attn_in = attn_back(own_first) + attn_back_recv.astype(F32)
    attn_in_rows = halving_rows(attn_in, bits)
    grad_attn_rows = halving_rows(grad_attn_all, bits)
    attn_parts = jnp.concatenate(
        [
            first_halving(attn_in_rows, dq),
            first_halving(attn_in_rows, dk),
            first_halving(attn_in_rows, dv),
            first_halving(grad_attn_rows, heads_out),
        ],
        axis=1,
    )

    norm_one, inv_one = layer_norm(tokens_float)
    scale_one_own = per_token(member_own, scale_one)
    grad_tokens = (
        grad_resid + norm_back(grad_attn_in * (1.0 + scale_one_own), norm_one, inv_one)
    ).astype(BF16)

    part_mod = jnp.concatenate(
        [
            per_item(member_own, grad_attn_in),
            per_item(member_own, grad_attn_in * norm_one),
            per_item(member_own, grad_resid * attn_out),
            per_item(member_own, grad_mlp_in),
            per_item(member_own, grad_mlp_in * norm_two),
            per_item(member_own, grad_out * mlp_out),
        ],
        axis=1,
    )
    gains = jnp.pad(gain_parts[:2].reshape(1, 2 * LANES), ((0, 0), (0, 6 * width - 2 * LANES)))
    part_small = jnp.concatenate([part_mod, gains]).astype(BF16)
    small = part_small.astype(F32) + swap(part_small).astype(F32)
    small_all = lax.all_gather(small.astype(BF16), "dp", axis=0, tiled=False)
    grad_mod_all = small_all[:, :items].reshape(dp * items, 6 * width)
    grad_gains = jnp.sum(small_all[:, items, : 2 * LANES].astype(F32), axis=0)
    grad_mod_weight = t_dot(mod_in_own, grad_mod_all)
    cond_part = dot_t(grad_mod_all, mod_weight)
    cond_parts = lax.all_to_all(
        cond_part.reshape(dp, items, owned), "dp", split_axis=0, concat_axis=0, tiled=True
    )
    grad_mod_in = cond_parts.transpose(1, 0, 2).reshape(items, dp * owned)
    grad_conditions = silu_grad(conditions.astype(F32)) * grad_mod_in

    grad_down = rest_of_halving(down_part, bits).T
    grad_gate = rest_of_halving(gate_part, bits)
    grad_up = rest_of_halving(up_part, bits)
    attn_sum = rest_of_halving(attn_parts, bits)
    grad_q, grad_k, grad_v, grad_proj = jnp.split(attn_sum, 4, axis=1)
    return (
        block_out,
        grad_tokens,
        grad_conditions,
        grad_mod_weight,
        grad_q,
        grad_k,
        grad_v,
        grad_proj.T,
        grad_gains[:HD],
        grad_gains[LANES : LANES + HD],
        grad_gate,
        grad_up,
        grad_down,
    )


def solution(mesh):
    tokens = P(("dp", "tensor"), None)
    rows = P("dp", None)
    columns = P(None, "tensor")
    inner = P("tensor", None)
    both = P("dp", "tensor")
    turned = P("tensor", "dp")
    return jax.shard_map(
        shards,
        mesh=mesh,
        in_specs=(
            tokens,
            rows,
            rows,
            rows,
            columns,
            columns,
            columns,
            inner,
            P(),
            P(),
            columns,
            columns,
            inner,
            tokens,
        ),
        out_specs=(
            tokens,
            tokens,
            rows,
            rows,
            both,
            both,
            both,
            turned,
            P(),
            P(),
            both,
            both,
            turned,
        ),
        check_vma=False,
    )
```

```python
import functools

import jax
import jax.numpy as jnp
from jax import lax
from jax.experimental import pallas as pl
from jax.experimental.pallas import tpu as pltpu
from jax.sharding import PartitionSpec as P

HD = 72
QUARTER = HD // 4
LANES = 128
SPAN = 256
TILE = 256
EPSILON = 1e-06
F32 = jnp.float32
BF16 = jnp.bfloat16
HIGH = lax.Precision.HIGHEST


def silu_grad(values):
    sigma = jax.nn.sigmoid(values)
    return sigma * (1.0 + values * (1.0 - sigma))


def dot(left, right):
    return jnp.dot(left, right, preferred_element_type=F32)


def dot_t(left, right):
    return lax.dot_general(left, right, (((1,), (1,)), ((), ())), preferred_element_type=F32)


def t_dot(left, right):
    return lax.dot_general(left, right, (((0,), (0,)), ((), ())), preferred_element_type=F32)


def geometry(row_grids, length):
    heights = row_grids[:, 0]
    widths = row_grids[:, 1]
    count = row_grids.shape[0]
    sizes = heights * widths
    ends = [sizes[0]]
    for item in range(1, count):
        ends.append(ends[-1] + sizes[item])
    starts = [ends[item] - sizes[item] for item in range(count)]
    positions = jnp.arange(length, dtype=jnp.int32)
    member = jnp.stack(
        [(positions >= starts[item]) & (positions < ends[item]) for item in range(count)], axis=1
    )
    origin = sum(jnp.where(member[:, item], starts[item], 0) for item in range(count))
    width = jnp.maximum(
        sum(jnp.where(member[:, item], widths[item], 0) for item in range(count)), 1
    )
    local = positions - origin
    spans = jnp.stack([jnp.stack(starts), sizes])
    return member.astype(F32), local // width, local % width, spans


def rope_tables(row_pos, col_pos):
    lane = jnp.arange(LANES)
    frequency = 10000.0 ** (-(lane % QUARTER).astype(F32) / QUARTER)
    along = jnp.where(lane[None, :] < 2 * QUARTER, row_pos[:, None], col_pos[:, None])
    angles = along.astype(F32) * frequency[None, :]
    valid = lane[None, :] < HD
    return jnp.where(valid, jnp.cos(angles), 0.0), jnp.where(valid, jnp.sin(angles), 0.0)


def turn(values):
    lane = lax.broadcasted_iota(jnp.int32, values.shape, 1)
    return jnp.where(
        lane % (2 * QUARTER) < QUARTER,
        -pltpu.roll(values, LANES - QUARTER, 1),
        pltpu.roll(values, QUARTER, 1),
    )


def only_head(values):
    lane = lax.broadcasted_iota(jnp.int32, values.shape, 1)
    return jnp.where(lane < HD, values, jnp.zeros_like(values))


def split_heads(wide, store, heads):
    rows = wide.shape[0]
    wide = jnp.concatenate([wide, jnp.zeros((rows, LANES), wide.dtype)], axis=1)
    for head in range(heads):
        store(head, only_head(wide[:, head * HD : head * HD + LANES]))


def attend_kernel(
    heads,
    items,
    spans,
    x_ref,
    w_ref,
    gq_ref,
    gk_ref,
    cos_ref,
    sin_ref,
    out_ref,
    qpre_ref,
    kpre_ref,
    q_ref,
    k_ref,
    v_ref,
    probs_ref,
    qraw,
    kraw,
    vraw,
    oraw,
    wide,
):
    length = x_ref.shape[0]
    head = pl.program_id(0)

    @pl.when(head == 0)
    def _():
        for first in range(0, length, TILE):
            rows = pl.ds(first, TILE)
            x = x_ref[rows, :]
            wide_in = dot(x, w_ref[...])
            wide_in = jnp.concatenate([wide_in, jnp.zeros((TILE, LANES), F32)], axis=1)
            for which, raw in enumerate((qraw, kraw, vraw)):
                for h in range(heads):
                    first_lane = (which * heads + h) * HD
                    part = only_head(wide_in[:, first_lane : first_lane + LANES])
                    raw[h, rows, :] = part.astype(raw.dtype)

    for raw, pre_ref, low_ref, gain_ref in (
        (qraw, qpre_ref, q_ref, gq_ref),
        (kraw, kpre_ref, k_ref, gk_ref),
    ):
        for first in range(0, length, TILE):
            rows = pl.ds(first, TILE)
            pre = raw[head, rows, :]
            pre_ref[0, rows, :] = pre
            inv = lax.rsqrt(jnp.sum(pre * pre, axis=1, keepdims=True) / HD + EPSILON)
            normed = pre * inv * gain_ref[...]
            low_ref[0, rows, :] = (
                normed * cos_ref[rows, :] + turn(normed) * sin_ref[rows, :]
            ).astype(BF16)
    v_ref[0] = vraw[head]
    oraw[head] = vraw[head].astype(F32)
    row = lax.broadcasted_iota(jnp.int32, (SPAN, SPAN), 0)
    col = lax.broadcasted_iota(jnp.int32, (SPAN, SPAN), 1)
    row_out = lax.broadcasted_iota(jnp.int32, (SPAN, LANES), 0)
    for item in range(items):
        start = pl.multiple_of(spans[0, item], 16)
        size = spans[1, item]
        rows = pl.ds(start, SPAN)
        scores = dot_t(q_ref[0, rows, :], k_ref[0, rows, :]) * HD**-0.5
        scores = jnp.where(col < size, scores, -1e30)
        top = jnp.max(scores, axis=1, keepdims=True)
        weights = jnp.exp(scores - top)
        total = jnp.sum(weights, axis=1, keepdims=True)
        probs = jnp.where(row < size, weights / total, 0.0).astype(BF16)
        probs_ref[0, item] = probs
        mixed = dot(probs, v_ref[0, rows, :])
        oraw[head, rows, :] = jnp.where(row_out < size, mixed, oraw[head, rows, :])

    @pl.when(head == heads - 1)
    def _():
        for h in range(heads):
            wide[:, h * HD : h * HD + HD] = oraw[h][:, :HD]
        out_ref[...] = wide[...].astype(BF16)


def attend_back_kernel(
    heads,
    items,
    spans,
    grad_ref,
    qpre_ref,
    kpre_ref,
    q_ref,
    k_ref,
    v_ref,
    probs_ref,
    gq_ref,
    gk_ref,
    cos_ref,
    sin_ref,
    d_ref,
    gain_ref,
    graw,
    dqraw,
    dkraw,
    dvraw,
    wide,
):
    length = grad_ref.shape[0]
    head = pl.program_id(0)

    @pl.when(head == 0)
    def _():
        gain_ref[...] = jnp.zeros_like(gain_ref)
        for first in range(0, length, TILE):
            rows = pl.ds(first, TILE)

            def store(h, part):
                graw[h, rows, :] = part.astype(BF16)

            split_heads(grad_ref[rows, :].astype(F32), store, heads)

    dqraw[head] = jnp.zeros((length, LANES), F32)
    dkraw[head] = jnp.zeros((length, LANES), F32)
    row_all = lax.broadcasted_iota(jnp.int32, (length, LANES), 0)
    used = spans[0, items - 1] + spans[1, items - 1]
    dvraw[head] = jnp.where(row_all >= used, graw[head].astype(F32), 0.0)
    for item in range(items):
        start = pl.multiple_of(spans[0, item], 16)
        rows = pl.ds(start, SPAN)
        probs_low = probs_ref[0, item]
        probs = probs_low.astype(F32)
        grad = graw[head, rows, :]
        grad_probs = dot_t(grad, v_ref[0, rows, :])
        inner = jnp.sum(probs * grad_probs, axis=1, keepdims=True) / jnp.maximum(
            jnp.sum(probs, axis=1, keepdims=True), 0.5
        )
        grad_scores = (probs * (grad_probs - inner)).astype(BF16)
        dqraw[head, rows, :] += dot(grad_scores, k_ref[0, rows, :])
        dkraw[head, rows, :] += t_dot(grad_scores, q_ref[0, rows, :])
        dvraw[head, rows, :] += t_dot(probs_low, grad)

    for raw, pre_ref, g_ref, which in (
        (dqraw, qpre_ref, gq_ref, 0),
        (dkraw, kpre_ref, gk_ref, 1),
    ):
        for first in range(0, length, TILE):
            rows = pl.ds(first, TILE)
            turned = raw[head, rows, :] * HD**-0.5
            normed = turned * cos_ref[rows, :] - turn(turned * sin_ref[rows, :])
            pre = pre_ref[0, rows, :]
            inv = lax.rsqrt(jnp.sum(pre * pre, axis=1, keepdims=True) / HD + EPSILON)
            unit = pre * inv
            gain_ref[which : which + 1, :] += jnp.sum(normed * unit, axis=0, keepdims=True)
            scaled = normed * g_ref[...]
            along = jnp.sum(scaled * unit, axis=1, keepdims=True) / HD
            raw[head, rows, :] = inv * (scaled - unit * along)

    @pl.when(head == heads - 1)
    def _():
        for which, raw in enumerate((dqraw, dkraw, dvraw)):
            for h in range(heads):
                first_lane = (which * heads + h) * HD
                wide[:, first_lane : first_lane + HD] = raw[h][:, :HD]
        d_ref[...] = wide[...].astype(BF16)


def whole(shape):
    return pl.BlockSpec(shape, lambda h, spans: (0,) * len(shape))


def per_head(shape):
    return pl.BlockSpec((1,) + shape, lambda h, spans: (h,) + (0,) * len(shape))


def attend(spans, x, w_qkv, gain_q, gain_k, cosine, sine):
    length, width = x.shape
    heads = w_qkv.shape[1] // HD // 3
    items = spans.shape[1]
    head_f32 = jax.ShapeDtypeStruct((heads, length, LANES), F32)
    head_low = jax.ShapeDtypeStruct((heads, length, LANES), BF16)
    return pl.pallas_call(
        functools.partial(attend_kernel, heads, items),
        grid_spec=pltpu.PrefetchScalarGridSpec(
            num_scalar_prefetch=1,
            grid=(heads,),
            in_specs=[
                whole(x.shape),
                whole(w_qkv.shape),
                whole((1, LANES)),
                whole((1, LANES)),
                whole((length, LANES)),
                whole((length, LANES)),
            ],
            out_specs=[
                whole((length, heads * HD)),
                per_head((length, LANES)),
                per_head((length, LANES)),
                per_head((length, LANES)),
                per_head((length, LANES)),
                per_head((length, LANES)),
                per_head((items, SPAN, SPAN)),
            ],
            scratch_shapes=[
                pltpu.VMEM((heads, length, LANES), F32),
                pltpu.VMEM((heads, length, LANES), F32),
                pltpu.VMEM((heads, length, LANES), BF16),
                pltpu.VMEM((heads, length, LANES), F32),
                pltpu.VMEM((length, heads * HD), F32),
            ],
        ),
        out_shape=[
            jax.ShapeDtypeStruct((length, heads * HD), BF16),
            head_f32,
            head_f32,
            head_low,
            head_low,
            head_low,
            jax.ShapeDtypeStruct((heads, items, SPAN, SPAN), BF16),
        ],
        compiler_params=pltpu.CompilerParams(vmem_limit_bytes=56 * 2**20),
        cost_estimate=pl.CostEstimate(
            flops=2 * length * width * heads * HD * 3 + 4 * heads * items * SPAN * SPAN * LANES,
            bytes_accessed=24 * 2**20,
            transcendentals=heads * items * SPAN * SPAN,
        ),
        name="attend",
    )(spans, x, w_qkv, gain_q, gain_k, cosine, sine)


def attend_back(spans, grad, saved, gain_q, gain_k, cosine, sine):
    length, width = grad.shape
    heads = width // HD
    items = spans.shape[1]
    return pl.pallas_call(
        functools.partial(attend_back_kernel, heads, items),
        grid_spec=pltpu.PrefetchScalarGridSpec(
            num_scalar_prefetch=1,
            grid=(heads,),
            in_specs=[
                whole(grad.shape),
                per_head((length, LANES)),
                per_head((length, LANES)),
                per_head((length, LANES)),
                per_head((length, LANES)),
                per_head((length, LANES)),
                per_head((items, SPAN, SPAN)),
                whole((1, LANES)),
                whole((1, LANES)),
                whole((length, LANES)),
                whole((length, LANES)),
            ],
            out_specs=[
                whole((length, 3 * width)),
                whole((8, LANES)),
            ],
            scratch_shapes=[
                pltpu.VMEM((heads, length, LANES), BF16),
                pltpu.VMEM((heads, length, LANES), F32),
                pltpu.VMEM((heads, length, LANES), F32),
                pltpu.VMEM((heads, length, LANES), F32),
                pltpu.VMEM((length, 3 * width), F32),
            ],
        ),
        out_shape=[
            jax.ShapeDtypeStruct((length, 3 * width), BF16),
            jax.ShapeDtypeStruct((8, LANES), F32),
        ],
        compiler_params=pltpu.CompilerParams(vmem_limit_bytes=56 * 2**20),
        cost_estimate=pl.CostEstimate(
            flops=8 * heads * items * SPAN * SPAN * LANES,
            bytes_accessed=24 * 2**20,
            transcendentals=0,
        ),
        name="attend_back",
    )(spans, grad, *saved, gain_q, gain_k, cosine, sine)


def layer_norm(values):
    centred = values - jnp.mean(values, axis=1, keepdims=True)
    inv_std = lax.rsqrt(jnp.mean(centred * centred, axis=1, keepdims=True) + EPSILON)
    return (centred * inv_std, inv_std)


def norm_back(grad_norm, normed, inv_std):
    return inv_std * (
        grad_norm
        - jnp.mean(grad_norm, axis=1, keepdims=True)
        - normed * jnp.mean(grad_norm * normed, axis=1, keepdims=True)
    )


def per_token(member, rows):
    return sum(member[:, item, None] * rows[item][None, :] for item in range(rows.shape[0]))


def per_item(member, values):
    return jnp.stack(
        [jnp.sum(member[:, item, None] * values, axis=0) for item in range(member.shape[1])]
    )


def swap(values):
    return lax.ppermute(values, "tensor", [(0, 1), (1, 0)])


def in_order(own, other, second):
    return jnp.concatenate([jnp.where(second, other, own), jnp.where(second, own, other)])


def halving_rows(values, bits):
    dp = 2**bits
    depth = values.shape[1] // dp
    blocks = values.T.reshape((2,) * bits + (depth, values.shape[0]))
    me = lax.axis_index("dp")
    for bit in range(bits):
        axis = bits - 1 - bit
        blocks = jnp.where((me >> bit) & 1 == 1, jnp.flip(blocks, axis), blocks)
    blocks = blocks.transpose(tuple(range(bits - 1, -1, -1)) + (bits, bits + 1))
    return blocks.reshape(dp * depth, values.shape[0])


def first_halving(rows, grads):
    half = rows.shape[0] // 2
    sent = lax.ppermute(dot(rows[half:], grads).astype(BF16), "dp", partners(0))
    return (dot(rows[:half], grads) + sent.astype(F32)).astype(BF16)


def partners(bit):
    return [(i, i ^ (1 << bit)) for i in range(lax.axis_size("dp"))]


def rest_of_halving(part, bits):
    for bit in range(1, bits):
        half = part.shape[0] // 2
        sent = lax.ppermute(part[half:], "dp", partners(bit))
        part = part[:half].astype(F32) + sent.astype(F32)
        if bit < bits - 1:
            part = part.astype(BF16)
    return part.astype(F32)


def remote(src, dst, send, recv, device):
    return pltpu.make_async_remote_copy(
        src_ref=src,
        dst_ref=dst,
        send_sem=send,
        recv_sem=recv,
        device_id=device,
        device_id_type=pl.DeviceIdType.MESH,
    )


def block_at(position, me, bits):
    block = 0
    for bit in range(bits):
        mine = (me // (1 << bit)) % 2
        there = (position >> (bits - 1 - bit)) & 1
        block = block + (1 << bit) * (1 - mine if there else mine)
    return block


def across(me, bit):
    return me + (1 << bit) - 2 * (1 << bit) * ((me // (1 << bit)) % 2)


def group_rows(count):
    return -(-count // 16) * 16


def greet(peers):
    barrier = pltpu.get_barrier_semaphore()
    for peer in peers:
        pl.semaphore_signal(
            barrier, inc=1, device_id=peer, device_id_type=pl.DeviceIdType.MESH
        )
    pl.semaphore_wait(barrier, len(peers))


def tail_kernel(
    dp,
    items,
    pieces,
    d_ref,
    attn_in_ref,
    grad_attn_ref,
    heads_ref,
    w_ref,
    tokens_ref,
    resid_ref,
    member_ref,
    scale_ref,
    early_ref,
    gain_ref,
    mod_ref,
    grad_tokens_ref,
    sums_ref,
    all_ref,
    gains_ref,
    cond_ref,
    part,
    y_out,
    y_in,
    back,
    core_out,
    core_in,
    core_keep,
    x_out,
    x_in,
    x_keep,
    z_out,
    z_in,
    z_keep,
    w_out,
    w_in,
    early_in,
    late_out,
    late_in,
    early_sum,
    late_sum,
    early_all,
    late_all,
    flat,
    late_rows,
    cond_out,
    y_sems,
    halving_sems,
    early_send,
    early_recv,
    late_send,
    late_recv,
    cond_send,
    cond_recv,
):
    bits = dp.bit_length() - 1
    me = lax.axis_index("dp")
    ten = lax.axis_index("tensor")
    half = tokens_ref.shape[0]
    width = tokens_ref.shape[1]
    depth = width // dp
    inner = d_ref.shape[1] // 3
    piece = core_out.shape[2]
    groups = width // LANES
    early_groups = 4 * groups
    late_groups = 2 * groups
    early_span = early_ref.shape[0] // items
    late_span = late_out.shape[0] // items
    y_peer = (me, 1 - ten)
    dp_peers = [((me + step) % dp, ten) for step in range(1, dp)]
    greet([y_peer] + dp_peers)

    def y_copy(which, src, dst):
        return remote(src, dst, y_sems.at[0, which], y_sems.at[1, which], y_peer)

    def halving(bit, which, src, dst):
        return remote(
            src,
            dst,
            halving_sems.at[0, bit, which],
            halving_sems.at[1, bit, which],
            (across(me, bit), ten),
        )

    def gather(src, all_there, send, recv):
        copies = []
        for step, peer in enumerate(dp_peers):
            copies.append(remote(src, all_there.at[me], send.at[step], recv.at[me], peer))
        return copies

    def gathered(src, all_here, send, recv):
        for step in range(1, dp):
            source = (me + dp - step) % dp
            remote(src, all_here.at[source], send.at[0], recv.at[source], y_peer).wait_recv()

    early_copy = y_copy(0, early_ref, early_in)
    early_copy.start()

    other_rows = pl.ds(pl.multiple_of((1 - ten) * half, half), half)
    own_rows = pl.ds(pl.multiple_of(ten * half, half), half)
    y_out[...] = dot_t(d_ref[other_rows, :], w_ref[...]).astype(BF16)
    back_copy = y_copy(1, y_out, y_in)
    back_copy.start()

    early_copy.wait_recv()
    early_sum[...] = (early_ref[...].astype(F32) + early_in[...].astype(F32)).astype(BF16)
    early_all[me] = early_sum[...]
    early_copies = gather(early_sum, early_all, early_send, early_recv)
    for copy in early_copies:
        copy.start()

    for first in range(0, width, LANES):
        rows = pl.ds(first, LANES)
        part[rows, : 3 * inner] = t_dot(attn_in_ref[:, rows], d_ref[...])
        part[rows, 3 * inner :] = t_dot(grad_attn_ref[:, rows], heads_ref[...])

    def packed(position, columns):
        def rows_of(p):
            return part[pl.ds(pl.multiple_of(block_at(p, me, bits) * depth, 8), depth), columns]

        return jnp.concatenate([rows_of(position), rows_of(position + 1)]).astype(BF16)

    core_copies = []
    for p in range(pieces):
        columns = pl.ds(p * piece, piece)
        for position in range(0, dp // 2, 2):
            rows = pl.ds(position * depth, 2 * depth)
            core_out[p, rows, :] = packed(dp // 2 + position, columns)
        core_copies.append(halving(0, p, core_out.at[p], core_in.at[p]))
        core_copies[p].start()
        for position in range(0, dp // 2, 2):
            rows = pl.ds(position * depth, 2 * depth)
            core_keep[p, rows, :] = packed(position, columns)

    back[...] = dot_t(d_ref[own_rows, :], w_ref[...])

    def level(bit, copies, keep, there, out, next_in, next_keep):
        sent = []
        size = keep.shape[1]
        for p in range(pieces):
            copies[p].wait_recv()
            out[p] = (
                keep[p, size // 2 :, :].astype(F32) + there[p, size // 2 :, :].astype(F32)
            ).astype(BF16)
            sent.append(halving(bit, p, out.at[p], next_in.at[p]))
            sent[p].start()
            next_keep[p] = (
                keep[p, : size // 2, :].astype(F32) + there[p, : size // 2, :].astype(F32)
            ).astype(BF16)
        return sent

    x_copies = level(1, core_copies, core_keep, core_in, x_out, x_in, x_keep)

    back_copy.wait_recv()
    shift_sums = [jnp.zeros((1, width), F32) for _ in range(items)]
    scale_sums = [jnp.zeros((1, width), F32) for _ in range(items)]
    for first in range(0, half, LANES):
        rows = pl.ds(first, LANES)
        values = tokens_ref[rows, :].astype(F32)
        centred = values - jnp.mean(values, axis=1, keepdims=True)
        inv = lax.rsqrt(jnp.mean(centred * centred, axis=1, keepdims=True) + EPSILON)
        normed = centred * inv
        grad = back[rows, :] + y_in[rows, :].astype(F32)
        member = [member_ref[rows, item : item + 1] for item in range(items)]
        scale = sum(member[item] * scale_ref[item : item + 1, :] for item in range(items))
        product = grad * normed
        for item in range(items):
            shift_sums[item] += jnp.sum(member[item] * grad, axis=0, keepdims=True)
            scale_sums[item] += jnp.sum(member[item] * product, axis=0, keepdims=True)
        n = grad * (1.0 + scale)
        mean_n = jnp.mean(n, axis=1, keepdims=True)
        mean_along = jnp.mean(n * normed, axis=1, keepdims=True)
        grad_tokens_ref[rows, :] = (
            resid_ref[rows, :] + inv * (n - mean_n - normed * mean_along)
        ).astype(BF16)
    late_rows[...] = jnp.zeros_like(late_rows)
    for item in range(items):
        for group in range(groups):
            lanes = slice(group * LANES, group * LANES + LANES)
            row = item * late_span + group
            late_rows[row : row + 1, :] = shift_sums[item][:, lanes]
            late_rows[row + groups : row + groups + 1, :] = scale_sums[item][:, lanes]
    late_rows[late_groups : late_groups + 2, :] = gain_ref[:2, :]
    late_out[...] = late_rows[...].astype(BF16)
    late_copy = y_copy(2, late_out, late_in)
    late_copy.start()

    z_copies = level(2, x_copies, x_keep, x_in, z_out, z_in, z_keep)

    late_copy.wait_recv()
    late_sum[...] = (late_out[...].astype(F32) + late_in[...].astype(F32)).astype(BF16)
    late_all[me] = late_sum[...]
    late_copies = gather(late_sum, late_all, late_send, late_recv)
    for copy in late_copies:
        copy.start()

    last_copies = []
    for p in range(pieces):
        z_copies[p].wait_recv()
        total = z_keep[p].astype(F32) + z_in[p].astype(F32)
        w_out[p, depth:, :] = jnp.zeros((w_out.shape[1] - depth, piece), BF16)
        w_out[p, :depth, :] = total[depth:].astype(BF16)
        last_copies.append(halving(3, p, w_out.at[p], w_in.at[p]))
        last_copies[p].start()
        sums_ref[p] = total[:depth]

    gathered(early_sum, early_all, early_send, early_recv)
    count = dp * items
    for source in range(dp):
        flat[pl.ds(source * items * early_span, items * early_span), :] = early_all[
            source
        ].astype(F32)
    for group in range(early_groups):
        lanes = pl.ds((late_groups + group) * LANES, LANES)
        all_ref[:, lanes] = flat[pl.ds(group, count, stride=early_span), :].astype(BF16)
    gathered(late_sum, late_all, late_send, late_recv)
    gains = jnp.zeros((2, LANES), F32)
    for source in range(dp):
        block = late_all[source].astype(F32)
        gains += block[late_groups : late_groups + 2]
        flat[pl.ds(source * items * late_span, items * late_span), :] = block
    gains_ref[...] = jnp.zeros_like(gains_ref)
    gains_ref[:2, :] = gains
    for group in range(late_groups):
        lanes = pl.ds(group * LANES, LANES)
        all_ref[:, lanes] = flat[pl.ds(group, count, stride=late_span), :].astype(BF16)
    cond_out[...] = jnp.zeros_like(cond_out)
    flat[:count, :depth] = dot_t(all_ref[...], mod_ref[...])
    for dest in range(dp):
        cond_out[dest, :items, :] = flat[pl.ds(dest * items, items), :]
    cond_ref[me] = cond_out[me]
    cond_copies = []
    for step, peer in enumerate(dp_peers):
        cond_copies.append(
            remote(cond_out.at[peer[0]], cond_ref.at[me], cond_send.at[step], cond_recv.at[me], peer)
        )
        cond_copies[-1].start()

    for p in range(pieces):
        last_copies[p].wait_recv()
        sums_ref[p] += w_in[p, :depth, :].astype(F32)
    gathered(cond_out.at[0], cond_ref, cond_send, cond_recv)
    for copy in (
        [early_copy, back_copy, late_copy]
        + early_copies
        + late_copies
        + cond_copies
        + core_copies
        + x_copies
        + z_copies
        + last_copies
    ):
        copy.wait_send()


def tail(dp, d, attn_in, grad_attn, heads_out, w_qkv, tokens, resid, member, scale, early, gains, mod):
    half, width = tokens.shape
    items = scale.shape[0]
    length = 2 * half
    inner = d.shape[1] // 3
    depth = width // dp
    pieces = 3
    piece = 4 * inner // pieces
    groups = width // LANES
    early_rows = early.shape[0]
    late_span = group_rows(2 * groups + 2)
    late_rows = items * late_span
    count = dp * items
    columns = mod.shape[1]
    vmem = pltpu.VMEM

    def level(rows):
        return [vmem((pieces, rows, piece), BF16)] * 3

    dma = pltpu.SemaphoreType.DMA
    return pl.pallas_call(
        functools.partial(tail_kernel, dp, items, pieces),
        out_shape=[
            jax.ShapeDtypeStruct((half, width), BF16),
            jax.ShapeDtypeStruct((pieces, depth, piece), F32),
            jax.ShapeDtypeStruct((count, columns), BF16),
            jax.ShapeDtypeStruct((8, LANES), F32),
            jax.ShapeDtypeStruct((dp, 8, LANES), F32),
        ],
        in_specs=[pl.BlockSpec(memory_space=pltpu.VMEM)] * 12,
        out_specs=[pl.BlockSpec(memory_space=pltpu.VMEM)] * 5,
        scratch_shapes=[
            vmem((width, 4 * inner), F32),
            vmem((half, width), BF16),
            vmem((half, width), BF16),
            vmem((half, width), F32),
            *level(width // 2),
            *level(width // 4),
            *level(width // 8),
            vmem((pieces, group_rows(depth), piece), BF16),
            vmem((pieces, group_rows(depth), piece), BF16),
            vmem((early_rows, LANES), BF16),
            vmem((late_rows, LANES), BF16),
            vmem((late_rows, LANES), BF16),
            vmem((early_rows, LANES), BF16),
            vmem((late_rows, LANES), BF16),
            vmem((dp, early_rows, LANES), BF16),
            vmem((dp, late_rows, LANES), BF16),
            vmem((dp * early_rows, LANES), F32),
            vmem((late_rows, LANES), F32),
            vmem((dp, 8, LANES), F32),
            dma((2, 3)),
            dma((2, 4, pieces)),
            dma((dp,)),
            dma((dp,)),
            dma((dp,)),
            dma((dp,)),
            dma((dp,)),
            dma((dp,)),
        ],
        compiler_params=pltpu.CompilerParams(
            collective_id=1, has_side_effects=True, vmem_limit_bytes=60 * 2**20
        ),
        cost_estimate=pl.CostEstimate(
            flops=4 * length * width * 4 * inner, bytes_accessed=20 * 2**20, transcendentals=0
        ),
        name="tail",
    )(
        d,
        attn_in,
        grad_attn,
        heads_out,
        w_qkv,
        tokens,
        resid,
        member,
        scale,
        early,
        gains,
        mod,
    )


def shards(
    tokens,
    conditions,
    item_grids,
    mod_weight,
    query_weight,
    key_weight,
    value_weight,
    proj_weight,
    query_gain,
    key_gain,
    gate_weight,
    up_weight,
    down_weight,
    out_grad,
):
    half, width = tokens.shape
    length = 2 * half
    dp = lax.axis_size("dp")
    bits = dp.bit_length() - 1
    me = lax.axis_index("dp")
    second = lax.axis_index("tensor") == 1
    own_first = lax.axis_index("tensor") * half
    other_first = half - own_first
    items = conditions.shape[0]
    owned = mod_weight.shape[0]

    tokens_other = swap(tokens)
    out_grad_other = swap(out_grad)

    member, row_pos, col_pos, spans = geometry(item_grids, length)
    cosine, sine = rope_tables(row_pos, col_pos)
    gain_q = jnp.pad(query_gain, (0, LANES - HD))[None, :]
    gain_k = jnp.pad(key_gain, (0, LANES - HD))[None, :]
    member_own = lax.dynamic_slice_in_dim(member, own_first, half, 0)
    member_other = lax.dynamic_slice_in_dim(member, other_first, half, 0)

    cond_all = lax.all_gather(conditions, "dp", axis=0, tiled=True)
    mod_in_all = jax.nn.silu(cond_all.astype(F32)).astype(BF16)
    mod_in_own = lax.dynamic_slice_in_dim(mod_in_all, me * owned, owned, 1)
    mod_part = dot(mod_in_own, mod_weight)
    mod_parts = lax.all_to_all(
        mod_part.reshape(dp, items, 6 * width), "dp", split_axis=0, concat_axis=0, tiled=True
    )
    modulation = jnp.sum(mod_parts.astype(F32), axis=0)
    shift_one, scale_one, gate_one, shift_two, scale_two, gate_two = jnp.split(
        modulation, 6, axis=1
    )

    tokens_float = tokens.astype(F32)
    tokens_all = in_order(tokens, tokens_other, second).astype(F32)
    norm_all, _ = layer_norm(tokens_all)
    attn_in = (
        norm_all * (1.0 + per_token(member, scale_one)) + per_token(member, shift_one)
    ).astype(BF16)

    w_qkv = jnp.concatenate([query_weight, key_weight, value_weight], axis=1)
    heads_out, *saved = attend(spans, attn_in, w_qkv, gain_q, gain_k, cosine, sine)
    heads_other = lax.dynamic_slice_in_dim(heads_out, other_first, half, 0)
    heads_own = lax.dynamic_slice_in_dim(heads_out, own_first, half, 0)
    attn_recv = swap(dot(heads_other, proj_weight).astype(BF16))
    attn_out = dot(heads_own, proj_weight) + attn_recv.astype(F32)

    gate_one_own = per_token(member_own, gate_one)
    scale_two_own = per_token(member_own, scale_two)
    resid = tokens_float + gate_one_own * attn_out
    norm_two, inv_two = layer_norm(resid)
    mlp_in = (norm_two * (1.0 + scale_two_own) + per_token(member_own, shift_two)).astype(BF16)
    mlp_in_all = jnp.concatenate([mlp_in, swap(mlp_in)])

    grad_out = out_grad.astype(F32)
    gate_two_own = per_token(member_own, gate_two)
    grad_mlp_all = jnp.concatenate(
        [
            (gate_two_own * grad_out).astype(BF16),
            (per_token(member_other, gate_two) * out_grad_other.astype(F32)).astype(BF16),
        ]
    )
    grad_hidden = dot_t(grad_mlp_all, down_weight)

    gate_pre = dot(mlp_in_all, gate_weight)
    up_pre = dot(mlp_in_all, up_weight)
    silu_gate = jax.nn.silu(gate_pre)
    hidden = (silu_gate * up_pre).astype(BF16)
    grad_gate_pre = (grad_hidden * up_pre * silu_grad(gate_pre)).astype(BF16)
    grad_up_pre = (grad_hidden * silu_gate).astype(BF16)

    back_other = dot_t(grad_gate_pre[half:], gate_weight) + dot_t(grad_up_pre[half:], up_weight)
    back_recv = swap(back_other.astype(BF16))
    mlp_recv = swap(dot(hidden[half:], down_weight).astype(BF16))
    grad_mlp_in = (
        dot_t(grad_gate_pre[:half], gate_weight)
        + dot_t(grad_up_pre[:half], up_weight)
        + back_recv.astype(F32)
    )

    grad_mlp_rows = halving_rows(grad_mlp_all, bits)
    mlp_in_rows = halving_rows(mlp_in_all, bits)
    down_part = first_halving(grad_mlp_rows, hidden)
    gate_part = first_halving(mlp_in_rows, grad_gate_pre)
    up_part = first_halving(mlp_in_rows, grad_up_pre)

    mlp_out = dot(hidden[:half], down_weight) + mlp_recv.astype(F32)
    block_out = (resid + gate_two_own * mlp_out).astype(BF16)

    grad_resid = grad_out + norm_back(grad_mlp_in * (1.0 + scale_two_own), norm_two, inv_two)
    grad_attn = (gate_one_own * grad_resid).astype(BF16)
    grad_attn_all = in_order(grad_attn, swap(grad_attn), second)
    grad_heads = dot_t(grad_attn_all, proj_weight).astype(BF16)
    grad_heads, down_part, gate_part, up_part = lax.optimization_barrier(
        (grad_heads, down_part, gate_part, up_part)
    )
    grad_down = rest_of_halving(down_part, bits).T
    grad_gate = rest_of_halving(gate_part, bits)
    grad_up = rest_of_halving(up_part, bits)
    d, gain_parts = attend_back(spans, grad_heads, saved, gain_q, gain_k, cosine, sine)
    early = jnp.concatenate(
        [
            per_item(member_own, grad_resid * attn_out),
            per_item(member_own, grad_mlp_in),
            per_item(member_own, grad_mlp_in * norm_two),
            per_item(member_own, grad_out * mlp_out),
        ],
        axis=1,
    )
    inner = heads_out.shape[1]

    if dp == 16 and owned % 8 == 0:
        groups = 4 * width // LANES
        early = early.reshape(items, groups, LANES)
        early = jnp.pad(early, ((0, 0), (0, group_rows(groups) - groups), (0, 0)))
        grad_tokens, attn_sum, grad_mod_all, gain_sums, cond_parts = tail(
            dp,
            d,
            attn_in,
            grad_attn_all,
            heads_out,
            w_qkv,
            tokens,
            grad_resid,
            member_own,
            scale_one,
            early.reshape(-1, LANES).astype(BF16),
            gain_parts,
            mod_weight,
        )
        attn_sum = jnp.concatenate(list(attn_sum), axis=1)
        cond_parts = cond_parts[:, :items, :owned]
    else:

        def attn_back(first):
            return dot_t(lax.dynamic_slice_in_dim(d, first, half, 0), w_qkv)

        attn_back_recv = swap(attn_back(other_first).astype(BF16))
        grad_attn_in = attn_back(own_first) + attn_back_recv.astype(F32)
        attn_sum = rest_of_halving(
            jnp.concatenate(
                [
                    first_halving(halving_rows(attn_in, bits), d),
                    first_halving(halving_rows(grad_attn_all, bits), heads_out),
                ],
                axis=1,
            ),
            bits,
        )
        norm_one, inv_one = layer_norm(tokens_float)
        scale_one_own = per_token(member_own, scale_one)
        grad_tokens = (
            grad_resid + norm_back(grad_attn_in * (1.0 + scale_one_own), norm_one, inv_one)
        ).astype(BF16)
        part_mod = jnp.concatenate(
            [per_item(member_own, grad_attn_in), per_item(member_own, grad_attn_in * norm_one), early],
            axis=1,
        )
        gains = jnp.pad(gain_parts[:2].reshape(1, 2 * LANES), ((0, 0), (0, 6 * width - 2 * LANES)))
        part_small = jnp.concatenate([part_mod, gains]).astype(BF16)
        small = part_small.astype(F32) + swap(part_small).astype(F32)
        small_all = lax.all_gather(small.astype(BF16), "dp", axis=0, tiled=False)
        grad_mod_all = small_all[:, :items].reshape(dp * items, 6 * width)
        gain_sums = jnp.sum(small_all[:, items, : 2 * LANES].astype(F32), axis=0).reshape(2, LANES)
        cond_parts = lax.all_to_all(
            dot_t(grad_mod_all, mod_weight).reshape(dp, items, owned),
            "dp",
            split_axis=0,
            concat_axis=0,
            tiled=True,
        )

    grad_mod_weight = t_dot(mod_in_own, grad_mod_all)
    grad_mod_in = cond_parts.transpose(1, 0, 2).reshape(items, dp * owned)
    grad_conditions = silu_grad(conditions.astype(F32)) * grad_mod_in
    grad_q, grad_k, grad_v, grad_proj = (
        attn_sum[:, which * inner : (which + 1) * inner] for which in range(4)
    )
    return (
        block_out,
        grad_tokens,
        grad_conditions,
        grad_mod_weight,
        grad_q,
        grad_k,
        grad_v,
        grad_proj.T,
        gain_sums[0, :HD],
        gain_sums[1, :HD],
        grad_gate,
        grad_up,
        grad_down,
    )


def solution(mesh):
    tokens = P(("dp", "tensor"), None)
    rows = P("dp", None)
    columns = P(None, "tensor")
    inner = P("tensor", None)
    both = P("dp", "tensor")
    turned = P("tensor", "dp")
    return jax.shard_map(
        shards,
        mesh=mesh,
        in_specs=(
            tokens,
            rows,
            rows,
            rows,
            columns,
            columns,
            columns,
            inner,
            P(),
            P(),
            columns,
            columns,
            inner,
            tokens,
        ),
        out_specs=(
            tokens,
            tokens,
            rows,
            rows,
            both,
            both,
            both,
            turned,
            P(),
            P(),
            both,
            both,
            turned,
        ),
        check_vma=False,
    )
```

```python
import functools

import jax
import jax.numpy as jnp
from jax import lax
from jax.experimental import pallas as pl
from jax.experimental.pallas import tpu as pltpu
from jax.sharding import PartitionSpec as P

HD = 72
QUARTER = HD // 4
LANES = 128
SPAN = 256
TILE = 256
EPSILON = 1e-06
F32 = jnp.float32
BF16 = jnp.bfloat16
HIGH = lax.Precision.HIGHEST


def silu_grad(values):
    sigma = jax.nn.sigmoid(values)
    return sigma * (1.0 + values * (1.0 - sigma))


def dot(left, right):
    return jnp.dot(left, right, preferred_element_type=F32)


def dot_t(left, right):
    return lax.dot_general(left, right, (((1,), (1,)), ((), ())), preferred_element_type=F32)


def t_dot(left, right):
    return lax.dot_general(left, right, (((0,), (0,)), ((), ())), preferred_element_type=F32)


def geometry(row_grids, length):
    heights = row_grids[:, 0]
    widths = row_grids[:, 1]
    count = row_grids.shape[0]
    sizes = heights * widths
    ends = [sizes[0]]
    for item in range(1, count):
        ends.append(ends[-1] + sizes[item])
    starts = [ends[item] - sizes[item] for item in range(count)]
    positions = jnp.arange(length, dtype=jnp.int32)
    member = jnp.stack(
        [(positions >= starts[item]) & (positions < ends[item]) for item in range(count)], axis=1
    )
    origin = sum(jnp.where(member[:, item], starts[item], 0) for item in range(count))
    width = jnp.maximum(
        sum(jnp.where(member[:, item], widths[item], 0) for item in range(count)), 1
    )
    local = positions - origin
    spans = jnp.stack([jnp.stack(starts), sizes])
    return member.astype(F32), local // width, local % width, spans


def rope_tables(row_pos, col_pos):
    lane = jnp.arange(LANES)
    frequency = 10000.0 ** (-(lane % QUARTER).astype(F32) / QUARTER)
    along = jnp.where(lane[None, :] < 2 * QUARTER, row_pos[:, None], col_pos[:, None])
    angles = along.astype(F32) * frequency[None, :]
    valid = lane[None, :] < HD
    return jnp.where(valid, jnp.cos(angles), 0.0), jnp.where(valid, jnp.sin(angles), 0.0)


def turn(values):
    lane = lax.broadcasted_iota(jnp.int32, values.shape, 1)
    return jnp.where(
        lane % (2 * QUARTER) < QUARTER,
        -pltpu.roll(values, LANES - QUARTER, 1),
        pltpu.roll(values, QUARTER, 1),
    )


def only_head(values):
    lane = lax.broadcasted_iota(jnp.int32, values.shape, 1)
    return jnp.where(lane < HD, values, jnp.zeros_like(values))


def split_heads(wide, store, heads):
    rows = wide.shape[0]
    wide = jnp.concatenate([wide, jnp.zeros((rows, LANES), wide.dtype)], axis=1)
    for head in range(heads):
        store(head, only_head(wide[:, head * HD : head * HD + LANES]))


def attend_kernel(
    heads,
    items,
    spans,
    x_ref,
    w_ref,
    gq_ref,
    gk_ref,
    cos_ref,
    sin_ref,
    out_ref,
    qpre_ref,
    kpre_ref,
    q_ref,
    k_ref,
    v_ref,
    probs_ref,
    qraw,
    kraw,
    vraw,
    oraw,
    wide,
):
    length = x_ref.shape[0]
    head = pl.program_id(0)

    @pl.when(head == 0)
    def _():
        for first in range(0, length, TILE):
            rows = pl.ds(first, TILE)
            x = x_ref[rows, :]
            wide_in = dot(x, w_ref[...])
            wide_in = jnp.concatenate([wide_in, jnp.zeros((TILE, LANES), F32)], axis=1)
            for which, raw in enumerate((qraw, kraw, vraw)):
                for h in range(heads):
                    first_lane = (which * heads + h) * HD
                    part = only_head(wide_in[:, first_lane : first_lane + LANES])
                    raw[h, rows, :] = part.astype(raw.dtype)

    for raw, pre_ref, low_ref, gain_ref in (
        (qraw, qpre_ref, q_ref, gq_ref),
        (kraw, kpre_ref, k_ref, gk_ref),
    ):
        for first in range(0, length, TILE):
            rows = pl.ds(first, TILE)
            pre = raw[head, rows, :]
            pre_ref[0, rows, :] = pre
            inv = lax.rsqrt(jnp.sum(pre * pre, axis=1, keepdims=True) / HD + EPSILON)
            normed = pre * inv * gain_ref[...]
            low_ref[0, rows, :] = (
                normed * cos_ref[rows, :] + turn(normed) * sin_ref[rows, :]
            ).astype(BF16)
    v_ref[0] = vraw[head]
    oraw[head] = vraw[head].astype(F32)
    row = lax.broadcasted_iota(jnp.int32, (SPAN, SPAN), 0)
    col = lax.broadcasted_iota(jnp.int32, (SPAN, SPAN), 1)
    row_out = lax.broadcasted_iota(jnp.int32, (SPAN, LANES), 0)
    for item in range(items):
        start = pl.multiple_of(spans[0, item], 16)
        size = spans[1, item]
        rows = pl.ds(start, SPAN)
        scores = dot_t(q_ref[0, rows, :], k_ref[0, rows, :]) * HD**-0.5
        scores = jnp.where(col < size, scores, -1e30)
        top = jnp.max(scores, axis=1, keepdims=True)
        weights = jnp.exp(scores - top)
        total = jnp.sum(weights, axis=1, keepdims=True)
        probs = jnp.where(row < size, weights / total, 0.0).astype(BF16)
        probs_ref[0, item] = probs
        mixed = dot(probs, v_ref[0, rows, :])
        oraw[head, rows, :] = jnp.where(row_out < size, mixed, oraw[head, rows, :])

    @pl.when(head == heads - 1)
    def _():
        for h in range(heads):
            wide[:, h * HD : h * HD + HD] = oraw[h][:, :HD]
        out_ref[...] = wide[...].astype(BF16)


def attend_back_kernel(
    heads,
    items,
    spans,
    grad_ref,
    qpre_ref,
    kpre_ref,
    q_ref,
    k_ref,
    v_ref,
    probs_ref,
    gq_ref,
    gk_ref,
    cos_ref,
    sin_ref,
    d_ref,
    gain_ref,
    graw,
    dqraw,
    dkraw,
    dvraw,
    wide,
):
    length = grad_ref.shape[0]
    head = pl.program_id(0)

    @pl.when(head == 0)
    def _():
        gain_ref[...] = jnp.zeros_like(gain_ref)
        for first in range(0, length, TILE):
            rows = pl.ds(first, TILE)

            def store(h, part):
                graw[h, rows, :] = part.astype(BF16)

            split_heads(grad_ref[rows, :].astype(F32), store, heads)

    dqraw[head] = jnp.zeros((length, LANES), F32)
    dkraw[head] = jnp.zeros((length, LANES), F32)
    row_all = lax.broadcasted_iota(jnp.int32, (length, LANES), 0)
    used = spans[0, items - 1] + spans[1, items - 1]
    dvraw[head] = jnp.where(row_all >= used, graw[head].astype(F32), 0.0)
    for item in range(items):
        start = pl.multiple_of(spans[0, item], 16)
        rows = pl.ds(start, SPAN)
        probs_low = probs_ref[0, item]
        probs = probs_low.astype(F32)
        grad = graw[head, rows, :]
        grad_probs = dot_t(grad, v_ref[0, rows, :])
        inner = jnp.sum(probs * grad_probs, axis=1, keepdims=True) / jnp.maximum(
            jnp.sum(probs, axis=1, keepdims=True), 0.5
        )
        grad_scores = (probs * (grad_probs - inner)).astype(BF16)
        dqraw[head, rows, :] += dot(grad_scores, k_ref[0, rows, :])
        dkraw[head, rows, :] += t_dot(grad_scores, q_ref[0, rows, :])
        dvraw[head, rows, :] += t_dot(probs_low, grad)

    for raw, pre_ref, g_ref, which in (
        (dqraw, qpre_ref, gq_ref, 0),
        (dkraw, kpre_ref, gk_ref, 1),
    ):
        for first in range(0, length, TILE):
            rows = pl.ds(first, TILE)
            turned = raw[head, rows, :] * HD**-0.5
            normed = turned * cos_ref[rows, :] - turn(turned * sin_ref[rows, :])
            pre = pre_ref[0, rows, :]
            inv = lax.rsqrt(jnp.sum(pre * pre, axis=1, keepdims=True) / HD + EPSILON)
            unit = pre * inv
            gain_ref[which : which + 1, :] += jnp.sum(normed * unit, axis=0, keepdims=True)
            scaled = normed * g_ref[...]
            along = jnp.sum(scaled * unit, axis=1, keepdims=True) / HD
            raw[head, rows, :] = inv * (scaled - unit * along)

    @pl.when(head == heads - 1)
    def _():
        for which, raw in enumerate((dqraw, dkraw, dvraw)):
            for h in range(heads):
                first_lane = (which * heads + h) * HD
                wide[:, first_lane : first_lane + HD] = raw[h][:, :HD]
        d_ref[...] = wide[...].astype(BF16)


def whole(shape):
    return pl.BlockSpec(shape, lambda h, spans: (0,) * len(shape))


def per_head(shape):
    return pl.BlockSpec((1,) + shape, lambda h, spans: (h,) + (0,) * len(shape))


def attend(spans, x, w_qkv, gain_q, gain_k, cosine, sine):
    length, width = x.shape
    heads = w_qkv.shape[1] // HD // 3
    items = spans.shape[1]
    head_f32 = jax.ShapeDtypeStruct((heads, length, LANES), F32)
    head_low = jax.ShapeDtypeStruct((heads, length, LANES), BF16)
    return pl.pallas_call(
        functools.partial(attend_kernel, heads, items),
        grid_spec=pltpu.PrefetchScalarGridSpec(
            num_scalar_prefetch=1,
            grid=(heads,),
            in_specs=[
                whole(x.shape),
                whole(w_qkv.shape),
                whole((1, LANES)),
                whole((1, LANES)),
                whole((length, LANES)),
                whole((length, LANES)),
            ],
            out_specs=[
                whole((length, heads * HD)),
                per_head((length, LANES)),
                per_head((length, LANES)),
                per_head((length, LANES)),
                per_head((length, LANES)),
                per_head((length, LANES)),
                per_head((items, SPAN, SPAN)),
            ],
            scratch_shapes=[
                pltpu.VMEM((heads, length, LANES), F32),
                pltpu.VMEM((heads, length, LANES), F32),
                pltpu.VMEM((heads, length, LANES), BF16),
                pltpu.VMEM((heads, length, LANES), F32),
                pltpu.VMEM((length, heads * HD), F32),
            ],
        ),
        out_shape=[
            jax.ShapeDtypeStruct((length, heads * HD), BF16),
            head_f32,
            head_f32,
            head_low,
            head_low,
            head_low,
            jax.ShapeDtypeStruct((heads, items, SPAN, SPAN), BF16),
        ],
        compiler_params=pltpu.CompilerParams(vmem_limit_bytes=56 * 2**20),
        cost_estimate=pl.CostEstimate(
            flops=2 * length * width * heads * HD * 3 + 4 * heads * items * SPAN * SPAN * LANES,
            bytes_accessed=24 * 2**20,
            transcendentals=heads * items * SPAN * SPAN,
        ),
        name="attend",
    )(spans, x, w_qkv, gain_q, gain_k, cosine, sine)


def attend_back(spans, grad, saved, gain_q, gain_k, cosine, sine):
    length, width = grad.shape
    heads = width // HD
    items = spans.shape[1]
    return pl.pallas_call(
        functools.partial(attend_back_kernel, heads, items),
        grid_spec=pltpu.PrefetchScalarGridSpec(
            num_scalar_prefetch=1,
            grid=(heads,),
            in_specs=[
                whole(grad.shape),
                per_head((length, LANES)),
                per_head((length, LANES)),
                per_head((length, LANES)),
                per_head((length, LANES)),
                per_head((length, LANES)),
                per_head((items, SPAN, SPAN)),
                whole((1, LANES)),
                whole((1, LANES)),
                whole((length, LANES)),
                whole((length, LANES)),
            ],
            out_specs=[
                whole((length, 3 * width)),
                whole((8, LANES)),
            ],
            scratch_shapes=[
                pltpu.VMEM((heads, length, LANES), BF16),
                pltpu.VMEM((heads, length, LANES), F32),
                pltpu.VMEM((heads, length, LANES), F32),
                pltpu.VMEM((heads, length, LANES), F32),
                pltpu.VMEM((length, 3 * width), F32),
            ],
        ),
        out_shape=[
            jax.ShapeDtypeStruct((length, 3 * width), BF16),
            jax.ShapeDtypeStruct((8, LANES), F32),
        ],
        compiler_params=pltpu.CompilerParams(vmem_limit_bytes=56 * 2**20),
        cost_estimate=pl.CostEstimate(
            flops=8 * heads * items * SPAN * SPAN * LANES,
            bytes_accessed=24 * 2**20,
            transcendentals=0,
        ),
        name="attend_back",
    )(spans, grad, *saved, gain_q, gain_k, cosine, sine)


def layer_norm(values):
    centred = values - jnp.mean(values, axis=1, keepdims=True)
    inv_std = lax.rsqrt(jnp.mean(centred * centred, axis=1, keepdims=True) + EPSILON)
    return (centred * inv_std, inv_std)


def norm_back(grad_norm, normed, inv_std):
    return inv_std * (
        grad_norm
        - jnp.mean(grad_norm, axis=1, keepdims=True)
        - normed * jnp.mean(grad_norm * normed, axis=1, keepdims=True)
    )


def per_token(member, rows):
    return sum(member[:, item, None] * rows[item][None, :] for item in range(rows.shape[0]))


def per_item(member, values):
    return jnp.stack(
        [jnp.sum(member[:, item, None] * values, axis=0) for item in range(member.shape[1])]
    )


def swap(values):
    return lax.ppermute(values, "tensor", [(0, 1), (1, 0)])


def in_order(own, other, second):
    return jnp.concatenate([jnp.where(second, other, own), jnp.where(second, own, other)])


def halving_rows(values, bits):
    dp = 2**bits
    depth = values.shape[1] // dp
    blocks = values.T.reshape((2,) * bits + (depth, values.shape[0]))
    me = lax.axis_index("dp")
    for bit in range(bits):
        axis = bits - 1 - bit
        blocks = jnp.where((me >> bit) & 1 == 1, jnp.flip(blocks, axis), blocks)
    blocks = blocks.transpose(tuple(range(bits - 1, -1, -1)) + (bits, bits + 1))
    return blocks.reshape(dp * depth, values.shape[0])


def first_halving(rows, grads):
    half = rows.shape[0] // 2
    sent = lax.ppermute(dot(rows[half:], grads).astype(BF16), "dp", partners(0))
    return (dot(rows[:half], grads) + sent.astype(F32)).astype(BF16)


def partners(bit):
    return [(i, i ^ (1 << bit)) for i in range(lax.axis_size("dp"))]


def rest_of_halving(part, bits):
    for bit in range(1, bits):
        half = part.shape[0] // 2
        sent = lax.ppermute(part[half:], "dp", partners(bit))
        part = part[:half].astype(F32) + sent.astype(F32)
        if bit < bits - 1:
            part = part.astype(BF16)
    return part.astype(F32)


def remote(src, dst, send, recv, device):
    return pltpu.make_async_remote_copy(
        src_ref=src,
        dst_ref=dst,
        send_sem=send,
        recv_sem=recv,
        device_id=device,
        device_id_type=pl.DeviceIdType.MESH,
    )


def block_at(position, me, bits):
    block = 0
    for bit in range(bits):
        mine = (me // (1 << bit)) % 2
        there = (position >> (bits - 1 - bit)) & 1
        block = block + (1 << bit) * (1 - mine if there else mine)
    return block


def across(me, bit):
    return me + (1 << bit) - 2 * (1 << bit) * ((me // (1 << bit)) % 2)


def group_rows(count):
    return -(-count // 16) * 16


def greet(peers):
    barrier = pltpu.get_barrier_semaphore()
    for peer in peers:
        pl.semaphore_signal(
            barrier, inc=1, device_id=peer, device_id_type=pl.DeviceIdType.MESH
        )
    pl.semaphore_wait(barrier, len(peers))


def tail_kernel(
    dp,
    items,
    pieces,
    d_ref,
    attn_in_ref,
    grad_attn_ref,
    heads_ref,
    w_ref,
    tokens_ref,
    resid_ref,
    member_ref,
    scale_ref,
    early_ref,
    gain_ref,
    mod_ref,
    paired_ref,
    crossed_ref,
    grad_tokens_ref,
    sums_ref,
    all_ref,
    gains_ref,
    cond_ref,
    part,
    y_out,
    y_in,
    back,
    core_out,
    core_in,
    core_keep,
    x_out,
    x_in,
    x_keep,
    z_out,
    z_in,
    z_keep,
    w_out,
    w_in,
    early_in,
    late_out,
    late_in,
    early_sum,
    late_sum,
    early_all,
    late_all,
    flat,
    late_rows,
    cond_out,
    y_sems,
    halving_sems,
    early_send,
    early_recv,
    late_send,
    late_recv,
    cond_send,
    cond_recv,
):
    bits = dp.bit_length() - 1
    me = lax.axis_index("dp")
    ten = lax.axis_index("tensor")
    half = tokens_ref.shape[0]
    width = tokens_ref.shape[1]
    depth = width // dp
    inner = d_ref.shape[1] // 3
    piece = core_out.shape[2]
    groups = width // LANES
    early_groups = 4 * groups
    late_groups = 2 * groups
    early_span = early_ref.shape[0] // items
    late_span = late_out.shape[0] // items
    y_peer = (me, 1 - ten)
    dp_peers = [((me + step) % dp, ten) for step in range(1, dp)]
    greet([y_peer] + dp_peers)

    def y_copy(which, src, dst):
        return remote(src, dst, y_sems.at[0, which], y_sems.at[1, which], y_peer)

    def halving(bit, which, src, dst):
        return remote(
            src,
            dst,
            halving_sems.at[0, bit, which],
            halving_sems.at[1, bit, which],
            (across(me, bit), ten),
        )

    def gather(src, all_there, send, recv):
        copies = []
        for step, peer in enumerate(dp_peers):
            copies.append(remote(src, all_there.at[me], send.at[step], recv.at[me], peer))
        return copies

    def gathered(src, all_here, send, recv):
        for step in range(1, dp):
            source = (me + dp - step) % dp
            remote(src, all_here.at[source], send.at[0], recv.at[source], y_peer).wait_recv()

    early_copy = y_copy(0, early_ref, early_in)
    early_copy.start()

    paired = paired_ref.shape[0]
    crossed = crossed_ref.shape[0]
    last_copies = {}

    def last_level(p, total):
        w_out[p, depth:, :] = jnp.zeros((w_out.shape[1] - depth, piece), BF16)
        w_out[p, :depth, :] = total[depth:].astype(BF16)
        last_copies[p] = halving(3, p, w_out.at[p], w_in.at[p])
        last_copies[p].start()
        sums_ref[p] = total[:depth]

    for p in range(crossed):
        last_level(pieces + paired + p, crossed_ref[p].astype(F32))
    paired_copies = []
    for p in range(paired):
        paired_copies.append(
            halving(2, pieces + p, paired_ref.at[p, pl.ds(2 * depth, 2 * depth), :], z_in.at[pieces + p])
        )
        paired_copies[p].start()

    other_rows = pl.ds(pl.multiple_of((1 - ten) * half, half), half)
    own_rows = pl.ds(pl.multiple_of(ten * half, half), half)
    y_out[...] = dot_t(d_ref[other_rows, :], w_ref[...]).astype(BF16)
    back_copy = y_copy(1, y_out, y_in)
    back_copy.start()

    early_copy.wait_recv()
    early_sum[...] = (early_ref[...].astype(F32) + early_in[...].astype(F32)).astype(BF16)
    early_all[me] = early_sum[...]
    early_copies = gather(early_sum, early_all, early_send, early_recv)
    for copy in early_copies:
        copy.start()

    for first in range(0, width, LANES):
        rows = pl.ds(first, LANES)
        part[rows, : 3 * inner] = t_dot(attn_in_ref[:, rows], d_ref[...])
        part[rows, 3 * inner :] = t_dot(grad_attn_ref[:, rows], heads_ref[...])

    def packed(position, columns):
        def rows_of(p):
            return part[pl.ds(pl.multiple_of(block_at(p, me, bits) * depth, 8), depth), columns]

        return jnp.concatenate([rows_of(position), rows_of(position + 1)]).astype(BF16)

    core_copies = []
    for p in range(pieces):
        columns = pl.ds(p * piece, piece)
        for position in range(0, dp // 2, 2):
            rows = pl.ds(position * depth, 2 * depth)
            core_out[p, rows, :] = packed(dp // 2 + position, columns)
        core_copies.append(halving(0, p, core_out.at[p], core_in.at[p]))
        core_copies[p].start()
        for position in range(0, dp // 2, 2):
            rows = pl.ds(position * depth, 2 * depth)
            core_keep[p, rows, :] = packed(position, columns)

    back[...] = dot_t(d_ref[own_rows, :], w_ref[...])

    def level(bit, copies, keep, there, out, next_in, next_keep):
        sent = []
        size = keep.shape[1]
        for p in range(pieces):
            copies[p].wait_recv()
            out[p] = (
                keep[p, size // 2 :, :].astype(F32) + there[p, size // 2 :, :].astype(F32)
            ).astype(BF16)
            sent.append(halving(bit, p, out.at[p], next_in.at[p]))
            sent[p].start()
            next_keep[p] = (
                keep[p, : size // 2, :].astype(F32) + there[p, : size // 2, :].astype(F32)
            ).astype(BF16)
        return sent

    x_copies = level(1, core_copies, core_keep, core_in, x_out, x_in, x_keep)

    for p in range(paired):
        paired_copies[p].wait_recv()
        last_level(
            pieces + p,
            paired_ref[p, : 2 * depth, :].astype(F32) + z_in[pieces + p].astype(F32),
        )

    back_copy.wait_recv()
    shift_sums = [jnp.zeros((1, width), F32) for _ in range(items)]
    scale_sums = [jnp.zeros((1, width), F32) for _ in range(items)]
    for first in range(0, half, LANES):
        rows = pl.ds(first, LANES)
        values = tokens_ref[rows, :].astype(F32)
        centred = values - jnp.mean(values, axis=1, keepdims=True)
        inv = lax.rsqrt(jnp.mean(centred * centred, axis=1, keepdims=True) + EPSILON)
        normed = centred * inv
        grad = back[rows, :] + y_in[rows, :].astype(F32)
        member = [member_ref[rows, item : item + 1] for item in range(items)]
        scale = sum(member[item] * scale_ref[item : item + 1, :] for item in range(items))
        product = grad * normed
        for item in range(items):
            shift_sums[item] += jnp.sum(member[item] * grad, axis=0, keepdims=True)
            scale_sums[item] += jnp.sum(member[item] * product, axis=0, keepdims=True)
        n = grad * (1.0 + scale)
        mean_n = jnp.mean(n, axis=1, keepdims=True)
        mean_along = jnp.mean(n * normed, axis=1, keepdims=True)
        grad_tokens_ref[rows, :] = (
            resid_ref[rows, :] + inv * (n - mean_n - normed * mean_along)
        ).astype(BF16)
    late_rows[...] = jnp.zeros_like(late_rows)
    for item in range(items):
        for group in range(groups):
            lanes = slice(group * LANES, group * LANES + LANES)
            row = item * late_span + group
            late_rows[row : row + 1, :] = shift_sums[item][:, lanes]
            late_rows[row + groups : row + groups + 1, :] = scale_sums[item][:, lanes]
    late_rows[late_groups : late_groups + 2, :] = gain_ref[:2, :]
    late_out[...] = late_rows[...].astype(BF16)
    late_copy = y_copy(2, late_out, late_in)
    late_copy.start()

    z_copies = level(2, x_copies, x_keep, x_in, z_out, z_in, z_keep)

    late_copy.wait_recv()
    late_sum[...] = (late_out[...].astype(F32) + late_in[...].astype(F32)).astype(BF16)
    late_all[me] = late_sum[...]
    late_copies = gather(late_sum, late_all, late_send, late_recv)
    for copy in late_copies:
        copy.start()

    for p in range(pieces):
        z_copies[p].wait_recv()
        last_level(p, z_keep[p].astype(F32) + z_in[p].astype(F32))

    gathered(early_sum, early_all, early_send, early_recv)
    count = dp * items
    for source in range(dp):
        flat[pl.ds(source * items * early_span, items * early_span), :] = early_all[
            source
        ].astype(F32)
    for group in range(early_groups):
        lanes = pl.ds((late_groups + group) * LANES, LANES)
        all_ref[:, lanes] = flat[pl.ds(group, count, stride=early_span), :].astype(BF16)
    gathered(late_sum, late_all, late_send, late_recv)
    gains = jnp.zeros((2, LANES), F32)
    for source in range(dp):
        block = late_all[source].astype(F32)
        gains += block[late_groups : late_groups + 2]
        flat[pl.ds(source * items * late_span, items * late_span), :] = block
    gains_ref[...] = jnp.zeros_like(gains_ref)
    gains_ref[:2, :] = gains
    for group in range(late_groups):
        lanes = pl.ds(group * LANES, LANES)
        all_ref[:, lanes] = flat[pl.ds(group, count, stride=late_span), :].astype(BF16)
    cond_out[...] = jnp.zeros_like(cond_out)
    flat[:count, :depth] = dot_t(all_ref[...], mod_ref[...])
    for dest in range(dp):
        cond_out[dest, :items, :] = flat[pl.ds(dest * items, items), :]
    cond_ref[me] = cond_out[me]
    cond_copies = []
    for step, peer in enumerate(dp_peers):
        cond_copies.append(
            remote(cond_out.at[peer[0]], cond_ref.at[me], cond_send.at[step], cond_recv.at[me], peer)
        )
        cond_copies[-1].start()

    for p in last_copies:
        last_copies[p].wait_recv()
        sums_ref[p] += w_in[p, :depth, :].astype(F32)
    gathered(cond_out.at[0], cond_ref, cond_send, cond_recv)
    for copy in (
        [early_copy, back_copy, late_copy]
        + early_copies
        + late_copies
        + cond_copies
        + core_copies
        + x_copies
        + z_copies
        + paired_copies
        + list(last_copies.values())
    ):
        copy.wait_send()


def tail(
    dp, d, attn_in, grad_attn, heads_out, w_qkv, tokens, resid, member, scale, early, gains, mod, paired, crossed
):
    half, width = tokens.shape
    items = scale.shape[0]
    length = 2 * half
    inner = d.shape[1] // 3
    depth = width // dp
    pieces = 3
    piece = 4 * inner // pieces
    groups = width // LANES
    early_rows = early.shape[0]
    late_span = group_rows(2 * groups + 2)
    late_rows = items * late_span
    count = dp * items
    columns = mod.shape[1]
    total = pieces + paired.shape[0] + crossed.shape[0]
    vmem = pltpu.VMEM

    def level(rows):
        return [vmem((pieces, rows, piece), BF16)] * 3

    dma = pltpu.SemaphoreType.DMA
    return pl.pallas_call(
        functools.partial(tail_kernel, dp, items, pieces),
        out_shape=[
            jax.ShapeDtypeStruct((half, width), BF16),
            jax.ShapeDtypeStruct((total, depth, piece), F32),
            jax.ShapeDtypeStruct((count, columns), BF16),
            jax.ShapeDtypeStruct((8, LANES), F32),
            jax.ShapeDtypeStruct((dp, 8, LANES), F32),
        ],
        in_specs=[pl.BlockSpec(memory_space=pltpu.VMEM)] * 14,
        out_specs=[pl.BlockSpec(memory_space=pltpu.VMEM)] * 5,
        scratch_shapes=[
            vmem((width, 4 * inner), F32),
            vmem((half, width), BF16),
            vmem((half, width), BF16),
            vmem((half, width), F32),
            *level(width // 2),
            *level(width // 4),
            vmem((pieces, width // 8, piece), BF16),
            vmem((pieces + paired.shape[0], width // 8, piece), BF16),
            vmem((pieces, width // 8, piece), BF16),
            vmem((total, group_rows(depth), piece), BF16),
            vmem((total, group_rows(depth), piece), BF16),
            vmem((early_rows, LANES), BF16),
            vmem((late_rows, LANES), BF16),
            vmem((late_rows, LANES), BF16),
            vmem((early_rows, LANES), BF16),
            vmem((late_rows, LANES), BF16),
            vmem((dp, early_rows, LANES), BF16),
            vmem((dp, late_rows, LANES), BF16),
            vmem((dp * early_rows, LANES), F32),
            vmem((late_rows, LANES), F32),
            vmem((dp, 8, LANES), F32),
            dma((2, 3)),
            dma((2, 4, total)),
            dma((dp,)),
            dma((dp,)),
            dma((dp,)),
            dma((dp,)),
            dma((dp,)),
            dma((dp,)),
        ],
        compiler_params=pltpu.CompilerParams(
            collective_id=1, has_side_effects=True, vmem_limit_bytes=60 * 2**20
        ),
        cost_estimate=pl.CostEstimate(
            flops=4 * length * width * 4 * inner, bytes_accessed=20 * 2**20, transcendentals=0
        ),
        name="tail",
    )(
        d,
        attn_in,
        grad_attn,
        heads_out,
        w_qkv,
        tokens,
        resid,
        member,
        scale,
        early,
        gains,
        mod,
        paired,
        crossed,
    )


def middle_kernel(
    items,
    chunk,
    step,
    heads_ref,
    proj_ref,
    tokens_ref,
    own_grad_ref,
    other_grad_ref,
    own_member_ref,
    other_member_ref,
    mod_ref,
    gate_hbm,
    up_hbm,
    down_hbm,
    grad_heads_ref,
    grad_attn_ref,
    grad_resid_ref,
    resid_ref,
    early_ref,
    mlp_other_ref,
    mlp_own_ref,
    crossed_ref,
    paired_ref,
    gate_ref,
    up_ref,
    down_ref,
    attn,
    grad_mlp,
    mlp_in,
    hidden,
    grad_gate,
    grad_up,
    y_out,
    y_in,
    part,
    core_out,
    core_keep,
    core_in,
    x_out,
    x_in,
    y_sems,
    core_sems,
    x_sems,
    load_sems,
):
    dp = lax.axis_size("dp")
    bits = dp.bit_length() - 1
    me = lax.axis_index("dp")
    ten = lax.axis_index("tensor")
    half, width = tokens_ref.shape
    depth = width // dp
    units = gate_ref.shape[1]
    piece = part.shape[1]
    per_weight = units // piece
    chunks = half // chunk
    y_peer = (me, 1 - ten)
    core_peer = (across(me, 0), ten)
    x_peer = (across(me, 1), ten)
    loads = [
        pltpu.make_async_copy(source, there, load_sems.at[which])
        for which, (source, there) in enumerate(
            ((gate_hbm, gate_ref), (up_hbm, up_ref), (down_hbm, down_ref))
        )
    ]
    for load in loads:
        load.start()
    greet([y_peer, core_peer, x_peer])

    def rows_at(first, count=chunk):
        return pl.ds(pl.multiple_of(first, 16), count)

    def y_copy(kind, c, src, dst):
        return remote(
            src, dst, y_sems.at[0, kind, c], y_sems.at[1, kind, c], y_peer
        )

    def mod_row(kind, item):
        return mod_ref[item : item + 1, kind * width : (kind + 1) * width]

    def token_values(member_ref, rows, kind):
        return sum(member_ref[rows, item : item + 1] * mod_row(kind, item) for item in range(items))

    def in_steps(c, body):
        def one(index, carry):
            body(pl.ds(pl.multiple_of(c * chunk + index * step, step), step))
            return carry

        lax.fori_loop(0, chunk // step, one, 0)

    proj_copies = []
    for c in range(chunks):
        rows = pl.ds(c * chunk, chunk)
        y_out[rows, :] = dot(
            heads_ref[rows_at((1 - ten) * half + c * chunk), :], proj_ref[...]
        ).astype(BF16)
        proj_copies.append(y_copy(0, c, y_out.at[rows, :], y_in.at[rows, :]))
        proj_copies[c].start()
    for c in range(chunks):
        attn[pl.ds(c * chunk, chunk), :] = dot(
            heads_ref[rows_at(ten * half + c * chunk), :], proj_ref[...]
        )
    for c in range(chunks):

        def scale_grads(rows):
            later = pl.ds(pl.multiple_of(rows.start + half, step), step)
            grad_mlp[rows, :] = (
                token_values(own_member_ref, rows, 5) * own_grad_ref[rows, :].astype(F32)
            ).astype(BF16)
            grad_mlp[later, :] = (
                token_values(other_member_ref, rows, 5) * other_grad_ref[rows, :].astype(F32)
            ).astype(BF16)

        in_steps(c, scale_grads)

    for load in loads:
        load.wait()

    def mlp(c):
        rows = pl.ds(c * chunk, chunk)
        for first in range(0, units, 256):
            columns = pl.ds(first, 256)
            gate = dot(mlp_in[rows, :], gate_ref[:, columns])
            up = dot(mlp_in[rows, :], up_ref[:, columns])
            grad = dot_t(grad_mlp[rows, :], down_ref[columns, :])
            sigma = 1.0 / (1.0 + jnp.exp(-gate))
            silu = gate * sigma
            hidden[rows, columns] = (silu * up).astype(BF16)
            grad_gate[rows, columns] = (
                grad * up * (sigma * (1.0 + gate * (1.0 - sigma)))
            ).astype(BF16)
            grad_up[rows, columns] = (grad * silu).astype(BF16)

    mlp_copies = []
    for c in range(chunks):
        proj_copies[c].wait_recv()

        def norm(rows):
            mixed = attn[rows, :] + y_in[rows, :].astype(F32)
            attn[rows, :] = mixed
            resid = tokens_ref[rows, :].astype(F32) + token_values(own_member_ref, rows, 2) * mixed
            resid_ref[rows, :] = resid
            normed, _ = layer_norm(resid)
            mlp_in[rows, :] = (
                normed * (1.0 + token_values(own_member_ref, rows, 4))
                + token_values(own_member_ref, rows, 3)
            ).astype(BF16)

        in_steps(c, norm)
        mlp_copies.append(
            y_copy(
                1, c, mlp_in.at[pl.ds(c * chunk, chunk), :], mlp_in.at[pl.ds(half + c * chunk, chunk), :]
            )
        )
        mlp_copies[c].start()
    for c in range(chunks):
        mlp(c)
    for c in range(chunks):
        mlp_copies[c].wait_recv()
        mlp(chunks + c)

    def back(first):
        rows = pl.ds(first, chunk)
        return dot_t(grad_gate[rows, :], gate_ref[...]) + dot_t(grad_up[rows, :], up_ref[...])

    back_copies = []
    for c in range(chunks):
        rows = pl.ds(c * chunk, chunk)
        proj_copies[c].wait_send()
        y_out[rows, :] = back(half + c * chunk).astype(BF16)
        back_copies.append(y_copy(2, c, y_out.at[rows, :], y_in.at[rows, :]))
        back_copies[c].start()

    def packed(position):
        def rows_of(p):
            return part[pl.ds(pl.multiple_of(block_at(p, me, bits) * depth, 8), depth), :]

        return jnp.concatenate([rows_of(position), rows_of(position + 1)]).astype(BF16)

    core_copies = []
    x_copies = []

    def weight_grad(p):
        which, column = divmod(p, per_weight)
        columns = pl.ds(column * piece, piece)
        left, right = ((grad_mlp, hidden), (mlp_in, grad_gate), (mlp_in, grad_up))[which]
        slot = p % 2
        for first in range(0, width, LANES):
            rows = pl.ds(first, LANES)
            part[rows, :] = t_dot(left[:, rows], right[:, columns])
        if p >= 2:
            core_copies[p - 2].wait_send()
        for position in range(0, dp // 2, 2):
            rows = pl.ds(position * depth, 2 * depth)
            core_out[slot, rows, :] = packed(dp // 2 + position)
        core_copies.append(
            remote(
                core_out.at[slot], core_in.at[p], core_sems.at[0, p], core_sems.at[1, p], core_peer
            )
        )
        core_copies[p].start()
        for position in range(0, dp // 2, 2):
            rows = pl.ds(position * depth, 2 * depth)
            core_keep[slot, rows, :] = packed(position)

    quarter = width // 4

    def cross(p):
        slot = p % 2
        core_copies[p].wait_recv()

        def total(rows):
            return (core_keep[slot, rows, :].astype(F32) + core_in[p, rows, :].astype(F32)).astype(
                BF16
            )

        if p < 2 * per_weight:
            x_out[p] = total(pl.ds(quarter, quarter))
            x_copies.append(
                remote(x_out.at[p], x_in.at[p], x_sems.at[0, p], x_sems.at[1, p], x_peer)
            )
            x_copies[p].start()
            crossed_ref[p] = total(pl.ds(0, quarter))
        else:
            paired_ref[p - 2 * per_weight] = total(pl.ds(0, 2 * quarter))

    pieces = 3 * per_weight
    weight_grad(0)
    for p in range(1, pieces - 1):
        weight_grad(p)
        cross(p - 1)
    for c in range(chunks):
        grad_resid_ref[pl.ds(c * chunk, chunk), :] = back(c * chunk)

    early_ref[...] = jnp.zeros_like(early_ref)
    grad_copies = []
    for c in range(chunks):
        back_copies[c].wait_recv()

        def norm_grad(rows):
            grad = grad_resid_ref[rows, :] + y_in[rows, :].astype(F32)
            normed, inv = layer_norm(resid_ref[rows, :])
            n = grad * (1.0 + token_values(own_member_ref, rows, 4))
            grad_resid = own_grad_ref[rows, :].astype(F32) + norm_back(n, normed, inv)
            grad_resid_ref[rows, :] = grad_resid
            there = pl.ds(pl.multiple_of(rows.start + ten * half, step), step)
            grad_attn_ref[there, :] = (token_values(own_member_ref, rows, 2) * grad_resid).astype(
                BF16
            )
            for kind, values in enumerate((grad_resid * attn[rows, :], grad, grad * normed)):
                lanes = slice(kind * width, (kind + 1) * width)
                for item in range(items):
                    early_ref[item : item + 1, lanes] += jnp.sum(
                        own_member_ref[rows, item : item + 1] * values, axis=0, keepdims=True
                    )

        in_steps(c, norm_grad)
        rows = rows_at(ten * half + c * chunk)
        grad_copies.append(y_copy(3, c, grad_attn_ref.at[rows, :], grad_attn_ref.at[rows, :]))
        grad_copies[c].start()

    weight_grad(pieces - 1)
    cross(pieces - 2)
    for c in range(chunks):
        rows = pl.ds(c * chunk, chunk)
        mlp_other_ref[rows, :] = dot(
            hidden[pl.ds(half + c * chunk, chunk), :], down_ref[...]
        ).astype(BF16)
        mlp_own_ref[rows, :] = dot(hidden[rows, :], down_ref[...])
        own_rows = rows_at(ten * half + c * chunk)
        grad_heads_ref[own_rows, :] = dot_t(grad_attn_ref[own_rows, :], proj_ref[...]).astype(BF16)
    cross(pieces - 1)
    for c in range(chunks):
        rows = rows_at((1 - ten) * half + c * chunk)
        y_copy(3, c, grad_attn_ref.at[rows, :], grad_attn_ref.at[rows, :]).wait_recv()
        grad_heads_ref[rows, :] = dot_t(grad_attn_ref[rows, :], proj_ref[...]).astype(BF16)
    for p in range(2 * per_weight):
        x_copies[p].wait_recv()
        crossed_ref[p] = (crossed_ref[p].astype(F32) + x_in[p].astype(F32)).astype(BF16)
    for copy in mlp_copies + back_copies + grad_copies + core_copies[-2:] + x_copies:
        copy.wait_send()


def middle(heads_out, proj, tokens, own_grad, other_grad, own_member, other_member, mod, gate, up, down):
    half, width = tokens.shape
    length = 2 * half
    units = gate.shape[1]
    inner = heads_out.shape[1]
    items = mod.shape[0]
    chunk = half // 2
    chunks = half // chunk
    piece = units // 2
    pieces = 6
    vmem = pltpu.VMEM
    dma = pltpu.SemaphoreType.DMA
    anywhere = pl.BlockSpec(memory_space=pl.ANY)
    return pl.pallas_call(
        functools.partial(middle_kernel, items, chunk, 32),
        out_shape=[
            jax.ShapeDtypeStruct((length, inner), BF16),
            jax.ShapeDtypeStruct((length, width), BF16),
            jax.ShapeDtypeStruct((half, width), F32),
            jax.ShapeDtypeStruct((half, width), F32),
            jax.ShapeDtypeStruct((8, 3 * width), F32),
            jax.ShapeDtypeStruct((half, width), BF16),
            jax.ShapeDtypeStruct((half, width), F32),
            jax.ShapeDtypeStruct((4, width // 4, piece), BF16),
            jax.ShapeDtypeStruct((2, width // 2, piece), BF16),
        ],
        in_specs=[pl.BlockSpec(memory_space=pltpu.VMEM)] * 8 + [anywhere] * 3,
        out_specs=[pl.BlockSpec(memory_space=pltpu.VMEM)] * 9,
        scratch_shapes=[
            vmem((width, units), BF16),
            vmem((width, units), BF16),
            vmem((units, width), BF16),
            vmem((half, width), F32),
            vmem((length, width), BF16),
            vmem((length, width), BF16),
            vmem((length, units), BF16),
            vmem((length, units), BF16),
            vmem((length, units), BF16),
            vmem((half, width), BF16),
            vmem((half, width), BF16),
            vmem((width, piece), F32),
            vmem((2, width // 2, piece), BF16),
            vmem((2, width // 2, piece), BF16),
            vmem((pieces, width // 2, piece), BF16),
            vmem((4, width // 4, piece), BF16),
            vmem((4, width // 4, piece), BF16),
            dma((2, 4, chunks)),
            dma((2, pieces)),
            dma((2, 4)),
            dma((3,)),
        ],
        compiler_params=pltpu.CompilerParams(
            collective_id=2, has_side_effects=True, vmem_limit_bytes=62 * 2**20
        ),
        cost_estimate=pl.CostEstimate(
            flops=18 * length * width * units, bytes_accessed=30 * 2**20, transcendentals=0
        ),
        name="middle",
    )(heads_out, proj, tokens, own_grad, other_grad, own_member, other_member, mod, gate, up, down)


def shards(
    tokens,
    conditions,
    item_grids,
    mod_weight,
    query_weight,
    key_weight,
    value_weight,
    proj_weight,
    query_gain,
    key_gain,
    gate_weight,
    up_weight,
    down_weight,
    out_grad,
):
    half, width = tokens.shape
    length = 2 * half
    dp = lax.axis_size("dp")
    bits = dp.bit_length() - 1
    me = lax.axis_index("dp")
    second = lax.axis_index("tensor") == 1
    own_first = lax.axis_index("tensor") * half
    other_first = half - own_first
    items = conditions.shape[0]
    owned = mod_weight.shape[0]

    tokens_other = swap(tokens)
    out_grad_other = swap(out_grad)

    member, row_pos, col_pos, spans = geometry(item_grids, length)
    cosine, sine = rope_tables(row_pos, col_pos)
    gain_q = jnp.pad(query_gain, (0, LANES - HD))[None, :]
    gain_k = jnp.pad(key_gain, (0, LANES - HD))[None, :]
    member_own = lax.dynamic_slice_in_dim(member, own_first, half, 0)
    member_other = lax.dynamic_slice_in_dim(member, other_first, half, 0)

    cond_all = lax.all_gather(conditions, "dp", axis=0, tiled=True)
    mod_in_all = jax.nn.silu(cond_all.astype(F32)).astype(BF16)
    mod_in_own = lax.dynamic_slice_in_dim(mod_in_all, me * owned, owned, 1)
    mod_part = dot(mod_in_own, mod_weight)
    mod_parts = lax.all_to_all(
        mod_part.reshape(dp, items, 6 * width), "dp", split_axis=0, concat_axis=0, tiled=True
    )
    modulation = jnp.sum(mod_parts.astype(F32), axis=0)
    shift_one, scale_one, gate_one, shift_two, scale_two, gate_two = jnp.split(
        modulation, 6, axis=1
    )

    tokens_float = tokens.astype(F32)
    tokens_all = in_order(tokens, tokens_other, second).astype(F32)
    norm_all, _ = layer_norm(tokens_all)
    attn_in = (
        norm_all * (1.0 + per_token(member, scale_one)) + per_token(member, shift_one)
    ).astype(BF16)

    w_qkv = jnp.concatenate([query_weight, key_weight, value_weight], axis=1)
    heads_out, *saved = attend(spans, attn_in, w_qkv, gain_q, gain_k, cosine, sine)
    inner = heads_out.shape[1]
    grad_out = out_grad.astype(F32)
    gate_two_own = per_token(member_own, gate_two)

    if dp == 16 and owned % 8 == 0:
        (
            grad_heads,
            grad_attn_all,
            grad_resid,
            resid,
            early,
            mlp_other,
            mlp_own,
            crossed,
            paired,
        ) = middle(
            heads_out,
            proj_weight,
            tokens,
            out_grad,
            out_grad_other,
            member_own,
            member_other,
            modulation,
            gate_weight,
            up_weight,
            down_weight,
        )
        mlp_recv = swap(mlp_other)
        fifth = crossed.shape[1] // 2
        crossed_recv = lax.ppermute(crossed[:, fifth:], "dp", partners(2))
        sixth = paired.shape[1] // 2
        paired_recv = lax.ppermute(paired[:, sixth:], "dp", partners(1))
        d, gain_parts = attend_back(spans, grad_heads, saved, gain_q, gain_k, cosine, sine)
        mlp_out = mlp_own + mlp_recv.astype(F32)
        block_out = (resid + gate_two_own * mlp_out).astype(BF16)
        early = jnp.concatenate([early[:items], per_item(member_own, grad_out * mlp_out)], axis=1)
        groups = 4 * width // LANES
        early = early.reshape(items, groups, LANES)
        early = jnp.pad(early, ((0, 0), (0, group_rows(groups) - groups), (0, 0)))
        grad_tokens, sums, grad_mod_all, gain_sums, cond_parts = tail(
            dp,
            d,
            attn_in,
            grad_attn_all,
            heads_out,
            w_qkv,
            tokens,
            grad_resid,
            member_own,
            scale_one,
            early.reshape(-1, LANES).astype(BF16),
            gain_parts,
            mod_weight,
            (paired[:, :sixth].astype(F32) + paired_recv.astype(F32)).astype(BF16),
            (crossed[:, :fifth].astype(F32) + crossed_recv.astype(F32)).astype(BF16),
        )
        attn_sum = jnp.concatenate(list(sums[:3]), axis=1)
        grad_up = jnp.concatenate(list(sums[3:5]), axis=1)
        grad_down = jnp.concatenate(list(sums[5:7]), axis=1).T
        grad_gate = jnp.concatenate(list(sums[7:9]), axis=1)
        cond_parts = cond_parts[:, :items, :owned]
    else:
        heads_other = lax.dynamic_slice_in_dim(heads_out, other_first, half, 0)
        heads_own = lax.dynamic_slice_in_dim(heads_out, own_first, half, 0)
        attn_recv = swap(dot(heads_other, proj_weight).astype(BF16))
        attn_out = dot(heads_own, proj_weight) + attn_recv.astype(F32)

        gate_one_own = per_token(member_own, gate_one)
        scale_two_own = per_token(member_own, scale_two)
        resid = tokens_float + gate_one_own * attn_out
        norm_two, inv_two = layer_norm(resid)
        mlp_in = (norm_two * (1.0 + scale_two_own) + per_token(member_own, shift_two)).astype(BF16)
        mlp_in_all = jnp.concatenate([mlp_in, swap(mlp_in)])

        grad_mlp_all = jnp.concatenate(
            [
                (gate_two_own * grad_out).astype(BF16),
                (per_token(member_other, gate_two) * out_grad_other.astype(F32)).astype(BF16),
            ]
        )
        grad_hidden = dot_t(grad_mlp_all, down_weight)

        gate_pre = dot(mlp_in_all, gate_weight)
        up_pre = dot(mlp_in_all, up_weight)
        silu_gate = jax.nn.silu(gate_pre)
        hidden = (silu_gate * up_pre).astype(BF16)
        grad_gate_pre = (grad_hidden * up_pre * silu_grad(gate_pre)).astype(BF16)
        grad_up_pre = (grad_hidden * silu_gate).astype(BF16)

        back_other = dot_t(grad_gate_pre[half:], gate_weight) + dot_t(grad_up_pre[half:], up_weight)
        back_recv = swap(back_other.astype(BF16))
        mlp_recv = swap(dot(hidden[half:], down_weight).astype(BF16))
        grad_mlp_in = (
            dot_t(grad_gate_pre[:half], gate_weight)
            + dot_t(grad_up_pre[:half], up_weight)
            + back_recv.astype(F32)
        )

        grad_mlp_rows = halving_rows(grad_mlp_all, bits)
        mlp_in_rows = halving_rows(mlp_in_all, bits)
        down_part = first_halving(grad_mlp_rows, hidden)
        gate_part = first_halving(mlp_in_rows, grad_gate_pre)
        up_part = first_halving(mlp_in_rows, grad_up_pre)

        mlp_out = dot(hidden[:half], down_weight) + mlp_recv.astype(F32)
        block_out = (resid + gate_two_own * mlp_out).astype(BF16)

        grad_resid = grad_out + norm_back(grad_mlp_in * (1.0 + scale_two_own), norm_two, inv_two)
        grad_attn = (gate_one_own * grad_resid).astype(BF16)
        grad_attn_all = in_order(grad_attn, swap(grad_attn), second)
        grad_heads = dot_t(grad_attn_all, proj_weight).astype(BF16)
        grad_heads, down_part, gate_part, up_part = lax.optimization_barrier(
            (grad_heads, down_part, gate_part, up_part)
        )
        grad_down = rest_of_halving(down_part, bits).T
        grad_gate = rest_of_halving(gate_part, bits)
        grad_up = rest_of_halving(up_part, bits)
        d, gain_parts = attend_back(spans, grad_heads, saved, gain_q, gain_k, cosine, sine)

        early = jnp.concatenate(
            [
                per_item(member_own, grad_resid * attn_out),
                per_item(member_own, grad_mlp_in),
                per_item(member_own, grad_mlp_in * norm_two),
                per_item(member_own, grad_out * mlp_out),
            ],
            axis=1,
        )
        def attn_back(first):
            return dot_t(lax.dynamic_slice_in_dim(d, first, half, 0), w_qkv)

        attn_back_recv = swap(attn_back(other_first).astype(BF16))
        grad_attn_in = attn_back(own_first) + attn_back_recv.astype(F32)
        attn_sum = rest_of_halving(
            jnp.concatenate(
                [
                    first_halving(halving_rows(attn_in, bits), d),
                    first_halving(halving_rows(grad_attn_all, bits), heads_out),
                ],
                axis=1,
            ),
            bits,
        )
        norm_one, inv_one = layer_norm(tokens_float)
        scale_one_own = per_token(member_own, scale_one)
        grad_tokens = (
            grad_resid + norm_back(grad_attn_in * (1.0 + scale_one_own), norm_one, inv_one)
        ).astype(BF16)
        part_mod = jnp.concatenate(
            [per_item(member_own, grad_attn_in), per_item(member_own, grad_attn_in * norm_one), early],
            axis=1,
        )
        gains = jnp.pad(gain_parts[:2].reshape(1, 2 * LANES), ((0, 0), (0, 6 * width - 2 * LANES)))
        part_small = jnp.concatenate([part_mod, gains]).astype(BF16)
        small = part_small.astype(F32) + swap(part_small).astype(F32)
        small_all = lax.all_gather(small.astype(BF16), "dp", axis=0, tiled=False)
        grad_mod_all = small_all[:, :items].reshape(dp * items, 6 * width)
        gain_sums = jnp.sum(small_all[:, items, : 2 * LANES].astype(F32), axis=0).reshape(2, LANES)
        cond_parts = lax.all_to_all(
            dot_t(grad_mod_all, mod_weight).reshape(dp, items, owned),
            "dp",
            split_axis=0,
            concat_axis=0,
            tiled=True,
        )

    grad_mod_weight = t_dot(mod_in_own, grad_mod_all)
    grad_mod_in = cond_parts.transpose(1, 0, 2).reshape(items, dp * owned)
    grad_conditions = silu_grad(conditions.astype(F32)) * grad_mod_in
    grad_q, grad_k, grad_v, grad_proj = (
        attn_sum[:, which * inner : (which + 1) * inner] for which in range(4)
    )
    return (
        block_out,
        grad_tokens,
        grad_conditions,
        grad_mod_weight,
        grad_q,
        grad_k,
        grad_v,
        grad_proj.T,
        gain_sums[0, :HD],
        gain_sums[1, :HD],
        grad_gate,
        grad_up,
        grad_down,
    )


def solution(mesh):
    tokens = P(("dp", "tensor"), None)
    rows = P("dp", None)
    columns = P(None, "tensor")
    inner = P("tensor", None)
    both = P("dp", "tensor")
    turned = P("tensor", "dp")
    return jax.shard_map(
        shards,
        mesh=mesh,
        in_specs=(
            tokens,
            rows,
            rows,
            rows,
            columns,
            columns,
            columns,
            inner,
            P(),
            P(),
            columns,
            columns,
            inner,
            tokens,
        ),
        out_specs=(
            tokens,
            tokens,
            rows,
            rows,
            both,
            both,
            both,
            turned,
            P(),
            P(),
            both,
            both,
            turned,
        ),
        check_vma=False,
    )
```

```python
import functools

import jax
import jax.numpy as jnp
import numpy as np
from jax import lax
from jax.experimental import pallas as pl
from jax.experimental.pallas import tpu as pltpu
from jax.sharding import PartitionSpec as P

HD = 72
QUARTER = HD // 4
LANES = 128
SPAN = 256
TILE = 256
STEP = 32
EPSILON = 1e-06
F32 = jnp.float32
BF16 = jnp.bfloat16
HIGH = lax.Precision.HIGHEST


def silu_grad(values):
    sigma = jax.nn.sigmoid(values)
    return sigma * (1.0 + values * (1.0 - sigma))


def dot(left, right):
    return jnp.dot(left, right, preferred_element_type=F32)


def dot_t(left, right):
    return lax.dot_general(left, right, (((1,), (1,)), ((), ())), preferred_element_type=F32)


def t_dot(left, right):
    return lax.dot_general(left, right, (((0,), (0,)), ((), ())), preferred_element_type=F32)


def geometry(row_grids, length):
    heights = row_grids[:, 0]
    widths = row_grids[:, 1]
    count = row_grids.shape[0]
    sizes = heights * widths
    ends = [sizes[0]]
    for item in range(1, count):
        ends.append(ends[-1] + sizes[item])
    starts = [ends[item] - sizes[item] for item in range(count)]
    positions = jnp.arange(length, dtype=jnp.int32)
    member = jnp.stack(
        [(positions >= starts[item]) & (positions < ends[item]) for item in range(count)], axis=1
    )
    origin = sum(jnp.where(member[:, item], starts[item], 0) for item in range(count))
    width = jnp.maximum(
        sum(jnp.where(member[:, item], widths[item], 0) for item in range(count)), 1
    )
    local = positions - origin
    return member.astype(F32), local // width, local % width


def rope_tables(row_pos, col_pos):
    lane = jnp.arange(LANES)
    frequency = 10000.0 ** (-(lane % QUARTER).astype(F32) / QUARTER)
    along = jnp.where(lane[None, :] < 2 * QUARTER, row_pos[:, None], col_pos[:, None])
    angles = along.astype(F32) * frequency[None, :]
    valid = lane[None, :] < HD
    return jnp.where(valid, jnp.cos(angles), 0.0), jnp.where(valid, jnp.sin(angles), 0.0)


def turn(values):
    lane = lax.broadcasted_iota(jnp.int32, values.shape, 1)
    return jnp.where(
        lane % (2 * QUARTER) < QUARTER,
        -pltpu.roll(values, LANES - QUARTER, 1),
        pltpu.roll(values, QUARTER, 1),
    )


def only_head(values):
    lane = lax.broadcasted_iota(jnp.int32, values.shape, 1)
    return jnp.where(lane < HD, values, jnp.zeros_like(values))


def split_heads(wide, store, heads):
    rows = wide.shape[0]
    wide = jnp.concatenate([wide, jnp.zeros((rows, LANES), wide.dtype)], axis=1)
    for head in range(heads):
        store(head, only_head(wide[:, head * HD : head * HD + LANES]))


def item_spans(grids, items):
    spans = []
    start = 0
    for item in range(items):
        size = grids[item, 0] * grids[item, 1]
        spans.append((start, size))
        start = start + size
    return spans


def members(grids, items, first, count):
    position = lax.broadcasted_iota(jnp.int32, (count, 1), 0) + first
    return [
        jnp.where((position >= start) & (position < start + size), 1.0, 0.0)
        for start, size in item_spans(grids, items)
    ]


def mod_values(masks, mod_ref, kind):
    width = mod_ref.shape[1] // 6
    lanes = slice(kind * width, (kind + 1) * width)
    return sum(mask * mod_ref[item : item + 1, lanes] for item, mask in enumerate(masks))


def padded_gain(gain_ref):
    return jnp.concatenate([gain_ref[...], jnp.zeros((1, LANES - HD), F32)], axis=1)


def attend_kernel(
    heads,
    items,
    grids,
    tokens_ref,
    mod_ref,
    wq_ref,
    wk_ref,
    wv_ref,
    gq_ref,
    gk_ref,
    cos_ref,
    sin_ref,
    x_ref,
    out_ref,
    qpre_ref,
    kpre_ref,
    q_ref,
    k_ref,
    v_ref,
    probs_ref,
    qraw,
    kraw,
    vraw,
    oraw,
    wide,
):
    length = x_ref.shape[0]
    head = pl.program_id(0)

    @pl.when(head == 0)
    def _():
        def norm(index, carry):
            first = pl.multiple_of(index * STEP, STEP)
            rows = pl.ds(first, STEP)
            masks = members(grids, items, first, STEP)
            normed, _ = layer_norm(tokens_ref[rows, :].astype(F32))
            x_ref[rows, :] = (
                normed * (1.0 + mod_values(masks, mod_ref, 1)) + mod_values(masks, mod_ref, 0)
            ).astype(BF16)
            return carry

        lax.fori_loop(0, length // STEP, norm, 0)
        for first in range(0, length, TILE):
            rows = pl.ds(first, TILE)
            x = x_ref[rows, :]
            for w_ref, raw in ((wq_ref, qraw), (wk_ref, kraw), (wv_ref, vraw)):

                def store(h, part, raw=raw):
                    raw[h, rows, :] = part.astype(raw.dtype)

                split_heads(dot_t(x, w_ref[...]), store, heads)

    for raw, pre_ref, low_ref, gain_ref in (
        (qraw, qpre_ref, q_ref, gq_ref),
        (kraw, kpre_ref, k_ref, gk_ref),
    ):
        for first in range(0, length, TILE):
            rows = pl.ds(first, TILE)
            pre = raw[head, rows, :]
            pre_ref[0, rows, :] = pre
            inv = lax.rsqrt(jnp.sum(pre * pre, axis=1, keepdims=True) / HD + EPSILON)
            normed = pre * inv * padded_gain(gain_ref)
            low_ref[0, rows, :] = (
                normed * cos_ref[rows, :] + turn(normed) * sin_ref[rows, :]
            ).astype(BF16)
    v_ref[0] = vraw[head]
    oraw[head] = vraw[head].astype(F32)
    row = lax.broadcasted_iota(jnp.int32, (SPAN, SPAN), 0)
    col = lax.broadcasted_iota(jnp.int32, (SPAN, SPAN), 1)
    row_out = lax.broadcasted_iota(jnp.int32, (SPAN, LANES), 0)
    for item, (start, size) in enumerate(item_spans(grids, items)):
        rows = pl.ds(pl.multiple_of(start, 16), SPAN)
        scores = dot_t(q_ref[0, rows, :], k_ref[0, rows, :]) * HD**-0.5
        scores = jnp.where(col < size, scores, -1e30)
        top = jnp.max(scores, axis=1, keepdims=True)
        weights = jnp.exp(scores - top)
        total = jnp.sum(weights, axis=1, keepdims=True)
        probs = jnp.where(row < size, weights / total, 0.0).astype(BF16)
        probs_ref[0, item] = probs
        mixed = dot(probs, v_ref[0, rows, :])
        oraw[head, rows, :] = jnp.where(row_out < size, mixed, oraw[head, rows, :])

    @pl.when(head == heads - 1)
    def _():
        for h in range(heads):
            wide[:, h * HD : h * HD + HD] = oraw[h][:, :HD]
        out_ref[...] = wide[...].astype(BF16)


def attend_back_kernel(
    heads,
    items,
    grids,
    grad_ref,
    qpre_ref,
    kpre_ref,
    q_ref,
    k_ref,
    v_ref,
    probs_ref,
    gq_ref,
    gk_ref,
    cos_ref,
    sin_ref,
    dq_ref,
    dk_ref,
    dv_ref,
    gain_ref,
    graw,
    dqraw,
    dkraw,
    dvraw,
    wide,
):
    length = grad_ref.shape[0]
    head = pl.program_id(0)

    @pl.when(head == 0)
    def _():
        gain_ref[...] = jnp.zeros_like(gain_ref)
        for first in range(0, length, TILE):
            rows = pl.ds(first, TILE)

            def store(h, part):
                graw[h, rows, :] = part.astype(BF16)

            split_heads(grad_ref[rows, :].astype(F32), store, heads)

    dqraw[head] = jnp.zeros((length, LANES), F32)
    dkraw[head] = jnp.zeros((length, LANES), F32)
    row_all = lax.broadcasted_iota(jnp.int32, (length, LANES), 0)
    used = sum(item_spans(grids, items)[-1])
    dvraw[head] = jnp.where(row_all >= used, graw[head].astype(F32), 0.0)
    for item, (start, _) in enumerate(item_spans(grids, items)):
        rows = pl.ds(pl.multiple_of(start, 16), SPAN)
        probs_low = probs_ref[0, item]
        probs = probs_low.astype(F32)
        grad = graw[head, rows, :]
        grad_probs = dot_t(grad, v_ref[0, rows, :])
        inner = jnp.sum(probs * grad_probs, axis=1, keepdims=True) / jnp.maximum(
            jnp.sum(probs, axis=1, keepdims=True), 0.5
        )
        grad_scores = (probs * (grad_probs - inner)).astype(BF16)
        dqraw[head, rows, :] += dot(grad_scores, k_ref[0, rows, :])
        dkraw[head, rows, :] += t_dot(grad_scores, q_ref[0, rows, :])
        dvraw[head, rows, :] += t_dot(probs_low, grad)

    for raw, pre_ref, g_ref, which in (
        (dqraw, qpre_ref, gq_ref, 0),
        (dkraw, kpre_ref, gk_ref, 1),
    ):
        for first in range(0, length, TILE):
            rows = pl.ds(first, TILE)
            turned = raw[head, rows, :] * HD**-0.5
            normed = turned * cos_ref[rows, :] - turn(turned * sin_ref[rows, :])
            pre = pre_ref[0, rows, :]
            inv = lax.rsqrt(jnp.sum(pre * pre, axis=1, keepdims=True) / HD + EPSILON)
            unit = pre * inv
            gain_ref[which : which + 1, :] += jnp.sum(normed * unit, axis=0, keepdims=True)
            scaled = normed * padded_gain(g_ref)
            along = jnp.sum(scaled * unit, axis=1, keepdims=True) / HD
            raw[head, rows, :] = inv * (scaled - unit * along)

    @pl.when(head == heads - 1)
    def _():
        for raw, o_ref in ((dqraw, dq_ref), (dkraw, dk_ref), (dvraw, dv_ref)):
            for h in range(heads):
                wide[:, h * HD : h * HD + HD] = raw[h][:, :HD]
            o_ref[...] = wide[...].astype(BF16)


def whole(shape):
    return pl.BlockSpec(shape, lambda h, grids: (0,) * len(shape))


def per_head(shape):
    return pl.BlockSpec((1,) + shape, lambda h, grids: (h,) + (0,) * len(shape))


def attend(grids, tokens, mod, wq, wk, wv, gain_q, gain_k, cosine, sine):
    length, width = tokens.shape
    heads = wq.shape[0] // HD
    items = grids.shape[0]
    head_f32 = jax.ShapeDtypeStruct((heads, length, LANES), F32)
    head_low = jax.ShapeDtypeStruct((heads, length, LANES), BF16)
    return pl.pallas_call(
        functools.partial(attend_kernel, heads, items),
        grid_spec=pltpu.PrefetchScalarGridSpec(
            num_scalar_prefetch=1,
            grid=(heads,),
            in_specs=[
                whole(tokens.shape),
                whole(mod.shape),
                whole(wq.shape),
                whole(wk.shape),
                whole(wv.shape),
                whole((1, HD)),
                whole((1, HD)),
                whole((length, LANES)),
                whole((length, LANES)),
            ],
            out_specs=[
                whole((length, width)),
                whole((length, heads * HD)),
                per_head((length, LANES)),
                per_head((length, LANES)),
                per_head((length, LANES)),
                per_head((length, LANES)),
                per_head((length, LANES)),
                per_head((items, SPAN, SPAN)),
            ],
            scratch_shapes=[
                pltpu.VMEM((heads, length, LANES), F32),
                pltpu.VMEM((heads, length, LANES), F32),
                pltpu.VMEM((heads, length, LANES), BF16),
                pltpu.VMEM((heads, length, LANES), F32),
                pltpu.VMEM((length, heads * HD), F32),
            ],
        ),
        out_shape=[
            jax.ShapeDtypeStruct((length, width), BF16),
            jax.ShapeDtypeStruct((length, heads * HD), BF16),
            head_f32,
            head_f32,
            head_low,
            head_low,
            head_low,
            jax.ShapeDtypeStruct((heads, items, SPAN, SPAN), BF16),
        ],
        compiler_params=pltpu.CompilerParams(vmem_limit_bytes=56 * 2**20),
        cost_estimate=pl.CostEstimate(
            flops=2 * length * width * heads * HD * 3 + 4 * heads * items * SPAN * SPAN * LANES,
            bytes_accessed=24 * 2**20,
            transcendentals=heads * items * SPAN * SPAN,
        ),
        name="attend",
    )(grids, tokens, mod, wq, wk, wv, gain_q, gain_k, cosine, sine)


def attend_back(grids, grad, saved, gain_q, gain_k, cosine, sine):
    length, width = grad.shape
    heads = width // HD
    items = grids.shape[0]
    out = jax.ShapeDtypeStruct((length, width), BF16)
    return pl.pallas_call(
        functools.partial(attend_back_kernel, heads, items),
        grid_spec=pltpu.PrefetchScalarGridSpec(
            num_scalar_prefetch=1,
            grid=(heads,),
            in_specs=[
                whole(grad.shape),
                per_head((length, LANES)),
                per_head((length, LANES)),
                per_head((length, LANES)),
                per_head((length, LANES)),
                per_head((length, LANES)),
                per_head((items, SPAN, SPAN)),
                whole((1, HD)),
                whole((1, HD)),
                whole((length, LANES)),
                whole((length, LANES)),
            ],
            out_specs=[
                whole((length, width)),
                whole((length, width)),
                whole((length, width)),
                whole((8, LANES)),
            ],
            scratch_shapes=[
                pltpu.VMEM((heads, length, LANES), BF16),
                pltpu.VMEM((heads, length, LANES), F32),
                pltpu.VMEM((heads, length, LANES), F32),
                pltpu.VMEM((heads, length, LANES), F32),
                pltpu.VMEM((length, width), F32),
            ],
        ),
        out_shape=[out, out, out, jax.ShapeDtypeStruct((8, LANES), F32)],
        compiler_params=pltpu.CompilerParams(vmem_limit_bytes=56 * 2**20),
        cost_estimate=pl.CostEstimate(
            flops=8 * heads * items * SPAN * SPAN * LANES,
            bytes_accessed=24 * 2**20,
            transcendentals=0,
        ),
        name="attend_back",
    )(grids, grad, *saved, gain_q, gain_k, cosine, sine)


def layer_norm(values):
    centred = values - jnp.mean(values, axis=1, keepdims=True)
    inv_std = lax.rsqrt(jnp.mean(centred * centred, axis=1, keepdims=True) + EPSILON)
    return (centred * inv_std, inv_std)


def norm_back(grad_norm, normed, inv_std):
    return inv_std * (
        grad_norm
        - jnp.mean(grad_norm, axis=1, keepdims=True)
        - normed * jnp.mean(grad_norm * normed, axis=1, keepdims=True)
    )


def per_token(member, rows):
    return sum(member[:, item, None] * rows[item][None, :] for item in range(rows.shape[0]))


def per_item(member, values):
    return jnp.stack(
        [jnp.sum(member[:, item, None] * values, axis=0) for item in range(member.shape[1])]
    )


def swap(values):
    return lax.ppermute(values, "tensor", [(0, 1), (1, 0)])


def in_order(own, other, second):
    return jnp.concatenate([jnp.where(second, other, own), jnp.where(second, own, other)])


def halving_rows(values, bits):
    dp = 2**bits
    depth = values.shape[1] // dp
    blocks = values.T.reshape((2,) * bits + (depth, values.shape[0]))
    me = lax.axis_index("dp")
    for bit in range(bits):
        axis = bits - 1 - bit
        blocks = jnp.where((me >> bit) & 1 == 1, jnp.flip(blocks, axis), blocks)
    blocks = blocks.transpose(tuple(range(bits - 1, -1, -1)) + (bits, bits + 1))
    return blocks.reshape(dp * depth, values.shape[0])


def first_halving(rows, grads):
    half = rows.shape[0] // 2
    sent = lax.ppermute(dot(rows[half:], grads).astype(BF16), "dp", partners(0))
    return (dot(rows[:half], grads) + sent.astype(F32)).astype(BF16)


def partners(bit):
    return [(i, i ^ (1 << bit)) for i in range(lax.axis_size("dp"))]


def rest_of_halving(part, bits):
    for bit in range(1, bits):
        half = part.shape[0] // 2
        sent = lax.ppermute(part[half:], "dp", partners(bit))
        part = part[:half].astype(F32) + sent.astype(F32)
        if bit < bits - 1:
            part = part.astype(BF16)
    return part.astype(F32)


def remote(src, dst, send, recv, device):
    return pltpu.make_async_remote_copy(
        src_ref=src,
        dst_ref=dst,
        send_sem=send,
        recv_sem=recv,
        device_id=device,
        device_id_type=pl.DeviceIdType.MESH,
    )


def block_at(position, me, order):
    block = 0
    for level, bit in enumerate(order):
        mine = (me // (1 << bit)) % 2
        there = (position >> (len(order) - 1 - level)) & 1
        block = block + (1 << bit) * (1 - mine if there else mine)
    return block


def across(me, bit):
    return me + (1 << bit) - 2 * (1 << bit) * ((me // (1 << bit)) % 2)


def group_rows(count):
    return -(-count // 16) * 16


def greet(peers):
    barrier = pltpu.get_barrier_semaphore()
    for peer in peers:
        pl.semaphore_signal(
            barrier, inc=1, device_id=peer, device_id_type=pl.DeviceIdType.MESH
        )
    pl.semaphore_wait(barrier, len(peers))


def tail_kernel(
    dp,
    items,
    dq_ref,
    dk_ref,
    dv_ref,
    attn_in_ref,
    grad_attn_ref,
    heads_ref,
    paired_keep_ref,
    paired_in_ref,
    early_ref,
    gain_ref,
    mod_ref,
    cond_ref,
    grids,
    wq_hbm,
    wk_hbm,
    wv_hbm,
    tokens_hbm,
    own_grad_hbm,
    grad_resid_hbm,
    resid_hbm,
    mlp_own_hbm,
    mlp_in_hbm,
    mod_weight_hbm,
    grad_tokens_ref,
    block_out_ref,
    sums_ref,
    all_ref,
    gains_ref,
    grad_cond_ref,
    wq_ref,
    wk_ref,
    wv_ref,
    tokens_ref,
    own_grad_ref,
    grad_resid_ref,
    resid_ref,
    mlp_own_ref,
    mlp_in_ref,
    mod_weight_ref,
    part,
    y_out,
    y_in,
    back,
    core_out,
    core_in,
    core_keep,
    x_out,
    x_in,
    x_keep,
    z_out,
    z_in,
    z_keep,
    w_out,
    w_in,
    early_rows,
    early_out,
    early_in,
    early_all,
    late_rows,
    late_out,
    late_in,
    late_all,
    flat,
    cond_out,
    cond_in,
    load_sems,
    y_sems,
    halving_sems,
    early_sems,
    late_sems,
    cond_send,
    cond_recv,
):
    bits = dp.bit_length() - 1
    me = lax.axis_index("dp")
    ten = lax.axis_index("tensor")
    half, width = grad_tokens_ref.shape
    depth = width // dp
    inner = dq_ref.shape[1]
    pieces, _, piece = core_out.shape
    paired = paired_keep_ref.shape[0]
    groups = width // LANES
    early_span = early_out.shape[0] // items
    late_span = late_out.shape[0] // items
    y_peer = (me, 1 - ten)
    dp_peers = [((me + step) % dp, ten) for step in range(1, dp)]
    loads = [
        pltpu.make_async_copy(source, there, load_sems.at[which])
        for which, (source, there) in enumerate(
            (
                (wq_hbm, wq_ref),
                (wk_hbm, wk_ref),
                (wv_hbm, wv_ref),
                (own_grad_hbm, own_grad_ref),
                (resid_hbm, resid_ref),
                (mlp_own_hbm, mlp_own_ref),
                (mlp_in_hbm, mlp_in_ref),
                (tokens_hbm, tokens_ref),
                (grad_resid_hbm, grad_resid_ref),
                (mod_weight_hbm, mod_weight_ref),
            )
        )
    ]
    for load in loads:
        load.start()
    greet([y_peer] + dp_peers)

    def y_copy(which, src, dst):
        return remote(src, dst, y_sems.at[0, which], y_sems.at[1, which], y_peer)

    orders = {p: (0, 1, 2, 3) for p in range(paired + pieces)}
    orders[paired + pieces - 1] = (0, 2, 3, 1)
    early_order = (1, 2, 3, 0)
    late_order = (2, 3, 0, 1)

    def halving(level, which, src, dst):
        return remote(
            src,
            dst,
            halving_sems.at[0, level, which],
            halving_sems.at[1, level, which],
            (across(me, orders[which][level]), ten),
        )

    def doubling(level, slots, sems, order):
        count = 1 << level
        return remote(
            slots.at[pl.ds(0, count)],
            slots.at[pl.ds(count, count)],
            sems.at[0, level],
            sems.at[1, level],
            (across(me, order[level]), ten),
        )

    def in_steps(body):
        def one(index, carry):
            body(pl.multiple_of(index * STEP, STEP))
            return carry

        lax.fori_loop(0, half // STEP, one, 0)

    last_copies = {}

    def last_level(p, total):
        w_out[p, depth:, :] = jnp.zeros((w_out.shape[1] - depth, piece), BF16)
        w_out[p, :depth, :] = total[depth:].astype(BF16)
        last_copies[p] = halving(3, p, w_out.at[p], w_in.at[p])
        last_copies[p].start()
        sums_ref[p] = total[:depth]

    def paired_sum(p, rows):
        return paired_keep_ref[p, rows, :].astype(F32) + paired_in_ref[p, rows, :].astype(F32)

    z_copies = []
    for p in range(paired):
        z_out[p] = paired_sum(p, pl.ds(2 * depth, 2 * depth)).astype(BF16)
        z_copies.append(halving(2, p, z_out.at[p], z_in.at[p]))
        z_copies[p].start()

    for load in loads[3:7]:
        load.wait()
    grad_cond_ref[...] = jnp.zeros_like(grad_cond_ref)

    def finish_block(first):
        rows = pl.ds(first, STEP)
        masks = members(grids, items, ten * half + first, STEP)
        mlp_out = mlp_own_ref[rows, :] + mlp_in_ref[rows, :].astype(F32)
        block_out_ref[rows, :] = (
            resid_ref[rows, :] + mod_values(masks, mod_ref, 5) * mlp_out
        ).astype(BF16)
        product = own_grad_ref[rows, :].astype(F32) * mlp_out
        for item in range(items):
            grad_cond_ref[item : item + 1, :] += jnp.sum(
                masks[item] * product, axis=0, keepdims=True
            )

    in_steps(finish_block)
    early_rows[...] = jnp.zeros_like(early_rows)
    for item in range(items):
        for group in range(4 * groups):
            row = item * early_span + group
            source = early_ref if group < 3 * groups else grad_cond_ref
            lane = (group if group < 3 * groups else group - 3 * groups) * LANES
            early_rows[row : row + 1, :] = source[item : item + 1, lane : lane + LANES]
    early_out[...] = early_rows[...].astype(BF16)
    early_copy = y_copy(0, early_out, early_in)
    early_copy.start()

    for load in loads[:3]:
        load.wait()

    def attn_back(first):
        rows = pl.ds(pl.multiple_of(first, half), half)
        return (
            dot(dq_ref[rows, :], wq_ref[...])
            + dot(dk_ref[rows, :], wk_ref[...])
            + dot(dv_ref[rows, :], wv_ref[...])
        )

    y_out[...] = attn_back((1 - ten) * half).astype(BF16)
    back_copy = y_copy(1, y_out, y_in)
    back_copy.start()
    early_copy.wait_recv()
    early_all[0] = (early_out[...].astype(F32) + early_in[...].astype(F32)).astype(BF16)
    early_copies = [doubling(level, early_all, early_sems, early_order) for level in range(bits)]
    early_copies[0].start()

    def weight_grad(which, left, right):
        columns = slice(which * inner, (which + 1) * inner)
        for first in range(0, width, LANES):
            rows = pl.ds(first, LANES)
            part[rows, columns] = t_dot(left[:, rows], right[...])

    core_copies = []

    def send_core(p):
        columns = pl.ds(p * piece, piece)

        def packed(position):
            def rows_of(at):
                block = block_at(at, me, orders[paired + p])
                return part[pl.ds(pl.multiple_of(block * depth, 8), depth), columns]

            return jnp.concatenate([rows_of(position), rows_of(position + 1)]).astype(BF16)

        for position in range(0, dp // 2, 2):
            core_out[p, pl.ds(position * depth, 2 * depth), :] = packed(dp // 2 + position)
        core_copies.append(halving(0, paired + p, core_out.at[p], core_in.at[p]))
        core_copies[p].start()
        for position in range(0, dp // 2, 2):
            core_keep[p, pl.ds(position * depth, 2 * depth), :] = packed(position)

    x_copies = []

    def cross(p):
        core_copies[p].wait_recv()
        for rows, there in (
            (pl.ds(4 * depth, 4 * depth), x_out),
            (pl.ds(0, 4 * depth), x_keep),
        ):
            there[p] = (core_keep[p, rows, :].astype(F32) + core_in[p, rows, :].astype(F32)).astype(
                BF16
            )
        x_copies.append(halving(1, paired + p, x_out.at[p], x_in.at[p]))
        x_copies[p].start()

    weight_grad(0, attn_in_ref, dq_ref)
    early_copies[0].wait_recv()
    early_copies[1].start()
    weight_grad(1, attn_in_ref, dk_ref)
    send_core(0)
    early_copies[1].wait_recv()
    early_copies[2].start()
    cross(0)
    weight_grad(2, attn_in_ref, dv_ref)
    send_core(1)
    early_copies[2].wait_recv()
    early_copies[3].start()
    weight_grad(3, grad_attn_ref, heads_ref)
    send_core(2)
    cross(1)
    cross(2)
    for p in range(paired):
        z_copies[p].wait_recv()
        last_level(p, paired_sum(p, pl.ds(0, 2 * depth)) + z_in[p].astype(F32))
    back[...] = attn_back(ten * half)
    count = dp * items

    def unpack(all_here, span, order, first_group, size):
        rows = items * span
        for slot in range(dp):
            source = block_at(slot, me, order[::-1])
            there = pl.multiple_of(source * rows, 16)
            flat[pl.ds(there, rows), :] = all_here[slot].astype(F32)
        for group in range(size):
            lanes = pl.ds((first_group + group) * LANES, LANES)
            all_ref[:, lanes] = flat[pl.ds(group, count, stride=span), :].astype(BF16)

    early_copies[3].wait_recv()
    unpack(early_all, early_span, early_order, 2 * groups, 4 * groups)

    def descend(p):
        there = paired + p
        x_copies[p].wait_recv()
        for rows, target in (
            (pl.ds(2 * depth, 2 * depth), z_out),
            (pl.ds(0, 2 * depth), z_keep),
        ):
            total = x_keep[p, rows, :].astype(F32) + x_in[p, rows, :].astype(F32)
            target[there if target is z_out else p] = total.astype(BF16)
        copy = halving(2, there, z_out.at[there], z_in.at[there])
        copy.start()
        descents[p] = copy

    def finish_halving(p):
        descents[p].wait_recv()
        last_level(paired + p, z_keep[p].astype(F32) + z_in[paired + p].astype(F32))

    descents = {}

    for load in loads[7:]:
        load.wait()
    back_copy.wait_recv()
    grad_cond_ref[...] = jnp.zeros_like(grad_cond_ref)
    gains_ref[...] = jnp.zeros_like(gains_ref)

    def norm_grad(first):
        rows = pl.ds(first, STEP)
        masks = members(grids, items, ten * half + first, STEP)
        normed, inv = layer_norm(tokens_ref[rows, :].astype(F32))
        grad = back[rows, :] + y_in[rows, :].astype(F32)
        n = grad * (1.0 + mod_values(masks, mod_ref, 1))
        grad_tokens_ref[rows, :] = (grad_resid_ref[rows, :] + norm_back(n, normed, inv)).astype(BF16)
        product = grad * normed
        for item in range(items):
            grad_cond_ref[item : item + 1, :] += jnp.sum(masks[item] * grad, axis=0, keepdims=True)
            gains_ref[item : item + 1, :] += jnp.sum(masks[item] * product, axis=0, keepdims=True)

    in_steps(norm_grad)
    late_rows[...] = jnp.zeros_like(late_rows)
    for item in range(items):
        for group in range(2 * groups):
            row = item * late_span + group
            source = grad_cond_ref if group < groups else gains_ref
            lane = (group % groups) * LANES
            late_rows[row : row + 1, :] = source[item : item + 1, lane : lane + LANES]
    late_rows[2 * groups : 2 * groups + 2, :] = gain_ref[:2, :]
    late_out[...] = late_rows[...].astype(BF16)
    late_copy = y_copy(2, late_out, late_in)
    late_copy.start()
    descend(0)
    late_copy.wait_recv()
    late_all[0] = (late_out[...].astype(F32) + late_in[...].astype(F32)).astype(BF16)
    late_copies = [doubling(level, late_all, late_sems, late_order) for level in range(bits)]
    late_copies[0].start()
    descend(2)
    late_copies[0].wait_recv()
    late_copies[1].start()
    finish_halving(0)
    late_copies[1].wait_recv()
    late_copies[2].start()
    late_copies[2].wait_recv()
    late_copies[3].start()
    descend(1)
    finish_halving(2)
    late_copies[3].wait_recv()
    unpack(late_all, late_span, late_order, 0, 2 * groups)
    finish_halving(1)
    gains = jnp.zeros((2, LANES), F32)
    for source in range(dp):
        row = source * items * late_span + 2 * groups
        gains += flat[row : row + 2, :]
    gains_ref[:2, :LANES] = gains
    flat[:count, :depth] = dot_t(all_ref[...], mod_weight_ref[...])
    cond_out[...] = jnp.zeros_like(cond_out)
    for dest in range(dp):
        cond_out[dest, :items, :depth] = flat[pl.ds(dest * items, items), :depth]
    cond_in[me] = cond_out[me]
    cond_copies = []
    for step, peer in enumerate(dp_peers):
        cond_copies.append(
            remote(cond_out.at[peer[0]], cond_in.at[me], cond_send.at[step], cond_recv.at[me], peer)
        )
        cond_copies[-1].start()
    for step in range(1, dp):
        source = (me + dp - step) % dp
        remote(
            cond_out.at[0], cond_in.at[source], cond_send.at[0], cond_recv.at[source], y_peer
        ).wait_recv()
    for source in range(dp):
        grad_cond_ref[:, source * depth : (source + 1) * depth] = cond_in[source, :, :depth]
    values = cond_ref[...].astype(F32)
    grad_cond_ref[:items, :] = grad_cond_ref[:items, :] * silu_grad(values)
    for p in last_copies:
        last_copies[p].wait_recv()
        sums_ref[p] += w_in[p, :depth, :].astype(F32)
    for copy in (
        [early_copy, back_copy, late_copy]
        + early_copies
        + late_copies
        + cond_copies
        + core_copies
        + x_copies
        + z_copies
        + list(descents.values())
        + list(last_copies.values())
    ):
        copy.wait_send()


def tail(
    dp,
    d,
    attn_in,
    grad_attn,
    heads_out,
    paired_keep,
    paired_in,
    early,
    gains,
    mod,
    conditions,
    grids,
    weights,
    tokens,
    own_grad,
    grad_resid,
    resid,
    mlp_own,
    mlp_in,
    mod_weight,
):
    half, width = tokens.shape
    items = grids.shape[0]
    length = 2 * half
    inner = d[0].shape[1]
    depth = width // dp
    pieces = 3
    piece = 4 * inner // pieces
    groups = width // LANES
    early_rows = items * group_rows(4 * groups)
    late_rows = items * group_rows(2 * groups + 2)
    count = dp * items
    paired = paired_keep.shape[0]
    total = pieces + paired
    columns = mod_weight.shape[1]
    vmem = pltpu.VMEM
    dma = pltpu.SemaphoreType.DMA
    anywhere = pl.BlockSpec(memory_space=pl.ANY)
    in_vmem = pl.BlockSpec(memory_space=pltpu.VMEM)
    later = (*weights, tokens, own_grad, grad_resid, resid, mlp_own, mlp_in, mod_weight)
    return pl.pallas_call(
        functools.partial(tail_kernel, dp, items),
        out_shape=[
            jax.ShapeDtypeStruct((half, width), BF16),
            jax.ShapeDtypeStruct((half, width), BF16),
            jax.ShapeDtypeStruct((total, depth, piece), F32),
            jax.ShapeDtypeStruct((count, columns), BF16),
            jax.ShapeDtypeStruct((8, width), F32),
            jax.ShapeDtypeStruct((8, width), F32),
        ],
        in_specs=[in_vmem] * 12
        + [pl.BlockSpec(memory_space=pltpu.SMEM)]
        + [anywhere] * len(later),
        out_specs=[in_vmem] * 6,
        scratch_shapes=[
            *[vmem(array.shape, array.dtype) for array in later],
            vmem((width, 4 * inner), F32),
            vmem((half, width), BF16),
            vmem((half, width), BF16),
            vmem((half, width), F32),
            vmem((pieces, width // 2, piece), BF16),
            vmem((pieces, width // 2, piece), BF16),
            vmem((pieces, width // 2, piece), BF16),
            vmem((pieces, width // 4, piece), BF16),
            vmem((pieces, width // 4, piece), BF16),
            vmem((pieces, width // 4, piece), BF16),
            vmem((total, width // 8, piece), BF16),
            vmem((total, width // 8, piece), BF16),
            vmem((pieces, width // 8, piece), BF16),
            vmem((total, group_rows(depth), piece), BF16),
            vmem((total, group_rows(depth), piece), BF16),
            vmem((early_rows, LANES), F32),
            vmem((early_rows, LANES), BF16),
            vmem((early_rows, LANES), BF16),
            vmem((dp, early_rows, LANES), BF16),
            vmem((late_rows, LANES), F32),
            vmem((late_rows, LANES), BF16),
            vmem((late_rows, LANES), BF16),
            vmem((dp, late_rows, LANES), BF16),
            vmem((dp * early_rows, LANES), F32),
            vmem((dp, 8, LANES), F32),
            vmem((dp, 8, LANES), F32),
            dma((len(later),)),
            dma((2, 3)),
            dma((2, 4, total)),
            dma((2, 4)),
            dma((2, 4)),
            dma((dp,)),
            dma((dp,)),
        ],
        compiler_params=pltpu.CompilerParams(
            collective_id=1, has_side_effects=True, vmem_limit_bytes=62 * 2**20
        ),
        cost_estimate=pl.CostEstimate(
            flops=4 * length * width * 4 * inner, bytes_accessed=20 * 2**20, transcendentals=0
        ),
        name="tail",
    )(
        *d,
        attn_in,
        grad_attn,
        heads_out,
        paired_keep,
        paired_in,
        early,
        gains,
        mod,
        conditions,
        grids,
        *later,
    )


def head_kernel(
    dp,
    cond_ref,
    mod_weight_ref,
    tokens_ref,
    grids,
    frequency_ref,
    mod_ref,
    mod_in_ref,
    tokens_all_ref,
    cos_ref,
    sin_ref,
    cond_out,
    cond_in,
    gathered,
    flat,
    out_0,
    in_0,
    out_1,
    in_1,
    keep_1,
    out_2,
    in_2,
    keep_2,
    out_3,
    in_3,
    halves,
    cond_send,
    cond_recv,
    halving_sems,
    y_sems,
):
    bits = dp.bit_length() - 1
    me = lax.axis_index("dp")
    ten = lax.axis_index("tensor")
    items = cond_ref.shape[0]
    half, width = tokens_ref.shape
    depth = width // dp
    count = dp * items
    groups = mod_weight_ref.shape[1] // LANES // 2
    span = flat.shape[0] // count
    block = items * span
    y_peer = (me, 1 - ten)
    dp_peers = [((me + step) % dp, ten) for step in range(1, dp)]

    cond_out[...] = jnp.zeros_like(cond_out)
    values = cond_ref[...].astype(F32)
    for dest in range(dp):
        cond_out[dest, :items, :depth] = values[:, dest * depth : (dest + 1) * depth]
    greet([y_peer] + dp_peers)
    cond_in[me] = cond_out[me]
    cond_copies = []
    for step, peer in enumerate(dp_peers):
        cond_copies.append(
            remote(cond_out.at[peer[0]], cond_in.at[me], cond_send.at[step], cond_recv.at[me], peer)
        )
        cond_copies[-1].start()
    own_rows = pl.ds(pl.multiple_of(ten * half, half), half)
    tokens_copy = remote(
        tokens_ref, tokens_all_ref.at[own_rows, :], y_sems.at[0, 0], y_sems.at[1, 0], y_peer
    )
    tokens_copy.start()
    tokens_all_ref[own_rows, :] = tokens_ref[...]
    for step in range(1, dp):
        source = (me + dp - step) % dp
        remote(
            cond_out.at[0], cond_in.at[source], cond_send.at[0], cond_recv.at[source], y_peer
        ).wait_recv()
    for source in range(dp):
        gathered[pl.ds(source * items, items), :] = cond_in[source, :items, :]
    raw = gathered[...]
    mod_in = (raw / (1.0 + jnp.exp(-raw))).astype(BF16)
    mod_in_ref[...] = mod_in

    for group in range(groups):
        lanes = pl.ds(pl.multiple_of((ten * groups + group) * LANES, LANES), LANES)
        flat[pl.ds(group, count, stride=span), :] = dot(mod_in[:, :depth], mod_weight_ref[:, lanes])

    def rows_of(position):
        return pl.ds(pl.multiple_of(block_at(position, me, range(bits)) * block, 8), block)

    def at(position):
        return pl.ds(position * block, block)

    def halving(bit, src, dst):
        copy = remote(
            src, dst, halving_sems.at[0, bit], halving_sems.at[1, bit], (across(me, bit), ten)
        )
        copy.start()
        return copy

    for position in range(dp // 2):
        out_0[at(position), :] = flat[rows_of(dp // 2 + position), :]
    copies = [halving(0, out_0, in_0)]

    lane = lax.broadcasted_iota(jnp.int32, (STEP, LANES), 1)

    def tables(first, last):
        def one(index, carry):
            first = pl.multiple_of(index * STEP, STEP)
            rows = pl.ds(first, STEP)
            position = lax.broadcasted_iota(jnp.int32, (STEP, LANES), 0) + first
            origin = jnp.zeros((STEP, LANES), jnp.int32)
            breadth = jnp.ones((STEP, LANES), jnp.int32)
            for item, (start, size) in enumerate(item_spans(grids, items)):
                inside = (position >= start) & (position < start + size)
                origin = jnp.where(inside, start, origin)
                breadth = jnp.where(inside, grids[item, 1], breadth)
            local = (position - origin).astype(F32)
            breadth = breadth.astype(F32)
            down = jnp.floor((local + 0.5) / breadth)
            angles = jnp.where(lane < 2 * QUARTER, down, local - down * breadth) * frequency_ref[...]
            cos_ref[rows, :] = jnp.where(lane < HD, jnp.cos(angles), 0.0)
            sin_ref[rows, :] = jnp.where(lane < HD, jnp.sin(angles), 0.0)
            return carry

        lax.fori_loop(first, last, one, 0)

    steps = 2 * half // STEP
    tables(0, steps // 3)
    copies[0].wait_recv()
    for position in range(dp // 4):
        out_1[at(position), :] = flat[rows_of(dp // 4 + position), :] + in_0[at(dp // 4 + position), :]
    copies.append(halving(1, out_1, in_1))
    for position in range(dp // 4):
        keep_1[at(position), :] = flat[rows_of(position), :] + in_0[at(position), :]
    tables(steps // 3, 2 * steps // 3)
    copies[1].wait_recv()
    for position in range(dp // 8):
        later = at(dp // 8 + position)
        out_2[at(position), :] = keep_1[later, :] + in_1[later, :]
    copies.append(halving(2, out_2, in_2))
    for position in range(dp // 8):
        keep_2[at(position), :] = keep_1[at(position), :] + in_1[at(position), :]
    tables(2 * steps // 3, steps)
    copies[2].wait_recv()
    out_3[...] = keep_2[at(1), :] + in_2[at(1), :]
    copies.append(halving(3, out_3, in_3))
    copies[3].wait_recv()
    halves[ten] = keep_2[at(0), :] + in_2[at(0), :] + in_3[...]
    mod_copy = remote(halves.at[ten], halves.at[ten], y_sems.at[0, 1], y_sems.at[1, 1], y_peer)
    mod_copy.start()
    mod_ref[...] = jnp.zeros_like(mod_ref)
    remote(
        halves.at[1 - ten], halves.at[1 - ten], y_sems.at[0, 1], y_sems.at[1, 1], y_peer
    ).wait_recv()
    for side in range(2):
        for item in range(items):
            for group in range(groups):
                first = (side * groups + group) * LANES
                row = item * span + group
                mod_ref[item : item + 1, first : first + LANES] = halves[side, row : row + 1, :]
    tokens_copy.wait_recv()
    for copy in cond_copies + copies + [tokens_copy, mod_copy]:
        copy.wait_send()


def head(dp, conditions, mod_weight, tokens, grids, frequency):
    half, width = tokens.shape
    items = conditions.shape[0]
    count = dp * items
    groups = mod_weight.shape[1] // LANES // 2
    span = -(-groups // 8) * 8
    block = items * span
    vmem = pltpu.VMEM
    dma = pltpu.SemaphoreType.DMA
    in_vmem = pl.BlockSpec(memory_space=pltpu.VMEM)
    return pl.pallas_call(
        functools.partial(head_kernel, dp),
        out_shape=[
            jax.ShapeDtypeStruct((8, 6 * width), F32),
            jax.ShapeDtypeStruct((count, LANES), BF16),
            jax.ShapeDtypeStruct((2 * half, width), BF16),
            jax.ShapeDtypeStruct((2 * half, LANES), F32),
            jax.ShapeDtypeStruct((2 * half, LANES), F32),
        ],
        in_specs=[in_vmem] * 3 + [pl.BlockSpec(memory_space=pltpu.SMEM), in_vmem],
        out_specs=[in_vmem] * 5,
        scratch_shapes=[
            vmem((dp, 8, LANES), F32),
            vmem((dp, 8, LANES), F32),
            vmem((count, LANES), F32),
            vmem((count * span, LANES), F32),
            vmem((dp // 2 * block, LANES), F32),
            vmem((dp // 2 * block, LANES), F32),
            vmem((dp // 4 * block, LANES), F32),
            vmem((dp // 4 * block, LANES), F32),
            vmem((dp // 4 * block, LANES), F32),
            vmem((dp // 8 * block, LANES), F32),
            vmem((dp // 8 * block, LANES), F32),
            vmem((dp // 8 * block, LANES), F32),
            vmem((block, LANES), F32),
            vmem((block, LANES), F32),
            vmem((2, block, LANES), F32),
            dma((dp,)),
            dma((dp,)),
            dma((2, 4)),
            dma((2, 2)),
        ],
        compiler_params=pltpu.CompilerParams(
            collective_id=3, has_side_effects=True, vmem_limit_bytes=40 * 2**20
        ),
        cost_estimate=pl.CostEstimate(
            flops=2 * count * width // dp * 6 * width, bytes_accessed=8 * 2**20, transcendentals=0
        ),
        name="head",
    )(conditions, mod_weight, tokens, grids, frequency)


def middle_kernel(
    items,
    chunk,
    step,
    heads_ref,
    proj_ref,
    tokens_ref,
    own_grad_ref,
    other_grad_ref,
    grids,
    mod_ref,
    gate_hbm,
    up_hbm,
    down_hbm,
    grad_heads_ref,
    grad_attn_ref,
    grad_resid_ref,
    resid_ref,
    early_ref,
    mlp_other_ref,
    mlp_own_ref,
    last_keep_ref,
    last_out_ref,
    paired_keep_ref,
    paired_out_ref,
    gate_ref,
    up_ref,
    down_ref,
    attn,
    grad_mlp,
    mlp_in,
    hidden,
    grad_gate,
    grad_up,
    y_out,
    y_in,
    part,
    core_out,
    core_keep,
    core_in,
    x_out,
    x_in,
    x_keep,
    z_in,
    y_sems,
    core_sems,
    x_sems,
    z_sems,
    load_sems,
):
    dp = lax.axis_size("dp")
    bits = dp.bit_length() - 1
    me = lax.axis_index("dp")
    ten = lax.axis_index("tensor")
    half, width = tokens_ref.shape
    depth = width // dp
    units = gate_ref.shape[1]
    piece = part.shape[1]
    per_weight = units // piece
    chunks = half // chunk
    y_peer = (me, 1 - ten)
    core_peer = (across(me, 0), ten)
    x_peer = (across(me, 1), ten)
    z_peer = (across(me, 2), ten)
    loads = [
        pltpu.make_async_copy(source, there, load_sems.at[which])
        for which, (source, there) in enumerate(
            ((gate_hbm, gate_ref), (up_hbm, up_ref), (down_hbm, down_ref))
        )
    ]
    for load in loads:
        load.start()
    greet([y_peer, core_peer, x_peer, z_peer])

    def rows_at(first, count=chunk):
        return pl.ds(pl.multiple_of(first, 16), count)

    def y_copy(kind, c, src, dst):
        return remote(
            src, dst, y_sems.at[0, kind, c], y_sems.at[1, kind, c], y_peer
        )

    def masks_at(first_token, rows):
        return members(grids, items, first_token + rows.start, step)

    def in_steps(c, body):
        def one(index, carry):
            body(pl.ds(pl.multiple_of(c * chunk + index * step, step), step))
            return carry

        lax.fori_loop(0, chunk // step, one, 0)

    proj_copies = []
    for c in range(chunks):
        rows = pl.ds(c * chunk, chunk)
        y_out[rows, :] = dot(
            heads_ref[rows_at((1 - ten) * half + c * chunk), :], proj_ref[...]
        ).astype(BF16)
        proj_copies.append(y_copy(0, c, y_out.at[rows, :], y_in.at[rows, :]))
        proj_copies[c].start()
    for c in range(chunks):
        attn[pl.ds(c * chunk, chunk), :] = dot(
            heads_ref[rows_at(ten * half + c * chunk), :], proj_ref[...]
        )
    for c in range(chunks):

        def scale_grads(rows):
            later = pl.ds(pl.multiple_of(rows.start + half, step), step)
            grad_mlp[rows, :] = (
                mod_values(masks_at(ten * half, rows), mod_ref, 5) * own_grad_ref[rows, :].astype(F32)
            ).astype(BF16)
            grad_mlp[later, :] = (
                mod_values(masks_at((1 - ten) * half, rows), mod_ref, 5)
                * other_grad_ref[rows, :].astype(F32)
            ).astype(BF16)

        in_steps(c, scale_grads)

    for load in loads:
        load.wait()

    def mlp(c):
        rows = pl.ds(c * chunk, chunk)
        for first in range(0, units, 256):
            columns = pl.ds(first, 256)
            gate = dot(mlp_in[rows, :], gate_ref[:, columns])
            up = dot(mlp_in[rows, :], up_ref[:, columns])
            grad = dot_t(grad_mlp[rows, :], down_ref[columns, :])
            sigma = 1.0 / (1.0 + jnp.exp(-gate))
            silu = gate * sigma
            hidden[rows, columns] = (silu * up).astype(BF16)
            grad_gate[rows, columns] = (
                grad * up * (sigma * (1.0 + gate * (1.0 - sigma)))
            ).astype(BF16)
            grad_up[rows, columns] = (grad * silu).astype(BF16)

    mlp_copies = []
    for c in range(chunks):
        proj_copies[c].wait_recv()

        def norm(rows):
            mixed = attn[rows, :] + y_in[rows, :].astype(F32)
            attn[rows, :] = mixed
            masks = masks_at(ten * half, rows)
            resid = tokens_ref[rows, :].astype(F32) + mod_values(masks, mod_ref, 2) * mixed
            resid_ref[rows, :] = resid
            normed, _ = layer_norm(resid)
            mlp_in[rows, :] = (
                normed * (1.0 + mod_values(masks, mod_ref, 4)) + mod_values(masks, mod_ref, 3)
            ).astype(BF16)

        in_steps(c, norm)
        mlp_copies.append(
            y_copy(
                1, c, mlp_in.at[pl.ds(c * chunk, chunk), :], mlp_in.at[pl.ds(half + c * chunk, chunk), :]
            )
        )
        mlp_copies[c].start()
    for c in range(chunks):
        mlp(c)

    def back(first):
        rows = pl.ds(first, chunk)
        return dot_t(grad_gate[rows, :], gate_ref[...]) + dot_t(grad_up[rows, :], up_ref[...])

    back_copies = []
    for c in range(chunks):
        mlp_copies[c].wait_recv()
        mlp(chunks + c)
        rows = pl.ds(c * chunk, chunk)
        proj_copies[c].wait_send()
        y_out[rows, :] = back(half + c * chunk).astype(BF16)
        back_copies.append(y_copy(2, c, y_out.at[rows, :], y_in.at[rows, :]))
        back_copies[c].start()

    orders = [(0, 2, 1, 3) if p % 2 and p < 2 * per_weight else (0, 1, 2, 3) for p in range(6)]

    def packed(position, order):
        def rows_of(p):
            return part[pl.ds(pl.multiple_of(block_at(p, me, order) * depth, 8), depth), :]

        return jnp.concatenate([rows_of(position), rows_of(position + 1)]).astype(BF16)

    core_copies = []
    x_copies = []

    def weight_grad(p):
        which, column = divmod(p, per_weight)
        columns = pl.ds(column * piece, piece)
        left, right = ((grad_mlp, hidden), (mlp_in, grad_gate), (mlp_in, grad_up))[which]
        slot = p % 2
        for first in range(0, width, LANES):
            rows = pl.ds(first, LANES)
            part[rows, :] = t_dot(left[:, rows], right[:, columns])
        if p >= 2:
            core_copies[p - 2].wait_send()
        for position in range(0, dp // 2, 2):
            rows = pl.ds(position * depth, 2 * depth)
            core_out[slot, rows, :] = packed(dp // 2 + position, orders[p])
        core_copies.append(
            remote(
                core_out.at[slot], core_in.at[p], core_sems.at[0, p], core_sems.at[1, p], core_peer
            )
        )
        core_copies[p].start()
        for position in range(0, dp // 2, 2):
            rows = pl.ds(position * depth, 2 * depth)
            core_keep[slot, rows, :] = packed(position, orders[p])

    quarter = width // 4

    def cross(p):
        slot = p % 2
        core_copies[p].wait_recv()

        def total(rows):
            return (core_keep[slot, rows, :].astype(F32) + core_in[p, rows, :].astype(F32)).astype(
                BF16
            )

        if p < 2 * per_weight:
            x_out[p] = total(pl.ds(quarter, quarter))
            x_copies.append(
                remote(
                    x_out.at[p],
                    x_in.at[p],
                    x_sems.at[0, p],
                    x_sems.at[1, p],
                    (across(me, orders[p][1]), ten),
                )
            )
            x_copies[p].start()
            x_keep[p] = total(pl.ds(0, quarter))
        else:
            paired_keep_ref[p - 2 * per_weight] = total(pl.ds(0, quarter))
            paired_out_ref[p - 2 * per_weight] = total(pl.ds(quarter, quarter))

    eighth = width // 8
    z_copies = []

    def ascend(p):
        x_copies[p].wait_recv()
        x_copies[p].wait_send()
        rows = pl.ds(eighth, eighth)
        z_out = x_out.at[p, pl.ds(0, eighth), :]
        x_out[p, :eighth, :] = (
            x_keep[p, rows, :].astype(F32) + x_in[p, rows, :].astype(F32)
        ).astype(BF16)
        next_peer = (across(me, orders[p][2]), ten)
        z_copies.append(remote(z_out, z_in.at[p], z_sems.at[0, p], z_sems.at[1, p], next_peer))
        z_copies[p].start()

    pieces = 3 * per_weight
    weight_grad(0)
    weight_grad(1)
    cross(0)
    for c in range(chunks):
        grad_resid_ref[pl.ds(c * chunk, chunk), :] = back(c * chunk)

    early_ref[...] = jnp.zeros_like(early_ref)
    grad_copies = []
    for c in range(chunks):
        back_copies[c].wait_recv()

        def norm_grad(rows):
            grad = grad_resid_ref[rows, :] + y_in[rows, :].astype(F32)
            normed, inv = layer_norm(resid_ref[rows, :])
            masks = masks_at(ten * half, rows)
            n = grad * (1.0 + mod_values(masks, mod_ref, 4))
            grad_resid = own_grad_ref[rows, :].astype(F32) + norm_back(n, normed, inv)
            grad_resid_ref[rows, :] = grad_resid
            there = pl.ds(pl.multiple_of(rows.start + ten * half, step), step)
            grad_attn_ref[there, :] = (mod_values(masks, mod_ref, 2) * grad_resid).astype(BF16)
            for kind, values in enumerate((grad_resid * attn[rows, :], grad, grad * normed)):
                lanes = slice(kind * width, (kind + 1) * width)
                for item in range(items):
                    early_ref[item : item + 1, lanes] += jnp.sum(
                        masks[item] * values, axis=0, keepdims=True
                    )

        in_steps(c, norm_grad)
        rows = rows_at(ten * half + c * chunk)
        grad_copies.append(y_copy(3, c, grad_attn_ref.at[rows, :], grad_attn_ref.at[rows, :]))
        grad_copies[c].start()
        weight_grad(2 + c)
        cross(1 + c)

    weight_grad(4)
    cross(3)
    ascend(0)
    weight_grad(5)
    cross(4)
    ascend(1)
    for c in range(chunks):
        rows = pl.ds(c * chunk, chunk)
        mlp_other_ref[rows, :] = dot(
            hidden[pl.ds(half + c * chunk, chunk), :], down_ref[...]
        ).astype(BF16)
        mlp_own_ref[rows, :] = dot(hidden[rows, :], down_ref[...])
        own_rows = rows_at(ten * half + c * chunk)
        grad_heads_ref[own_rows, :] = dot_t(grad_attn_ref[own_rows, :], proj_ref[...]).astype(BF16)
    cross(5)
    ascend(2)
    for c in range(chunks):
        rows = rows_at((1 - ten) * half + c * chunk)
        y_copy(3, c, grad_attn_ref.at[rows, :], grad_attn_ref.at[rows, :]).wait_recv()
        grad_heads_ref[rows, :] = dot_t(grad_attn_ref[rows, :], proj_ref[...]).astype(BF16)
    ascend(3)
    for p in range(2 * per_weight):
        z_copies[p].wait_recv()
        total = (
            x_keep[p, :eighth, :].astype(F32)
            + x_in[p, :eighth, :].astype(F32)
            + z_in[p].astype(F32)
        )
        last_keep_ref[p] = total[:depth].astype(BF16)
        last_out_ref[p] = total[depth:].astype(BF16)
    for copy in mlp_copies + back_copies + grad_copies + core_copies[-2:] + z_copies:
        copy.wait_send()


def middle(heads_out, proj, tokens, own_grad, other_grad, grids, mod, gate, up, down):
    half, width = tokens.shape
    length = 2 * half
    units = gate.shape[1]
    inner = heads_out.shape[1]
    items = grids.shape[0]
    dp = lax.axis_size("dp")
    chunk = half // 2
    chunks = half // chunk
    piece = units // 2
    pieces = 6
    vmem = pltpu.VMEM
    dma = pltpu.SemaphoreType.DMA
    anywhere = pl.BlockSpec(memory_space=pl.ANY)
    return pl.pallas_call(
        functools.partial(middle_kernel, items, chunk, STEP),
        out_shape=[
            jax.ShapeDtypeStruct((length, inner), BF16),
            jax.ShapeDtypeStruct((length, width), BF16),
            jax.ShapeDtypeStruct((half, width), F32),
            jax.ShapeDtypeStruct((half, width), F32),
            jax.ShapeDtypeStruct((8, 3 * width), F32),
            jax.ShapeDtypeStruct((half, width), BF16),
            jax.ShapeDtypeStruct((half, width), F32),
            jax.ShapeDtypeStruct((4, width // dp, piece), BF16),
            jax.ShapeDtypeStruct((4, width // dp, piece), BF16),
            jax.ShapeDtypeStruct((2, width // 4, piece), BF16),
            jax.ShapeDtypeStruct((2, width // 4, piece), BF16),
        ],
        in_specs=[pl.BlockSpec(memory_space=pltpu.VMEM)] * 5
        + [pl.BlockSpec(memory_space=pltpu.SMEM), pl.BlockSpec(memory_space=pltpu.VMEM)]
        + [anywhere] * 3,
        out_specs=[pl.BlockSpec(memory_space=pltpu.VMEM)] * 11,
        scratch_shapes=[
            vmem((width, units), BF16),
            vmem((width, units), BF16),
            vmem((units, width), BF16),
            vmem((half, width), F32),
            vmem((length, width), BF16),
            vmem((length, width), BF16),
            vmem((length, units), BF16),
            vmem((length, units), BF16),
            vmem((length, units), BF16),
            vmem((half, width), BF16),
            vmem((half, width), BF16),
            vmem((width, piece), F32),
            vmem((2, width // 2, piece), BF16),
            vmem((2, width // 2, piece), BF16),
            vmem((pieces, width // 2, piece), BF16),
            vmem((4, width // 4, piece), BF16),
            vmem((4, width // 4, piece), BF16),
            vmem((4, width // 4, piece), BF16),
            vmem((4, width // 8, piece), BF16),
            dma((2, 4, chunks)),
            dma((2, pieces)),
            dma((2, 4)),
            dma((2, 4)),
            dma((3,)),
        ],
        compiler_params=pltpu.CompilerParams(
            collective_id=2, has_side_effects=True, vmem_limit_bytes=62 * 2**20
        ),
        cost_estimate=pl.CostEstimate(
            flops=18 * length * width * units, bytes_accessed=30 * 2**20, transcendentals=0
        ),
        name="middle",
    )(heads_out, proj, tokens, own_grad, other_grad, grids, mod, gate, up, down)


def shards_in_kernels(
    tokens,
    conditions,
    item_grids,
    mod_weight,
    query_weight,
    key_weight,
    value_weight,
    proj_weight,
    query_gain,
    key_gain,
    gate_weight,
    up_weight,
    down_weight,
    out_grad,
):
    half, width = tokens.shape
    dp = lax.axis_size("dp")
    items = conditions.shape[0]
    owned = mod_weight.shape[0]
    grids = item_grids
    lane = np.arange(LANES)
    frequency = jnp.asarray(
        (10000.0 ** (-(lane % QUARTER) / QUARTER)).astype(np.float32)[None, :]
    )
    mod, mod_in_own, tokens_all, cosine, sine = head(
        dp, conditions, mod_weight, tokens, grids, frequency
    )
    out_grad_later, mod = lax.optimization_barrier((out_grad, mod))
    out_grad_other = swap(out_grad_later)
    gain_q = query_gain[None, :]
    gain_k = key_gain[None, :]
    weights = (query_weight.T, key_weight.T, value_weight.T)
    attn_in, heads_out, *saved = attend(
        grids, tokens_all, mod, *weights, gain_q, gain_k, cosine, sine
    )
    (
        grad_heads,
        grad_attn_all,
        grad_resid,
        resid,
        early,
        mlp_other,
        mlp_own,
        last_keep,
        last_out,
        paired_keep,
        paired_out,
    ) = middle(
        heads_out,
        proj_weight,
        tokens,
        out_grad,
        out_grad_other,
        grids,
        mod,
        gate_weight,
        up_weight,
        down_weight,
    )
    mlp_recv = swap(mlp_other)
    last_in = lax.ppermute(last_out, "dp", partners(3))
    paired_in = lax.ppermute(paired_out, "dp", partners(1))
    *d, gain_parts = attend_back(grids, grad_heads, saved, gain_q, gain_k, cosine, sine)
    grad_tokens, block_out, sums, grad_mod_all, gain_sums, grad_cond = tail(
        dp,
        d,
        attn_in,
        grad_attn_all,
        heads_out,
        paired_keep,
        paired_in,
        early,
        gain_parts,
        mod,
        conditions,
        grids,
        weights,
        tokens,
        out_grad,
        grad_resid,
        resid,
        mlp_own,
        mlp_recv,
        mod_weight,
    )
    last = last_keep.astype(F32) + last_in.astype(F32)
    grad_mod_weight = t_dot(mod_in_own[:, :owned], grad_mod_all)
    attn_sum = jnp.concatenate(list(sums[2:]), axis=1)
    inner = heads_out.shape[1]
    grad_q, grad_k, grad_v, grad_proj = (
        attn_sum[:, which * inner : (which + 1) * inner] for which in range(4)
    )
    return (
        block_out,
        grad_tokens,
        grad_cond[:items],
        grad_mod_weight,
        grad_q,
        grad_k,
        grad_v,
        grad_proj.T,
        gain_sums[0, :HD],
        gain_sums[1, :HD],
        jnp.concatenate([last[2], last[3]], axis=1),
        jnp.concatenate(list(sums[:2]), axis=1),
        jnp.concatenate([last[0], last[1]], axis=1).T,
    )


def shards(
    tokens,
    conditions,
    item_grids,
    mod_weight,
    query_weight,
    key_weight,
    value_weight,
    proj_weight,
    query_gain,
    key_gain,
    gate_weight,
    up_weight,
    down_weight,
    out_grad,
):
    half, width = tokens.shape
    length = 2 * half
    dp = lax.axis_size("dp")
    bits = dp.bit_length() - 1
    me = lax.axis_index("dp")
    second = lax.axis_index("tensor") == 1
    own_first = lax.axis_index("tensor") * half
    other_first = half - own_first
    items = conditions.shape[0]
    owned = mod_weight.shape[0]

    tokens_other = swap(tokens)
    out_grad_other = swap(out_grad)

    member, row_pos, col_pos = geometry(item_grids, length)
    cosine, sine = rope_tables(row_pos, col_pos)
    gain_q = query_gain[None, :]
    gain_k = key_gain[None, :]
    member_own = lax.dynamic_slice_in_dim(member, own_first, half, 0)
    member_other = lax.dynamic_slice_in_dim(member, other_first, half, 0)

    cond_all = lax.all_gather(conditions, "dp", axis=0, tiled=True)
    mod_in_all = jax.nn.silu(cond_all.astype(F32)).astype(BF16)
    mod_in_own = lax.dynamic_slice_in_dim(mod_in_all, me * owned, owned, 1)
    mod_part = dot(mod_in_own, mod_weight)
    mod_parts = lax.all_to_all(
        mod_part.reshape(dp, items, 6 * width), "dp", split_axis=0, concat_axis=0, tiled=True
    )
    modulation = jnp.sum(mod_parts.astype(F32), axis=0)
    shift_one, scale_one, gate_one, shift_two, scale_two, gate_two = jnp.split(
        modulation, 6, axis=1
    )

    tokens_float = tokens.astype(F32)
    tokens_all = in_order(tokens, tokens_other, second)

    w_qkv = jnp.concatenate([query_weight, key_weight, value_weight], axis=1)
    mod = jnp.pad(modulation, ((0, 8 - items), (0, 0)))
    attn_in, heads_out, *saved = attend(
        item_grids,
        tokens_all,
        mod,
        query_weight.T,
        key_weight.T,
        value_weight.T,
        gain_q,
        gain_k,
        cosine,
        sine,
    )
    inner = heads_out.shape[1]
    grad_out = out_grad.astype(F32)
    gate_two_own = per_token(member_own, gate_two)

    heads_other = lax.dynamic_slice_in_dim(heads_out, other_first, half, 0)
    heads_own = lax.dynamic_slice_in_dim(heads_out, own_first, half, 0)
    attn_recv = swap(dot(heads_other, proj_weight).astype(BF16))
    attn_out = dot(heads_own, proj_weight) + attn_recv.astype(F32)

    gate_one_own = per_token(member_own, gate_one)
    scale_two_own = per_token(member_own, scale_two)
    resid = tokens_float + gate_one_own * attn_out
    norm_two, inv_two = layer_norm(resid)
    mlp_in = (norm_two * (1.0 + scale_two_own) + per_token(member_own, shift_two)).astype(BF16)
    mlp_in_all = jnp.concatenate([mlp_in, swap(mlp_in)])

    grad_mlp_all = jnp.concatenate(
        [
            (gate_two_own * grad_out).astype(BF16),
            (per_token(member_other, gate_two) * out_grad_other.astype(F32)).astype(BF16),
        ]
    )
    grad_hidden = dot_t(grad_mlp_all, down_weight)

    gate_pre = dot(mlp_in_all, gate_weight)
    up_pre = dot(mlp_in_all, up_weight)
    silu_gate = jax.nn.silu(gate_pre)
    hidden = (silu_gate * up_pre).astype(BF16)
    grad_gate_pre = (grad_hidden * up_pre * silu_grad(gate_pre)).astype(BF16)
    grad_up_pre = (grad_hidden * silu_gate).astype(BF16)

    back_other = dot_t(grad_gate_pre[half:], gate_weight) + dot_t(grad_up_pre[half:], up_weight)
    back_recv = swap(back_other.astype(BF16))
    mlp_recv = swap(dot(hidden[half:], down_weight).astype(BF16))
    grad_mlp_in = (
        dot_t(grad_gate_pre[:half], gate_weight)
        + dot_t(grad_up_pre[:half], up_weight)
        + back_recv.astype(F32)
    )

    grad_mlp_rows = halving_rows(grad_mlp_all, bits)
    mlp_in_rows = halving_rows(mlp_in_all, bits)
    down_part = first_halving(grad_mlp_rows, hidden)
    gate_part = first_halving(mlp_in_rows, grad_gate_pre)
    up_part = first_halving(mlp_in_rows, grad_up_pre)

    mlp_out = dot(hidden[:half], down_weight) + mlp_recv.astype(F32)
    block_out = (resid + gate_two_own * mlp_out).astype(BF16)

    grad_resid = grad_out + norm_back(grad_mlp_in * (1.0 + scale_two_own), norm_two, inv_two)
    grad_attn = (gate_one_own * grad_resid).astype(BF16)
    grad_attn_all = in_order(grad_attn, swap(grad_attn), second)
    grad_heads = dot_t(grad_attn_all, proj_weight).astype(BF16)
    grad_heads, down_part, gate_part, up_part = lax.optimization_barrier(
        (grad_heads, down_part, gate_part, up_part)
    )
    grad_down = rest_of_halving(down_part, bits).T
    grad_gate = rest_of_halving(gate_part, bits)
    grad_up = rest_of_halving(up_part, bits)
    *d, gain_parts = attend_back(item_grids, grad_heads, saved, gain_q, gain_k, cosine, sine)

    d = jnp.concatenate(d, axis=1)
    early = jnp.concatenate(
        [
            per_item(member_own, grad_resid * attn_out),
            per_item(member_own, grad_mlp_in),
            per_item(member_own, grad_mlp_in * norm_two),
            per_item(member_own, grad_out * mlp_out),
        ],
        axis=1,
    )
    def attn_back(first):
        return dot_t(lax.dynamic_slice_in_dim(d, first, half, 0), w_qkv)

    attn_back_recv = swap(attn_back(other_first).astype(BF16))
    grad_attn_in = attn_back(own_first) + attn_back_recv.astype(F32)
    attn_sum = rest_of_halving(
        jnp.concatenate(
            [
                first_halving(halving_rows(attn_in, bits), d),
                first_halving(halving_rows(grad_attn_all, bits), heads_out),
            ],
            axis=1,
        ),
        bits,
    )
    norm_one, inv_one = layer_norm(tokens_float)
    scale_one_own = per_token(member_own, scale_one)
    grad_tokens = (
        grad_resid + norm_back(grad_attn_in * (1.0 + scale_one_own), norm_one, inv_one)
    ).astype(BF16)
    part_mod = jnp.concatenate(
        [per_item(member_own, grad_attn_in), per_item(member_own, grad_attn_in * norm_one), early],
        axis=1,
    )
    gains = jnp.pad(gain_parts[:2].reshape(1, 2 * LANES), ((0, 0), (0, 6 * width - 2 * LANES)))
    part_small = jnp.concatenate([part_mod, gains]).astype(BF16)
    small = part_small.astype(F32) + swap(part_small).astype(F32)
    small_all = lax.all_gather(small.astype(BF16), "dp", axis=0, tiled=False)
    grad_mod_all = small_all[:, :items].reshape(dp * items, 6 * width)
    gain_sums = jnp.sum(small_all[:, items, : 2 * LANES].astype(F32), axis=0).reshape(2, LANES)
    cond_parts = lax.all_to_all(
        dot_t(grad_mod_all, mod_weight).reshape(dp, items, owned),
        "dp",
        split_axis=0,
        concat_axis=0,
        tiled=True,
    )

    grad_mod_weight = t_dot(mod_in_own, grad_mod_all)
    grad_mod_in = cond_parts.transpose(1, 0, 2).reshape(items, dp * owned)
    grad_conditions = silu_grad(conditions.astype(F32)) * grad_mod_in
    grad_q, grad_k, grad_v, grad_proj = (
        attn_sum[:, which * inner : (which + 1) * inner] for which in range(4)
    )
    return (
        block_out,
        grad_tokens,
        grad_conditions,
        grad_mod_weight,
        grad_q,
        grad_k,
        grad_v,
        grad_proj.T,
        gain_sums[0, :HD],
        gain_sums[1, :HD],
        grad_gate,
        grad_up,
        grad_down,
    )


def solution(mesh):
    tokens = P(("dp", "tensor"), None)
    rows = P("dp", None)
    columns = P(None, "tensor")
    inner = P("tensor", None)
    both = P("dp", "tensor")
    turned = P("tensor", "dp")
    in_kernels = mesh.shape["dp"] == 16
    return jax.shard_map(
        shards_in_kernels if in_kernels else shards,
        mesh=mesh,
        in_specs=(
            tokens,
            rows,
            rows,
            rows,
            columns,
            columns,
            columns,
            inner,
            P(),
            P(),
            columns,
            columns,
            inner,
            tokens,
        ),
        out_specs=(
            tokens,
            tokens,
            rows,
            rows,
            both,
            both,
            both,
            turned,
            P(),
            P(),
            both,
            both,
            turned,
        ),
        check_vma=False,
    )
```

```python
import functools

import jax
import jax.numpy as jnp
import numpy as np
from jax import lax
from jax.experimental import pallas as pl
from jax.experimental.pallas import tpu as pltpu
from jax.sharding import PartitionSpec as P

HD = 72
QUARTER = HD // 4
LANES = 128
SPAN = 256
TILE = 256
UNROLL = 8
STEP = 16
EPSILON = 1e-06
F32 = jnp.float32
BF16 = jnp.bfloat16
HIGH = lax.Precision.HIGHEST


def silu_grad(values):
    sigma = jax.nn.sigmoid(values)
    return sigma * (1.0 + values * (1.0 - sigma))


def dot(left, right):
    return jnp.dot(left, right, preferred_element_type=F32)


def dot_t(left, right):
    return lax.dot_general(left, right, (((1,), (1,)), ((), ())), preferred_element_type=F32)


def t_dot(left, right):
    return lax.dot_general(left, right, (((0,), (0,)), ((), ())), preferred_element_type=F32)


def geometry(row_grids, length):
    heights = row_grids[:, 0]
    widths = row_grids[:, 1]
    count = row_grids.shape[0]
    sizes = heights * widths
    ends = [sizes[0]]
    for item in range(1, count):
        ends.append(ends[-1] + sizes[item])
    starts = [ends[item] - sizes[item] for item in range(count)]
    positions = jnp.arange(length, dtype=jnp.int32)
    member = jnp.stack(
        [(positions >= starts[item]) & (positions < ends[item]) for item in range(count)], axis=1
    )
    origin = sum(jnp.where(member[:, item], starts[item], 0) for item in range(count))
    width = jnp.maximum(
        sum(jnp.where(member[:, item], widths[item], 0) for item in range(count)), 1
    )
    local = positions - origin
    return member.astype(F32), local // width, local % width


def rope_tables(row_pos, col_pos):
    lane = jnp.arange(LANES)
    frequency = 10000.0 ** (-(lane % QUARTER).astype(F32) / QUARTER)
    along = jnp.where(lane[None, :] < 2 * QUARTER, row_pos[:, None], col_pos[:, None])
    angles = along.astype(F32) * frequency[None, :]
    valid = lane[None, :] < HD
    return jnp.where(valid, jnp.cos(angles), 0.0), jnp.where(valid, jnp.sin(angles), 0.0)


def turn(values):
    lane = lax.broadcasted_iota(jnp.int32, values.shape, 1)
    return jnp.where(
        lane % (2 * QUARTER) < QUARTER,
        -pltpu.roll(values, LANES - QUARTER, 1),
        pltpu.roll(values, QUARTER, 1),
    )


def only_head(values):
    lane = lax.broadcasted_iota(jnp.int32, values.shape, 1)
    return jnp.where(lane < HD, values, jnp.zeros_like(values))


def split_heads(wide, store, heads):
    rows = wide.shape[0]
    wide = jnp.concatenate([wide, jnp.zeros((rows, LANES), wide.dtype)], axis=1)
    for head in range(heads):
        store(head, only_head(wide[:, head * HD : head * HD + LANES]))


def item_spans(grids, items):
    spans = []
    start = 0
    for item in range(items):
        size = grids[item, 0] * grids[item, 1]
        spans.append((start, size))
        start = start + size
    return spans


def item_of(grids, items, first):
    which = 0
    for start, size in item_spans(grids, items):
        which = which + jnp.where(first >= start + size, 1, 0)
    return which


def mod_values(item, mod_ref, kind):
    width = mod_ref.shape[1] // 6
    return mod_ref[pl.ds(item, 1), kind * width : (kind + 1) * width]


def add_rows(sums_ref, item, items, values, lanes=slice(None)):
    row = jnp.sum(values, axis=0, keepdims=True)
    for which in range(items):
        sums_ref[which : which + 1, lanes] += jnp.where(item == which, row, 0.0)


def padded_gain(gain_ref):
    return jnp.concatenate([gain_ref[...], jnp.zeros((1, LANES - HD), F32)], axis=1)


def attend_kernel(
    heads,
    items,
    grids,
    tokens_ref,
    mod_ref,
    wq_ref,
    wk_ref,
    wv_ref,
    gq_ref,
    gk_ref,
    cos_ref,
    sin_ref,
    x_ref,
    out_ref,
    qpre_ref,
    kpre_ref,
    q_ref,
    k_ref,
    v_ref,
    probs_ref,
    qraw,
    kraw,
    vraw,
    oraw,
    wide,
):
    length = x_ref.shape[0]
    head = pl.program_id(0)

    @pl.when(head == 0)
    def _():
        def norm(index, carry):
            first = pl.multiple_of(index * STEP, STEP)
            rows = pl.ds(first, STEP)
            item = item_of(grids, items, first)
            normed, _ = layer_norm(tokens_ref[rows, :].astype(F32))
            x_ref[rows, :] = (
                normed * (1.0 + mod_values(item, mod_ref, 1)) + mod_values(item, mod_ref, 0)
            ).astype(BF16)
            return carry

        lax.fori_loop(0, length // STEP, norm, 0, unroll=UNROLL)
        for first in range(0, length, TILE):
            rows = pl.ds(first, TILE)
            x = x_ref[rows, :]
            for w_ref, raw in ((wq_ref, qraw), (wk_ref, kraw), (wv_ref, vraw)):

                def store(h, part, raw=raw):
                    raw[h, rows, :] = part.astype(raw.dtype)

                split_heads(dot_t(x, w_ref[...]), store, heads)

    for raw, pre_ref, low_ref, gain_ref in (
        (qraw, qpre_ref, q_ref, gq_ref),
        (kraw, kpre_ref, k_ref, gk_ref),
    ):
        for first in range(0, length, TILE):
            rows = pl.ds(first, TILE)
            pre = raw[head, rows, :]
            pre_ref[0, rows, :] = pre
            inv = lax.rsqrt(jnp.sum(pre * pre, axis=1, keepdims=True) / HD + EPSILON)
            normed = pre * inv * padded_gain(gain_ref)
            low_ref[0, rows, :] = (
                normed * cos_ref[rows, :] + turn(normed) * sin_ref[rows, :]
            ).astype(BF16)
    v_ref[0] = vraw[head]
    oraw[head] = vraw[head].astype(F32)
    row = lax.broadcasted_iota(jnp.int32, (SPAN, SPAN), 0)
    col = lax.broadcasted_iota(jnp.int32, (SPAN, SPAN), 1)
    row_out = lax.broadcasted_iota(jnp.int32, (SPAN, LANES), 0)
    for item, (start, size) in enumerate(item_spans(grids, items)):
        rows = pl.ds(pl.multiple_of(start, 16), SPAN)
        scores = dot_t(q_ref[0, rows, :], k_ref[0, rows, :]) * HD**-0.5
        scores = jnp.where(col < size, scores, -1e30)
        top = jnp.max(scores, axis=1, keepdims=True)
        weights = jnp.exp(scores - top)
        total = jnp.sum(weights, axis=1, keepdims=True)
        probs = jnp.where(row < size, weights / total, 0.0).astype(BF16)
        probs_ref[0, item] = probs
        mixed = dot(probs, v_ref[0, rows, :])
        oraw[head, rows, :] = jnp.where(row_out < size, mixed, oraw[head, rows, :])

    @pl.when(head == heads - 1)
    def _():
        for h in range(heads):
            wide[:, h * HD : h * HD + HD] = oraw[h][:, :HD]
        out_ref[...] = wide[...].astype(BF16)


def attend_back_kernel(
    heads,
    items,
    grids,
    grad_ref,
    qpre_ref,
    kpre_ref,
    q_ref,
    k_ref,
    v_ref,
    probs_ref,
    gq_ref,
    gk_ref,
    cos_ref,
    sin_ref,
    dq_ref,
    dk_ref,
    dv_ref,
    gain_ref,
    graw,
    dqraw,
    dkraw,
    dvraw,
    wide,
):
    length = grad_ref.shape[0]
    head = pl.program_id(0)

    @pl.when(head == 0)
    def _():
        gain_ref[...] = jnp.zeros_like(gain_ref)
        for first in range(0, length, TILE):
            rows = pl.ds(first, TILE)

            def store(h, part):
                graw[h, rows, :] = part.astype(BF16)

            split_heads(grad_ref[rows, :].astype(F32), store, heads)

    dqraw[head] = jnp.zeros((length, LANES), F32)
    dkraw[head] = jnp.zeros((length, LANES), F32)
    row_all = lax.broadcasted_iota(jnp.int32, (length, LANES), 0)
    used = sum(item_spans(grids, items)[-1])
    dvraw[head] = jnp.where(row_all >= used, graw[head].astype(F32), 0.0)
    for item, (start, _) in enumerate(item_spans(grids, items)):
        rows = pl.ds(pl.multiple_of(start, 16), SPAN)
        probs_low = probs_ref[0, item]
        probs = probs_low.astype(F32)
        grad = graw[head, rows, :]
        grad_probs = dot_t(grad, v_ref[0, rows, :])
        inner = jnp.sum(probs * grad_probs, axis=1, keepdims=True) / jnp.maximum(
            jnp.sum(probs, axis=1, keepdims=True), 0.5
        )
        grad_scores = (probs * (grad_probs - inner)).astype(BF16)
        dqraw[head, rows, :] += dot(grad_scores, k_ref[0, rows, :])
        dkraw[head, rows, :] += t_dot(grad_scores, q_ref[0, rows, :])
        dvraw[head, rows, :] += t_dot(probs_low, grad)

    for raw, pre_ref, g_ref, which in (
        (dqraw, qpre_ref, gq_ref, 0),
        (dkraw, kpre_ref, gk_ref, 1),
    ):
        for first in range(0, length, TILE):
            rows = pl.ds(first, TILE)
            turned = raw[head, rows, :] * HD**-0.5
            normed = turned * cos_ref[rows, :] - turn(turned * sin_ref[rows, :])
            pre = pre_ref[0, rows, :]
            inv = lax.rsqrt(jnp.sum(pre * pre, axis=1, keepdims=True) / HD + EPSILON)
            unit = pre * inv
            gain_ref[which : which + 1, :] += jnp.sum(normed * unit, axis=0, keepdims=True)
            scaled = normed * padded_gain(g_ref)
            along = jnp.sum(scaled * unit, axis=1, keepdims=True) / HD
            raw[head, rows, :] = inv * (scaled - unit * along)

    @pl.when(head == heads - 1)
    def _():
        for raw, o_ref in ((dqraw, dq_ref), (dkraw, dk_ref), (dvraw, dv_ref)):
            for h in range(heads):
                wide[:, h * HD : h * HD + HD] = raw[h][:, :HD]
            o_ref[...] = wide[...].astype(BF16)


def whole(shape):
    return pl.BlockSpec(shape, lambda h, grids: (0,) * len(shape))


def per_head(shape):
    return pl.BlockSpec((1,) + shape, lambda h, grids: (h,) + (0,) * len(shape))


def attend(grids, tokens, mod, wq, wk, wv, gain_q, gain_k, cosine, sine):
    length, width = tokens.shape
    heads = wq.shape[0] // HD
    items = grids.shape[0]
    head_f32 = jax.ShapeDtypeStruct((heads, length, LANES), F32)
    head_low = jax.ShapeDtypeStruct((heads, length, LANES), BF16)
    return pl.pallas_call(
        functools.partial(attend_kernel, heads, items),
        grid_spec=pltpu.PrefetchScalarGridSpec(
            num_scalar_prefetch=1,
            grid=(heads,),
            in_specs=[
                whole(tokens.shape),
                whole(mod.shape),
                whole(wq.shape),
                whole(wk.shape),
                whole(wv.shape),
                whole((1, HD)),
                whole((1, HD)),
                whole((length, LANES)),
                whole((length, LANES)),
            ],
            out_specs=[
                whole((length, width)),
                whole((length, heads * HD)),
                per_head((length, LANES)),
                per_head((length, LANES)),
                per_head((length, LANES)),
                per_head((length, LANES)),
                per_head((length, LANES)),
                per_head((items, SPAN, SPAN)),
            ],
            scratch_shapes=[
                pltpu.VMEM((heads, length, LANES), F32),
                pltpu.VMEM((heads, length, LANES), F32),
                pltpu.VMEM((heads, length, LANES), BF16),
                pltpu.VMEM((heads, length, LANES), F32),
                pltpu.VMEM((length, heads * HD), F32),
            ],
        ),
        out_shape=[
            jax.ShapeDtypeStruct((length, width), BF16),
            jax.ShapeDtypeStruct((length, heads * HD), BF16),
            head_f32,
            head_f32,
            head_low,
            head_low,
            head_low,
            jax.ShapeDtypeStruct((heads, items, SPAN, SPAN), BF16),
        ],
        compiler_params=pltpu.CompilerParams(vmem_limit_bytes=62 * 2**20),
        cost_estimate=pl.CostEstimate(
            flops=2 * length * width * heads * HD * 3 + 4 * heads * items * SPAN * SPAN * LANES,
            bytes_accessed=24 * 2**20,
            transcendentals=heads * items * SPAN * SPAN,
        ),
        name="attend",
    )(grids, tokens, mod, wq, wk, wv, gain_q, gain_k, cosine, sine)


def attend_back(grids, grad, saved, gain_q, gain_k, cosine, sine):
    length, width = grad.shape
    heads = width // HD
    items = grids.shape[0]
    out = jax.ShapeDtypeStruct((length, width), BF16)
    return pl.pallas_call(
        functools.partial(attend_back_kernel, heads, items),
        grid_spec=pltpu.PrefetchScalarGridSpec(
            num_scalar_prefetch=1,
            grid=(heads,),
            in_specs=[
                whole(grad.shape),
                per_head((length, LANES)),
                per_head((length, LANES)),
                per_head((length, LANES)),
                per_head((length, LANES)),
                per_head((length, LANES)),
                per_head((items, SPAN, SPAN)),
                whole((1, HD)),
                whole((1, HD)),
                whole((length, LANES)),
                whole((length, LANES)),
            ],
            out_specs=[
                whole((length, width)),
                whole((length, width)),
                whole((length, width)),
                whole((8, LANES)),
            ],
            scratch_shapes=[
                pltpu.VMEM((heads, length, LANES), BF16),
                pltpu.VMEM((heads, length, LANES), F32),
                pltpu.VMEM((heads, length, LANES), F32),
                pltpu.VMEM((heads, length, LANES), F32),
                pltpu.VMEM((length, width), F32),
            ],
        ),
        out_shape=[out, out, out, jax.ShapeDtypeStruct((8, LANES), F32)],
        compiler_params=pltpu.CompilerParams(vmem_limit_bytes=62 * 2**20),
        cost_estimate=pl.CostEstimate(
            flops=8 * heads * items * SPAN * SPAN * LANES,
            bytes_accessed=24 * 2**20,
            transcendentals=0,
        ),
        name="attend_back",
    )(grids, grad, *saved, gain_q, gain_k, cosine, sine)


def layer_norm(values):
    centred = values - jnp.mean(values, axis=1, keepdims=True)
    inv_std = lax.rsqrt(jnp.mean(centred * centred, axis=1, keepdims=True) + EPSILON)
    return (centred * inv_std, inv_std)


def norm_back(grad_norm, normed, inv_std):
    return inv_std * (
        grad_norm
        - jnp.mean(grad_norm, axis=1, keepdims=True)
        - normed * jnp.mean(grad_norm * normed, axis=1, keepdims=True)
    )


def per_token(member, rows):
    return sum(member[:, item, None] * rows[item][None, :] for item in range(rows.shape[0]))


def per_item(member, values):
    return jnp.stack(
        [jnp.sum(member[:, item, None] * values, axis=0) for item in range(member.shape[1])]
    )


def swap(values):
    return lax.ppermute(values, "tensor", [(0, 1), (1, 0)])


def in_order(own, other, second):
    return jnp.concatenate([jnp.where(second, other, own), jnp.where(second, own, other)])


def halving_rows(values, bits):
    dp = 2**bits
    depth = values.shape[1] // dp
    blocks = values.T.reshape((2,) * bits + (depth, values.shape[0]))
    me = lax.axis_index("dp")
    for bit in range(bits):
        axis = bits - 1 - bit
        blocks = jnp.where((me >> bit) & 1 == 1, jnp.flip(blocks, axis), blocks)
    blocks = blocks.transpose(tuple(range(bits - 1, -1, -1)) + (bits, bits + 1))
    return blocks.reshape(dp * depth, values.shape[0])


def first_halving(rows, grads):
    half = rows.shape[0] // 2
    sent = lax.ppermute(dot(rows[half:], grads).astype(BF16), "dp", partners(0))
    return (dot(rows[:half], grads) + sent.astype(F32)).astype(BF16)


def partners(bit):
    return [(i, i ^ (1 << bit)) for i in range(lax.axis_size("dp"))]


def rest_of_halving(part, bits):
    for bit in range(1, bits):
        half = part.shape[0] // 2
        sent = lax.ppermute(part[half:], "dp", partners(bit))
        part = part[:half].astype(F32) + sent.astype(F32)
        if bit < bits - 1:
            part = part.astype(BF16)
    return part.astype(F32)


def remote(src, dst, send, recv, device):
    return pltpu.make_async_remote_copy(
        src_ref=src,
        dst_ref=dst,
        send_sem=send,
        recv_sem=recv,
        device_id=device,
        device_id_type=pl.DeviceIdType.MESH,
    )


def block_at(position, me, order):
    block = 0
    for level, bit in enumerate(order):
        mine = (me // (1 << bit)) % 2
        there = (position >> (len(order) - 1 - level)) & 1
        block = block + (1 << bit) * (1 - mine if there else mine)
    return block


def across(me, bit):
    return me + (1 << bit) - 2 * (1 << bit) * ((me // (1 << bit)) % 2)


def group_rows(count):
    return -(-count // 16) * 16


def pack_rows(rows_ref, items, sources):
    span = rows_ref.shape[0] // items
    rows_ref[...] = jnp.zeros_like(rows_ref)
    for item in range(items):
        row = item * span
        for source, part in sources:
            width = rows_ref.shape[1]
            groups = source.shape[1] // width if part is None else source.shape[1] // width // 3
            for group in range(groups):
                lane = ((part or 0) * groups + group) * width
                rows_ref[row : row + 1, :] = source[item : item + 1, lane : lane + width]
                row += 1


def greet(peers):
    barrier = pltpu.get_barrier_semaphore()
    for peer in peers:
        pl.semaphore_signal(
            barrier, inc=1, device_id=peer, device_id_type=pl.DeviceIdType.MESH
        )
    pl.semaphore_wait(barrier, len(peers))


def tail_kernel(
    dp,
    items,
    dq_ref,
    dk_ref,
    dv_ref,
    attn_in_ref,
    grad_attn_ref,
    heads_ref,
    paired_keep_ref,
    paired_in_ref,
    early_ref,
    gain_ref,
    mod_ref,
    cond_ref,
    grids,
    wq_hbm,
    wk_hbm,
    wv_hbm,
    tokens_hbm,
    own_grad_hbm,
    grad_resid_hbm,
    resid_hbm,
    mlp_own_hbm,
    mlp_in_hbm,
    mod_weight_hbm,
    grad_tokens_ref,
    block_out_ref,
    sums_ref,
    all_ref,
    gains_ref,
    grad_cond_ref,
    wq_ref,
    wk_ref,
    wv_ref,
    tokens_ref,
    own_grad_ref,
    grad_resid_ref,
    resid_ref,
    mlp_own_ref,
    mlp_in_ref,
    mod_weight_ref,
    part,
    y_out,
    y_in,
    back,
    core_out,
    core_in,
    core_keep,
    x_out,
    x_in,
    x_keep,
    z_out,
    z_in,
    z_keep,
    w_out,
    w_in,
    gate_sums,
    early_all,
    late_rows,
    late_out,
    late_in,
    late_all,
    flat,
    cond_out,
    cond_in,
    load_sems,
    y_sems,
    halving_sems,
    early_sems,
    late_sems,
    cond_send,
    cond_recv,
):
    bits = dp.bit_length() - 1
    me = lax.axis_index("dp")
    ten = lax.axis_index("tensor")
    half, width = grad_tokens_ref.shape
    depth = width // dp
    inner = dq_ref.shape[1]
    pieces, _, piece = core_out.shape
    paired = paired_keep_ref.shape[0]
    groups = width // LANES
    early_span = early_ref.shape[0] // items
    late_span = late_out.shape[0] // items
    y_peer = (me, 1 - ten)
    dp_peers = [((me + step) % dp, ten) for step in range(1, dp)]
    loads = [
        pltpu.make_async_copy(source, there, load_sems.at[which])
        for which, (source, there) in enumerate(
            (
                (wq_hbm, wq_ref),
                (wk_hbm, wk_ref),
                (wv_hbm, wv_ref),
                (own_grad_hbm, own_grad_ref),
                (resid_hbm, resid_ref),
                (mlp_own_hbm, mlp_own_ref),
                (mlp_in_hbm, mlp_in_ref),
                (tokens_hbm, tokens_ref),
                (grad_resid_hbm, grad_resid_ref),
                (mod_weight_hbm, mod_weight_ref),
            )
        )
    ]
    for load in loads:
        load.start()
    greet([y_peer] + dp_peers)

    def y_copy(which, src, dst):
        return remote(src, dst, y_sems.at[0, which], y_sems.at[1, which], y_peer)

    order = (0, 1, 2, 3)
    gather_order = (1, 2, 3, 0)

    def halving(level, which, src, dst):
        return remote(
            src,
            dst,
            halving_sems.at[0, level, which],
            halving_sems.at[1, level, which],
            (across(me, order[level]), ten),
        )

    def doubling(level, slots, sems):
        count = 1 << level
        return remote(
            slots.at[pl.ds(0, count)],
            slots.at[pl.ds(count, count)],
            sems.at[0, level],
            sems.at[1, level],
            (across(me, gather_order[level]), ten),
        )

    def in_steps(body):
        def one(index, carry):
            body(pl.multiple_of(index * STEP, STEP))
            return carry

        lax.fori_loop(0, half // STEP, one, 0, unroll=UNROLL)

    last_copies = {}

    def last_level(p, total):
        w_out[p, depth:, :] = jnp.zeros((w_out.shape[1] - depth, piece), BF16)
        w_out[p, :depth, :] = total[depth:].astype(BF16)
        last_copies[p] = halving(3, p, w_out.at[p], w_in.at[p])
        last_copies[p].start()
        sums_ref[p] = total[:depth]

    def paired_sum(p, rows):
        return paired_keep_ref[p, rows, :].astype(F32) + paired_in_ref[p, rows, :].astype(F32)

    early_all[0] = early_ref[...]
    early_copies = [doubling(level, early_all, early_sems) for level in range(bits)]
    early_copies[0].start()

    for load in loads[:3]:
        load.wait()

    def attn_back(first):
        rows = pl.ds(pl.multiple_of(first, half), half)
        return (
            dot(dq_ref[rows, :], wq_ref[...])
            + dot(dk_ref[rows, :], wk_ref[...])
            + dot(dv_ref[rows, :], wv_ref[...])
        )

    y_out[...] = attn_back((1 - ten) * half).astype(BF16)
    back_copy = y_copy(1, y_out, y_in)
    back_copy.start()
    early_copies[0].wait_recv()
    early_copies[1].start()
    z_copies = []
    for p in range(paired):
        z_out[p] = paired_sum(p, pl.ds(2 * depth, 2 * depth)).astype(BF16)
        z_copies.append(halving(2, p, z_out.at[p], z_in.at[p]))
        z_copies[p].start()

    def weight_grad(which, left, right):
        columns = slice(which * inner, (which + 1) * inner)
        for first in range(0, width, LANES):
            rows = pl.ds(first, LANES)
            part[rows, columns] = t_dot(left[:, rows], right[...])

    core_copies = []

    def send_core(p):
        columns = pl.ds(p * piece, piece)

        def packed(position):
            def rows_of(at):
                block = block_at(at, me, order)
                return part[pl.ds(pl.multiple_of(block * depth, 8), depth), columns]

            return jnp.concatenate([rows_of(position), rows_of(position + 1)]).astype(BF16)

        for position in range(0, dp // 2, 2):
            core_out[p, pl.ds(position * depth, 2 * depth), :] = packed(dp // 2 + position)
        core_copies.append(halving(0, paired + p, core_out.at[p], core_in.at[p]))
        core_copies[p].start()
        for position in range(0, dp // 2, 2):
            core_keep[p, pl.ds(position * depth, 2 * depth), :] = packed(position)

    x_copies = []

    def cross(p):
        core_copies[p].wait_recv()
        for rows, there in (
            (pl.ds(4 * depth, 4 * depth), x_out),
            (pl.ds(0, 4 * depth), x_keep),
        ):
            there[p] = (core_keep[p, rows, :].astype(F32) + core_in[p, rows, :].astype(F32)).astype(
                BF16
            )
        x_copies.append(halving(1, paired + p, x_out.at[p], x_in.at[p]))
        x_copies[p].start()

    descents = {}

    def descend(p):
        there = paired + p
        x_copies[p].wait_recv()
        for rows, target in (
            (pl.ds(2 * depth, 2 * depth), z_out),
            (pl.ds(0, 2 * depth), z_keep),
        ):
            total = x_keep[p, rows, :].astype(F32) + x_in[p, rows, :].astype(F32)
            target[there if target is z_out else p] = total.astype(BF16)
        descents[p] = halving(2, there, z_out.at[there], z_in.at[there])
        descents[p].start()

    def finish_halving(p):
        descents[p].wait_recv()
        last_level(paired + p, z_keep[p].astype(F32) + z_in[paired + p].astype(F32))

    weight_grad(0, attn_in_ref, dq_ref)
    weight_grad(1, attn_in_ref, dk_ref)
    send_core(0)
    early_copies[1].wait_recv()
    early_copies[2].start()
    cross(0)
    weight_grad(2, attn_in_ref, dv_ref)
    send_core(1)
    for p in range(paired):
        z_copies[p].wait_recv()
        last_level(p, paired_sum(p, pl.ds(0, 2 * depth)) + z_in[p].astype(F32))
    cross(1)
    weight_grad(3, grad_attn_ref, heads_ref)
    send_core(2)

    for load in loads[3:7]:
        load.wait()
    gate_sums[...] = jnp.zeros_like(gate_sums)

    def finish_block(first):
        rows = pl.ds(first, STEP)
        item = item_of(grids, items, ten * half + first)
        mlp_out = mlp_own_ref[rows, :] + mlp_in_ref[rows, :].astype(F32)
        block_out_ref[rows, :] = (
            resid_ref[rows, :] + mod_values(item, mod_ref, 5) * mlp_out
        ).astype(BF16)
        add_rows(gate_sums, item, items, own_grad_ref[rows, :].astype(F32) * mlp_out)

    in_steps(finish_block)

    back[...] = attn_back(ten * half)
    descend(0)

    count = dp * items

    def unpack(all_here, span, places):
        rows = items * span
        for slot in range(dp):
            source = block_at(slot, me, gather_order[::-1])
            there = pl.multiple_of(source * rows, 16)
            flat[pl.ds(there, rows), :] = all_here[slot].astype(F32)
        for group, place in enumerate(places):
            lanes = pl.ds(place * LANES, LANES)
            all_ref[:, lanes] = flat[pl.ds(group, count, stride=span), :].astype(BF16)

    for load in loads[7:]:
        load.wait()
    back_copy.wait_recv()
    grad_cond_ref[...] = jnp.zeros_like(grad_cond_ref)
    gains_ref[...] = jnp.zeros_like(gains_ref)

    def norm_grad(first):
        rows = pl.ds(first, STEP)
        item = item_of(grids, items, ten * half + first)
        normed, inv = layer_norm(tokens_ref[rows, :].astype(F32))
        grad = back[rows, :] + y_in[rows, :].astype(F32)
        n = grad * (1.0 + mod_values(item, mod_ref, 1))
        grad_tokens_ref[rows, :] = (grad_resid_ref[rows, :] + norm_back(n, normed, inv)).astype(BF16)
        add_rows(grad_cond_ref, item, items, grad)
        add_rows(gains_ref, item, items, grad * normed)

    in_steps(norm_grad)
    pack_rows(late_rows, items, [(grad_cond_ref, None), (gains_ref, None), (gate_sums, None)])
    late_rows[3 * groups : 3 * groups + 2, :] = gain_ref[:2, :]
    late_out[...] = late_rows[...].astype(BF16)
    late_copy = y_copy(2, late_out, late_in)
    late_copy.start()
    early_copies[2].wait_recv()
    early_copies[3].start()
    late_copy.wait_recv()
    late_all[0] = (late_out[...].astype(F32) + late_in[...].astype(F32)).astype(BF16)
    late_copies = [doubling(level, late_all, late_sems) for level in range(bits)]
    late_copies[0].start()
    cross(2)
    early_copies[3].wait_recv()
    unpack(early_all, early_span, range(2 * groups, 5 * groups))
    late_copies[0].wait_recv()
    late_copies[1].start()
    descend(1)
    late_copies[1].wait_recv()
    late_copies[2].start()
    finish_halving(0)
    late_copies[2].wait_recv()
    late_copies[3].start()
    descend(2)
    late_copies[3].wait_recv()
    unpack(late_all, late_span, [*range(2 * groups), *range(5 * groups, 6 * groups)])
    gains = jnp.zeros((2, LANES), F32)
    for source in range(dp):
        row = source * items * late_span + 3 * groups
        gains += flat[row : row + 2, :]
    gains_ref[:2, :LANES] = gains
    flat[:count, :depth] = dot_t(all_ref[...], mod_weight_ref[...])
    cond_out[...] = jnp.zeros_like(cond_out)
    for dest in range(dp):
        cond_out[dest, :items, :depth] = flat[pl.ds(dest * items, items), :depth]
    cond_in[me] = cond_out[me]
    cond_copies = []
    for step, peer in enumerate(dp_peers):
        cond_copies.append(
            remote(cond_out.at[peer[0]], cond_in.at[me], cond_send.at[step], cond_recv.at[me], peer)
        )
        cond_copies[-1].start()
    finish_halving(1)
    finish_halving(2)
    for step in range(1, dp):
        source = (me + dp - step) % dp
        remote(
            cond_out.at[0], cond_in.at[source], cond_send.at[0], cond_recv.at[source], y_peer
        ).wait_recv()
    for source in range(dp):
        grad_cond_ref[:, source * depth : (source + 1) * depth] = cond_in[source, :, :depth]
    values = cond_ref[...].astype(F32)
    grad_cond_ref[:items, :] = grad_cond_ref[:items, :] * silu_grad(values)
    for p in last_copies:
        last_copies[p].wait_recv()
        sums_ref[p] += w_in[p, :depth, :].astype(F32)
    for copy in (
        [back_copy, late_copy]
        + early_copies
        + late_copies
        + cond_copies
        + core_copies
        + x_copies
        + z_copies
        + list(descents.values())
        + list(last_copies.values())
    ):
        copy.wait_send()


def tail(
    dp,
    d,
    attn_in,
    grad_attn,
    heads_out,
    paired_keep,
    paired_in,
    early,
    gains,
    mod,
    conditions,
    grids,
    weights,
    tokens,
    own_grad,
    grad_resid,
    resid,
    mlp_own,
    mlp_in,
    mod_weight,
):
    half, width = tokens.shape
    items = grids.shape[0]
    length = 2 * half
    inner = d[0].shape[1]
    depth = width // dp
    pieces = 3
    piece = 4 * inner // pieces
    groups = width // LANES
    early_rows = early.shape[0]
    late_rows = items * group_rows(3 * groups + 2)
    count = dp * items
    paired = paired_keep.shape[0]
    total = pieces + paired
    columns = mod_weight.shape[1]
    vmem = pltpu.VMEM
    dma = pltpu.SemaphoreType.DMA
    anywhere = pl.BlockSpec(memory_space=pl.ANY)
    in_vmem = pl.BlockSpec(memory_space=pltpu.VMEM)
    later = (*weights, tokens, own_grad, grad_resid, resid, mlp_own, mlp_in, mod_weight)
    return pl.pallas_call(
        functools.partial(tail_kernel, dp, items),
        out_shape=[
            jax.ShapeDtypeStruct((half, width), BF16),
            jax.ShapeDtypeStruct((half, width), BF16),
            jax.ShapeDtypeStruct((total, depth, piece), F32),
            jax.ShapeDtypeStruct((count, columns), BF16),
            jax.ShapeDtypeStruct((8, width), F32),
            jax.ShapeDtypeStruct((8, width), F32),
        ],
        in_specs=[in_vmem] * 12
        + [pl.BlockSpec(memory_space=pltpu.SMEM)]
        + [anywhere] * len(later),
        out_specs=[in_vmem] * 6,
        scratch_shapes=[
            *[vmem(array.shape, array.dtype) for array in later],
            vmem((width, 4 * inner), F32),
            vmem((half, width), BF16),
            vmem((half, width), BF16),
            vmem((half, width), F32),
            vmem((pieces, width // 2, piece), BF16),
            vmem((pieces, width // 2, piece), BF16),
            vmem((pieces, width // 2, piece), BF16),
            vmem((pieces, width // 4, piece), BF16),
            vmem((pieces, width // 4, piece), BF16),
            vmem((pieces, width // 4, piece), BF16),
            vmem((total, width // 8, piece), BF16),
            vmem((total, width // 8, piece), BF16),
            vmem((pieces, width // 8, piece), BF16),
            vmem((total, group_rows(depth), piece), BF16),
            vmem((total, group_rows(depth), piece), BF16),
            vmem((8, width), F32),
            vmem((dp, early_rows, LANES), BF16),
            vmem((late_rows, LANES), F32),
            vmem((late_rows, LANES), BF16),
            vmem((late_rows, LANES), BF16),
            vmem((dp, late_rows, LANES), BF16),
            vmem((dp * max(early_rows, late_rows), LANES), F32),
            vmem((dp, 8, LANES), F32),
            vmem((dp, 8, LANES), F32),
            dma((len(later),)),
            dma((2, 3)),
            dma((2, 4, total)),
            dma((2, 4)),
            dma((2, 4)),
            dma((dp,)),
            dma((dp,)),
        ],
        compiler_params=pltpu.CompilerParams(
            collective_id=1, has_side_effects=True, vmem_limit_bytes=62 * 2**20
        ),
        cost_estimate=pl.CostEstimate(
            flops=4 * length * width * 4 * inner, bytes_accessed=20 * 2**20, transcendentals=0
        ),
        name="tail",
    )(
        *d,
        attn_in,
        grad_attn,
        heads_out,
        paired_keep,
        paired_in,
        early,
        gains,
        mod,
        conditions,
        grids,
        *later,
    )


def head_kernel(
    dp,
    cond_ref,
    mod_weight_ref,
    tokens_ref,
    grids,
    frequency_ref,
    mod_ref,
    mod_in_ref,
    tokens_all_ref,
    cos_ref,
    sin_ref,
    cond_out,
    cond_in,
    gathered,
    flat,
    out_0,
    in_0,
    out_1,
    in_1,
    keep_1,
    out_2,
    in_2,
    keep_2,
    out_3,
    in_3,
    halves,
    cond_send,
    cond_recv,
    halving_sems,
    y_sems,
):
    bits = dp.bit_length() - 1
    me = lax.axis_index("dp")
    ten = lax.axis_index("tensor")
    items = cond_ref.shape[0]
    half, width = tokens_ref.shape
    depth = width // dp
    count = dp * items
    groups = mod_weight_ref.shape[1] // LANES // 2
    span = flat.shape[0] // count
    block = items * span
    y_peer = (me, 1 - ten)
    dp_peers = [((me + step) % dp, ten) for step in range(1, dp)]

    cond_out[...] = jnp.zeros_like(cond_out)
    values = cond_ref[...].astype(F32)
    for dest in range(dp):
        cond_out[dest, :items, :depth] = values[:, dest * depth : (dest + 1) * depth]
    greet([y_peer] + dp_peers)
    cond_in[me] = cond_out[me]
    cond_copies = []
    for step, peer in enumerate(dp_peers):
        cond_copies.append(
            remote(cond_out.at[peer[0]], cond_in.at[me], cond_send.at[step], cond_recv.at[me], peer)
        )
        cond_copies[-1].start()
    own_rows = pl.ds(pl.multiple_of(ten * half, half), half)
    tokens_copy = remote(
        tokens_ref, tokens_all_ref.at[own_rows, :], y_sems.at[0, 0], y_sems.at[1, 0], y_peer
    )
    tokens_copy.start()
    tokens_all_ref[own_rows, :] = tokens_ref[...]
    for step in range(1, dp):
        source = (me + dp - step) % dp
        remote(
            cond_out.at[0], cond_in.at[source], cond_send.at[0], cond_recv.at[source], y_peer
        ).wait_recv()
    for source in range(dp):
        gathered[pl.ds(source * items, items), :] = cond_in[source, :items, :]
    raw = gathered[...]
    mod_in = (raw / (1.0 + jnp.exp(-raw))).astype(BF16)
    mod_in_ref[...] = mod_in

    for group in range(groups):
        lanes = pl.ds(pl.multiple_of((ten * groups + group) * LANES, LANES), LANES)
        flat[pl.ds(group, count, stride=span), :] = dot(mod_in[:, :depth], mod_weight_ref[:, lanes])

    def rows_of(position):
        return pl.ds(pl.multiple_of(block_at(position, me, range(bits)) * block, 8), block)

    def at(position):
        return pl.ds(position * block, block)

    def halving(bit, src, dst):
        copy = remote(
            src, dst, halving_sems.at[0, bit], halving_sems.at[1, bit], (across(me, bit), ten)
        )
        copy.start()
        return copy

    for position in range(dp // 2):
        out_0[at(position), :] = flat[rows_of(dp // 2 + position), :]
    copies = [halving(0, out_0, in_0)]

    lane = lax.broadcasted_iota(jnp.int32, (STEP, LANES), 1)

    def tables(first, last):
        def one(index, carry):
            first = pl.multiple_of(index * STEP, STEP)
            rows = pl.ds(first, STEP)
            position = lax.broadcasted_iota(jnp.int32, (STEP, LANES), 0) + first
            origin = jnp.zeros((STEP, LANES), jnp.int32)
            breadth = jnp.ones((STEP, LANES), jnp.int32)
            for item, (start, size) in enumerate(item_spans(grids, items)):
                inside = (position >= start) & (position < start + size)
                origin = jnp.where(inside, start, origin)
                breadth = jnp.where(inside, grids[item, 1], breadth)
            local = (position - origin).astype(F32)
            breadth = breadth.astype(F32)
            down = jnp.floor((local + 0.5) / breadth)
            angles = jnp.where(lane < 2 * QUARTER, down, local - down * breadth) * frequency_ref[...]
            cos_ref[rows, :] = jnp.where(lane < HD, jnp.cos(angles), 0.0)
            sin_ref[rows, :] = jnp.where(lane < HD, jnp.sin(angles), 0.0)
            return carry

        lax.fori_loop(first, last, one, 0)

    steps = 2 * half // STEP
    tables(0, steps // 3)
    copies[0].wait_recv()
    for position in range(dp // 4):
        out_1[at(position), :] = flat[rows_of(dp // 4 + position), :] + in_0[at(dp // 4 + position), :]
    copies.append(halving(1, out_1, in_1))
    for position in range(dp // 4):
        keep_1[at(position), :] = flat[rows_of(position), :] + in_0[at(position), :]
    tables(steps // 3, 2 * steps // 3)
    copies[1].wait_recv()
    for position in range(dp // 8):
        later = at(dp // 8 + position)
        out_2[at(position), :] = keep_1[later, :] + in_1[later, :]
    copies.append(halving(2, out_2, in_2))
    for position in range(dp // 8):
        keep_2[at(position), :] = keep_1[at(position), :] + in_1[at(position), :]
    tables(2 * steps // 3, steps)
    copies[2].wait_recv()
    out_3[...] = keep_2[at(1), :] + in_2[at(1), :]
    copies.append(halving(3, out_3, in_3))
    copies[3].wait_recv()
    halves[ten] = keep_2[at(0), :] + in_2[at(0), :] + in_3[...]
    mod_copy = remote(halves.at[ten], halves.at[ten], y_sems.at[0, 1], y_sems.at[1, 1], y_peer)
    mod_copy.start()
    mod_ref[...] = jnp.zeros_like(mod_ref)
    remote(
        halves.at[1 - ten], halves.at[1 - ten], y_sems.at[0, 1], y_sems.at[1, 1], y_peer
    ).wait_recv()
    for side in range(2):
        for item in range(items):
            for group in range(groups):
                first = (side * groups + group) * LANES
                row = item * span + group
                mod_ref[item : item + 1, first : first + LANES] = halves[side, row : row + 1, :]
    tokens_copy.wait_recv()
    for copy in cond_copies + copies + [tokens_copy, mod_copy]:
        copy.wait_send()


def head(dp, conditions, mod_weight, tokens, grids, frequency):
    half, width = tokens.shape
    items = conditions.shape[0]
    count = dp * items
    groups = mod_weight.shape[1] // LANES // 2
    span = -(-groups // 8) * 8
    block = items * span
    vmem = pltpu.VMEM
    dma = pltpu.SemaphoreType.DMA
    in_vmem = pl.BlockSpec(memory_space=pltpu.VMEM)
    return pl.pallas_call(
        functools.partial(head_kernel, dp),
        out_shape=[
            jax.ShapeDtypeStruct((8, 6 * width), F32),
            jax.ShapeDtypeStruct((count, LANES), BF16),
            jax.ShapeDtypeStruct((2 * half, width), BF16),
            jax.ShapeDtypeStruct((2 * half, LANES), F32),
            jax.ShapeDtypeStruct((2 * half, LANES), F32),
        ],
        in_specs=[in_vmem] * 3 + [pl.BlockSpec(memory_space=pltpu.SMEM), in_vmem],
        out_specs=[in_vmem] * 5,
        scratch_shapes=[
            vmem((dp, 8, LANES), F32),
            vmem((dp, 8, LANES), F32),
            vmem((count, LANES), F32),
            vmem((count * span, LANES), F32),
            vmem((dp // 2 * block, LANES), F32),
            vmem((dp // 2 * block, LANES), F32),
            vmem((dp // 4 * block, LANES), F32),
            vmem((dp // 4 * block, LANES), F32),
            vmem((dp // 4 * block, LANES), F32),
            vmem((dp // 8 * block, LANES), F32),
            vmem((dp // 8 * block, LANES), F32),
            vmem((dp // 8 * block, LANES), F32),
            vmem((block, LANES), F32),
            vmem((block, LANES), F32),
            vmem((2, block, LANES), F32),
            dma((dp,)),
            dma((dp,)),
            dma((2, 4)),
            dma((2, 2)),
        ],
        compiler_params=pltpu.CompilerParams(
            collective_id=3, has_side_effects=True, vmem_limit_bytes=62 * 2**20
        ),
        cost_estimate=pl.CostEstimate(
            flops=2 * count * width // dp * 6 * width, bytes_accessed=8 * 2**20, transcendentals=0
        ),
        name="head",
    )(conditions, mod_weight, tokens, grids, frequency)


def middle_kernel(
    items,
    chunk,
    step,
    heads_ref,
    proj_ref,
    tokens_ref,
    own_grad_ref,
    other_grad_ref,
    grids,
    mod_ref,
    gate_hbm,
    up_hbm,
    down_hbm,
    grad_heads_ref,
    grad_attn_ref,
    grad_resid_ref,
    resid_ref,
    early_sum_ref,
    mlp_other_ref,
    mlp_own_ref,
    last_keep_ref,
    last_out_ref,
    paired_keep_ref,
    paired_out_ref,
    gate_ref,
    up_ref,
    down_ref,
    attn,
    grad_mlp,
    mlp_in,
    hidden,
    grad_gate,
    grad_up,
    y_out,
    y_in,
    part,
    core_out,
    core_keep,
    core_in,
    x_out,
    x_in,
    x_keep,
    z_in,
    early_ref,
    early_rows,
    early_out,
    early_in,
    y_sems,
    core_sems,
    x_sems,
    z_sems,
    load_sems,
):
    dp = lax.axis_size("dp")
    bits = dp.bit_length() - 1
    me = lax.axis_index("dp")
    ten = lax.axis_index("tensor")
    half, width = tokens_ref.shape
    depth = width // dp
    units = gate_ref.shape[1]
    piece = part.shape[1]
    per_weight = units // piece
    chunks = half // chunk
    y_peer = (me, 1 - ten)
    core_peer = (across(me, 0), ten)
    x_peer = (across(me, 1), ten)
    z_peer = (across(me, 2), ten)
    loads = [
        pltpu.make_async_copy(source, there, load_sems.at[which])
        for which, (source, there) in enumerate(
            ((gate_hbm, gate_ref), (up_hbm, up_ref), (down_hbm, down_ref))
        )
    ]
    for load in loads:
        load.start()
    greet([y_peer, core_peer, x_peer, z_peer])

    def rows_at(first, count=chunk):
        return pl.ds(pl.multiple_of(first, 16), count)

    def y_copy(kind, c, src, dst):
        return remote(
            src, dst, y_sems.at[0, kind, c], y_sems.at[1, kind, c], y_peer
        )

    def item_at(first_token, rows):
        return item_of(grids, items, first_token + rows.start)

    def in_steps(c, body):
        def one(index, carry):
            body(pl.ds(pl.multiple_of(c * chunk + index * step, step), step))
            return carry

        lax.fori_loop(0, chunk // step, one, 0, unroll=UNROLL)

    proj_copies = []
    for c in range(chunks):
        rows = pl.ds(c * chunk, chunk)
        y_out[rows, :] = dot(
            heads_ref[rows_at((1 - ten) * half + c * chunk), :], proj_ref[...]
        ).astype(BF16)
        proj_copies.append(y_copy(0, c, y_out.at[rows, :], y_in.at[rows, :]))
        proj_copies[c].start()
    for c in range(chunks):
        attn[pl.ds(c * chunk, chunk), :] = dot(
            heads_ref[rows_at(ten * half + c * chunk), :], proj_ref[...]
        )
    for c in range(chunks):

        def scale_grads(rows):
            later = pl.ds(pl.multiple_of(rows.start + half, step), step)
            grad_mlp[rows, :] = (
                mod_values(item_at(ten * half, rows), mod_ref, 5) * own_grad_ref[rows, :].astype(F32)
            ).astype(BF16)
            grad_mlp[later, :] = (
                mod_values(item_at((1 - ten) * half, rows), mod_ref, 5)
                * other_grad_ref[rows, :].astype(F32)
            ).astype(BF16)

        in_steps(c, scale_grads)

    for load in loads:
        load.wait()

    def mlp(c):
        rows = pl.ds(c * chunk, chunk)
        for first in range(0, units, 256):
            columns = pl.ds(first, 256)
            gate = dot(mlp_in[rows, :], gate_ref[:, columns])
            up = dot(mlp_in[rows, :], up_ref[:, columns])
            grad = dot_t(grad_mlp[rows, :], down_ref[columns, :])
            sigma = 1.0 / (1.0 + jnp.exp(-gate))
            silu = gate * sigma
            hidden[rows, columns] = (silu * up).astype(BF16)
            grad_gate[rows, columns] = (
                grad * up * (sigma * (1.0 + gate * (1.0 - sigma)))
            ).astype(BF16)
            grad_up[rows, columns] = (grad * silu).astype(BF16)

    mlp_copies = []
    for c in range(chunks):
        proj_copies[c].wait_recv()

        def norm(rows):
            mixed = attn[rows, :] + y_in[rows, :].astype(F32)
            attn[rows, :] = mixed
            item = item_at(ten * half, rows)
            resid = tokens_ref[rows, :].astype(F32) + mod_values(item, mod_ref, 2) * mixed
            resid_ref[rows, :] = resid
            normed, _ = layer_norm(resid)
            mlp_in[rows, :] = (
                normed * (1.0 + mod_values(item, mod_ref, 4)) + mod_values(item, mod_ref, 3)
            ).astype(BF16)

        in_steps(c, norm)
        mlp_copies.append(
            y_copy(
                1, c, mlp_in.at[pl.ds(c * chunk, chunk), :], mlp_in.at[pl.ds(half + c * chunk, chunk), :]
            )
        )
        mlp_copies[c].start()
    for c in range(chunks):
        mlp(c)

    def back(first):
        rows = pl.ds(first, chunk)
        return dot_t(grad_gate[rows, :], gate_ref[...]) + dot_t(grad_up[rows, :], up_ref[...])

    back_copies = []
    for c in range(chunks):
        mlp_copies[c].wait_recv()
        mlp(chunks + c)
        rows = pl.ds(c * chunk, chunk)
        proj_copies[c].wait_send()
        y_out[rows, :] = back(half + c * chunk).astype(BF16)
        back_copies.append(y_copy(2, c, y_out.at[rows, :], y_in.at[rows, :]))
        back_copies[c].start()

    orders = [(0, 2, 1, 3) if p % 2 and p < 2 * per_weight else (0, 1, 2, 3) for p in range(6)]

    def packed(position, order):
        def rows_of(p):
            return part[pl.ds(pl.multiple_of(block_at(p, me, order) * depth, 8), depth), :]

        return jnp.concatenate([rows_of(position), rows_of(position + 1)]).astype(BF16)

    core_copies = []
    x_copies = []

    def weight_grad(p):
        which, column = divmod(p, per_weight)
        columns = pl.ds(column * piece, piece)
        left, right = ((grad_mlp, hidden), (mlp_in, grad_gate), (mlp_in, grad_up))[which]
        slot = p % 2
        for first in range(0, width, LANES):
            rows = pl.ds(first, LANES)
            part[rows, :] = t_dot(left[:, rows], right[:, columns])
        if p >= 2:
            core_copies[p - 2].wait_send()
        for position in range(0, dp // 2, 2):
            rows = pl.ds(position * depth, 2 * depth)
            core_out[slot, rows, :] = packed(dp // 2 + position, orders[p])
        core_copies.append(
            remote(
                core_out.at[slot], core_in.at[p], core_sems.at[0, p], core_sems.at[1, p], core_peer
            )
        )
        core_copies[p].start()
        for position in range(0, dp // 2, 2):
            rows = pl.ds(position * depth, 2 * depth)
            core_keep[slot, rows, :] = packed(position, orders[p])

    quarter = width // 4

    def cross(p):
        slot = p % 2
        core_copies[p].wait_recv()

        def total(rows):
            return (core_keep[slot, rows, :].astype(F32) + core_in[p, rows, :].astype(F32)).astype(
                BF16
            )

        if p < 2 * per_weight:
            x_out[p] = total(pl.ds(quarter, quarter))
            x_copies.append(
                remote(
                    x_out.at[p],
                    x_in.at[p],
                    x_sems.at[0, p],
                    x_sems.at[1, p],
                    (across(me, orders[p][1]), ten),
                )
            )
            x_copies[p].start()
            x_keep[p] = total(pl.ds(0, quarter))
        else:
            paired_keep_ref[p - 2 * per_weight] = total(pl.ds(0, quarter))
            paired_out_ref[p - 2 * per_weight] = total(pl.ds(quarter, quarter))

    eighth = width // 8
    z_copies = []

    def ascend(p):
        x_copies[p].wait_recv()
        x_copies[p].wait_send()
        rows = pl.ds(eighth, eighth)
        z_out = x_out.at[p, pl.ds(0, eighth), :]
        x_out[p, :eighth, :] = (
            x_keep[p, rows, :].astype(F32) + x_in[p, rows, :].astype(F32)
        ).astype(BF16)
        next_peer = (across(me, orders[p][2]), ten)
        z_copies.append(remote(z_out, z_in.at[p], z_sems.at[0, p], z_sems.at[1, p], next_peer))
        z_copies[p].start()

    pieces = 3 * per_weight
    weight_grad(0)
    weight_grad(1)
    cross(0)
    for c in range(chunks):
        grad_resid_ref[pl.ds(c * chunk, chunk), :] = back(c * chunk)

    early_ref[...] = jnp.zeros_like(early_ref)
    grad_copies = []
    for c in range(chunks):
        back_copies[c].wait_recv()

        def norm_grad(rows):
            grad = grad_resid_ref[rows, :] + y_in[rows, :].astype(F32)
            normed, inv = layer_norm(resid_ref[rows, :])
            item = item_at(ten * half, rows)
            n = grad * (1.0 + mod_values(item, mod_ref, 4))
            grad_resid = own_grad_ref[rows, :].astype(F32) + norm_back(n, normed, inv)
            grad_resid_ref[rows, :] = grad_resid
            there = pl.ds(pl.multiple_of(rows.start + ten * half, step), step)
            grad_attn_ref[there, :] = (mod_values(item, mod_ref, 2) * grad_resid).astype(BF16)
            for kind, values in enumerate((grad_resid * attn[rows, :], grad, grad * normed)):
                lanes = slice(kind * width, (kind + 1) * width)
                add_rows(early_ref, item, items, values, lanes)

        in_steps(c, norm_grad)
        rows = rows_at(ten * half + c * chunk)
        grad_copies.append(y_copy(3, c, grad_attn_ref.at[rows, :], grad_attn_ref.at[rows, :]))
        grad_copies[c].start()
        weight_grad(2 + c)
        cross(1 + c)

    pack_rows(early_rows, items, [(early_ref, 0), (early_ref, 1), (early_ref, 2)])
    early_out[...] = early_rows[...].astype(BF16)
    early_copy = y_copy(4, 0, early_out, early_in)
    early_copy.start()

    weight_grad(4)
    cross(3)
    ascend(0)
    weight_grad(5)
    cross(4)
    ascend(1)
    for c in range(chunks):
        rows = pl.ds(c * chunk, chunk)
        mlp_other_ref[rows, :] = dot(
            hidden[pl.ds(half + c * chunk, chunk), :], down_ref[...]
        ).astype(BF16)
        mlp_own_ref[rows, :] = dot(hidden[rows, :], down_ref[...])
        own_rows = rows_at(ten * half + c * chunk)
        grad_heads_ref[own_rows, :] = dot_t(grad_attn_ref[own_rows, :], proj_ref[...]).astype(BF16)
    cross(5)
    ascend(2)
    for c in range(chunks):
        rows = rows_at((1 - ten) * half + c * chunk)
        y_copy(3, c, grad_attn_ref.at[rows, :], grad_attn_ref.at[rows, :]).wait_recv()
        grad_heads_ref[rows, :] = dot_t(grad_attn_ref[rows, :], proj_ref[...]).astype(BF16)
    early_copy.wait_recv()
    early_sum_ref[...] = (early_out[...].astype(F32) + early_in[...].astype(F32)).astype(BF16)
    ascend(3)
    for p in range(2 * per_weight):
        z_copies[p].wait_recv()
        total = (
            x_keep[p, :eighth, :].astype(F32)
            + x_in[p, :eighth, :].astype(F32)
            + z_in[p].astype(F32)
        )
        last_keep_ref[p] = total[:depth].astype(BF16)
        last_out_ref[p] = total[depth:].astype(BF16)
    for copy in mlp_copies + back_copies + grad_copies + core_copies[-2:] + z_copies + [early_copy]:
        copy.wait_send()


def middle(heads_out, proj, tokens, own_grad, other_grad, grids, mod, gate, up, down):
    half, width = tokens.shape
    length = 2 * half
    units = gate.shape[1]
    inner = heads_out.shape[1]
    items = grids.shape[0]
    dp = lax.axis_size("dp")
    early_rows = items * group_rows(3 * width // LANES)
    chunk = half // 2
    chunks = half // chunk
    piece = units // 2
    pieces = 6
    vmem = pltpu.VMEM
    dma = pltpu.SemaphoreType.DMA
    anywhere = pl.BlockSpec(memory_space=pl.ANY)
    return pl.pallas_call(
        functools.partial(middle_kernel, items, chunk, STEP),
        out_shape=[
            jax.ShapeDtypeStruct((length, inner), BF16),
            jax.ShapeDtypeStruct((length, width), BF16),
            jax.ShapeDtypeStruct((half, width), F32),
            jax.ShapeDtypeStruct((half, width), F32),
            jax.ShapeDtypeStruct((early_rows, LANES), BF16),
            jax.ShapeDtypeStruct((half, width), BF16),
            jax.ShapeDtypeStruct((half, width), F32),
            jax.ShapeDtypeStruct((4, width // dp, piece), BF16),
            jax.ShapeDtypeStruct((4, width // dp, piece), BF16),
            jax.ShapeDtypeStruct((2, width // 4, piece), BF16),
            jax.ShapeDtypeStruct((2, width // 4, piece), BF16),
        ],
        in_specs=[pl.BlockSpec(memory_space=pltpu.VMEM)] * 5
        + [pl.BlockSpec(memory_space=pltpu.SMEM), pl.BlockSpec(memory_space=pltpu.VMEM)]
        + [anywhere] * 3,
        out_specs=[pl.BlockSpec(memory_space=pltpu.VMEM)] * 11,
        scratch_shapes=[
            vmem((width, units), BF16),
            vmem((width, units), BF16),
            vmem((units, width), BF16),
            vmem((half, width), F32),
            vmem((length, width), BF16),
            vmem((length, width), BF16),
            vmem((length, units), BF16),
            vmem((length, units), BF16),
            vmem((length, units), BF16),
            vmem((half, width), BF16),
            vmem((half, width), BF16),
            vmem((width, piece), F32),
            vmem((2, width // 2, piece), BF16),
            vmem((2, width // 2, piece), BF16),
            vmem((pieces, width // 2, piece), BF16),
            vmem((4, width // 4, piece), BF16),
            vmem((4, width // 4, piece), BF16),
            vmem((4, width // 4, piece), BF16),
            vmem((4, width // 8, piece), BF16),
            vmem((8, 3 * width), F32),
            vmem((early_rows, LANES), F32),
            vmem((early_rows, LANES), BF16),
            vmem((early_rows, LANES), BF16),
            dma((2, 5, chunks)),
            dma((2, pieces)),
            dma((2, 4)),
            dma((2, 4)),
            dma((3,)),
        ],
        compiler_params=pltpu.CompilerParams(
            collective_id=2, has_side_effects=True, vmem_limit_bytes=62 * 2**20
        ),
        cost_estimate=pl.CostEstimate(
            flops=18 * length * width * units, bytes_accessed=30 * 2**20, transcendentals=0
        ),
        name="middle",
    )(heads_out, proj, tokens, own_grad, other_grad, grids, mod, gate, up, down)


def shards_in_kernels(
    tokens,
    conditions,
    item_grids,
    mod_weight,
    query_weight,
    key_weight,
    value_weight,
    proj_weight,
    query_gain,
    key_gain,
    gate_weight,
    up_weight,
    down_weight,
    out_grad,
):
    half, width = tokens.shape
    dp = lax.axis_size("dp")
    items = conditions.shape[0]
    owned = mod_weight.shape[0]
    grids = item_grids
    lane = np.arange(LANES)
    frequency = jnp.asarray(
        (10000.0 ** (-(lane % QUARTER) / QUARTER)).astype(np.float32)[None, :]
    )
    mod, mod_in_own, tokens_all, cosine, sine = head(
        dp, conditions, mod_weight, tokens, grids, frequency
    )
    out_grad_later, mod = lax.optimization_barrier((out_grad, mod))
    out_grad_other = swap(out_grad_later)
    gain_q = query_gain[None, :]
    gain_k = key_gain[None, :]
    weights = (query_weight.T, key_weight.T, value_weight.T)
    attn_in, heads_out, *saved = attend(
        grids, tokens_all, mod, *weights, gain_q, gain_k, cosine, sine
    )
    (
        grad_heads,
        grad_attn_all,
        grad_resid,
        resid,
        early,
        mlp_other,
        mlp_own,
        last_keep,
        last_out,
        paired_keep,
        paired_out,
    ) = middle(
        heads_out,
        proj_weight,
        tokens,
        out_grad,
        out_grad_other,
        grids,
        mod,
        gate_weight,
        up_weight,
        down_weight,
    )
    mlp_recv = swap(mlp_other)
    last_in = lax.ppermute(last_out, "dp", partners(3))
    paired_in = lax.ppermute(paired_out, "dp", partners(1))
    *d, gain_parts = attend_back(grids, grad_heads, saved, gain_q, gain_k, cosine, sine)
    grad_tokens, block_out, sums, grad_mod_all, gain_sums, grad_cond = tail(
        dp,
        d,
        attn_in,
        grad_attn_all,
        heads_out,
        paired_keep,
        paired_in,
        early,
        gain_parts,
        mod,
        conditions,
        grids,
        weights,
        tokens,
        out_grad,
        grad_resid,
        resid,
        mlp_own,
        mlp_recv,
        mod_weight,
    )
    last = last_keep.astype(F32) + last_in.astype(F32)
    grad_mod_weight = t_dot(mod_in_own[:, :owned], grad_mod_all)
    attn_sum = jnp.concatenate(list(sums[2:]), axis=1)
    inner = heads_out.shape[1]
    grad_q, grad_k, grad_v, grad_proj = (
        attn_sum[:, which * inner : (which + 1) * inner] for which in range(4)
    )
    return (
        block_out,
        grad_tokens,
        grad_cond[:items],
        grad_mod_weight,
        grad_q,
        grad_k,
        grad_v,
        grad_proj.T,
        gain_sums[0, :HD],
        gain_sums[1, :HD],
        jnp.concatenate([last[2], last[3]], axis=1),
        jnp.concatenate(list(sums[:2]), axis=1),
        jnp.concatenate([last[0], last[1]], axis=1).T,
    )


def shards(
    tokens,
    conditions,
    item_grids,
    mod_weight,
    query_weight,
    key_weight,
    value_weight,
    proj_weight,
    query_gain,
    key_gain,
    gate_weight,
    up_weight,
    down_weight,
    out_grad,
):
    half, width = tokens.shape
    length = 2 * half
    dp = lax.axis_size("dp")
    bits = dp.bit_length() - 1
    me = lax.axis_index("dp")
    second = lax.axis_index("tensor") == 1
    own_first = lax.axis_index("tensor") * half
    other_first = half - own_first
    items = conditions.shape[0]
    owned = mod_weight.shape[0]

    tokens_other = swap(tokens)
    out_grad_other = swap(out_grad)

    member, row_pos, col_pos = geometry(item_grids, length)
    cosine, sine = rope_tables(row_pos, col_pos)
    gain_q = query_gain[None, :]
    gain_k = key_gain[None, :]
    member_own = lax.dynamic_slice_in_dim(member, own_first, half, 0)
    member_other = lax.dynamic_slice_in_dim(member, other_first, half, 0)

    cond_all = lax.all_gather(conditions, "dp", axis=0, tiled=True)
    mod_in_all = jax.nn.silu(cond_all.astype(F32)).astype(BF16)
    mod_in_own = lax.dynamic_slice_in_dim(mod_in_all, me * owned, owned, 1)
    mod_part = dot(mod_in_own, mod_weight)
    mod_parts = lax.all_to_all(
        mod_part.reshape(dp, items, 6 * width), "dp", split_axis=0, concat_axis=0, tiled=True
    )
    modulation = jnp.sum(mod_parts.astype(F32), axis=0)
    shift_one, scale_one, gate_one, shift_two, scale_two, gate_two = jnp.split(
        modulation, 6, axis=1
    )

    tokens_float = tokens.astype(F32)
    tokens_all = in_order(tokens, tokens_other, second)

    w_qkv = jnp.concatenate([query_weight, key_weight, value_weight], axis=1)
    mod = jnp.pad(modulation, ((0, 8 - items), (0, 0)))
    attn_in, heads_out, *saved = attend(
        item_grids,
        tokens_all,
        mod,
        query_weight.T,
        key_weight.T,
        value_weight.T,
        gain_q,
        gain_k,
        cosine,
        sine,
    )
    inner = heads_out.shape[1]
    grad_out = out_grad.astype(F32)
    gate_two_own = per_token(member_own, gate_two)

    heads_other = lax.dynamic_slice_in_dim(heads_out, other_first, half, 0)
    heads_own = lax.dynamic_slice_in_dim(heads_out, own_first, half, 0)
    attn_recv = swap(dot(heads_other, proj_weight).astype(BF16))
    attn_out = dot(heads_own, proj_weight) + attn_recv.astype(F32)

    gate_one_own = per_token(member_own, gate_one)
    scale_two_own = per_token(member_own, scale_two)
    resid = tokens_float + gate_one_own * attn_out
    norm_two, inv_two = layer_norm(resid)
    mlp_in = (norm_two * (1.0 + scale_two_own) + per_token(member_own, shift_two)).astype(BF16)
    mlp_in_all = jnp.concatenate([mlp_in, swap(mlp_in)])

    grad_mlp_all = jnp.concatenate(
        [
            (gate_two_own * grad_out).astype(BF16),
            (per_token(member_other, gate_two) * out_grad_other.astype(F32)).astype(BF16),
        ]
    )
    grad_hidden = dot_t(grad_mlp_all, down_weight)

    gate_pre = dot(mlp_in_all, gate_weight)
    up_pre = dot(mlp_in_all, up_weight)
    silu_gate = jax.nn.silu(gate_pre)
    hidden = (silu_gate * up_pre).astype(BF16)
    grad_gate_pre = (grad_hidden * up_pre * silu_grad(gate_pre)).astype(BF16)
    grad_up_pre = (grad_hidden * silu_gate).astype(BF16)

    back_other = dot_t(grad_gate_pre[half:], gate_weight) + dot_t(grad_up_pre[half:], up_weight)
    back_recv = swap(back_other.astype(BF16))
    mlp_recv = swap(dot(hidden[half:], down_weight).astype(BF16))
    grad_mlp_in = (
        dot_t(grad_gate_pre[:half], gate_weight)
        + dot_t(grad_up_pre[:half], up_weight)
        + back_recv.astype(F32)
    )

    grad_mlp_rows = halving_rows(grad_mlp_all, bits)
    mlp_in_rows = halving_rows(mlp_in_all, bits)
    down_part = first_halving(grad_mlp_rows, hidden)
    gate_part = first_halving(mlp_in_rows, grad_gate_pre)
    up_part = first_halving(mlp_in_rows, grad_up_pre)

    mlp_out = dot(hidden[:half], down_weight) + mlp_recv.astype(F32)
    block_out = (resid + gate_two_own * mlp_out).astype(BF16)

    grad_resid = grad_out + norm_back(grad_mlp_in * (1.0 + scale_two_own), norm_two, inv_two)
    grad_attn = (gate_one_own * grad_resid).astype(BF16)
    grad_attn_all = in_order(grad_attn, swap(grad_attn), second)
    grad_heads = dot_t(grad_attn_all, proj_weight).astype(BF16)
    grad_heads, down_part, gate_part, up_part = lax.optimization_barrier(
        (grad_heads, down_part, gate_part, up_part)
    )
    grad_down = rest_of_halving(down_part, bits).T
    grad_gate = rest_of_halving(gate_part, bits)
    grad_up = rest_of_halving(up_part, bits)
    *d, gain_parts = attend_back(item_grids, grad_heads, saved, gain_q, gain_k, cosine, sine)

    d = jnp.concatenate(d, axis=1)
    early = jnp.concatenate(
        [
            per_item(member_own, grad_resid * attn_out),
            per_item(member_own, grad_mlp_in),
            per_item(member_own, grad_mlp_in * norm_two),
            per_item(member_own, grad_out * mlp_out),
        ],
        axis=1,
    )
    def attn_back(first):
        return dot_t(lax.dynamic_slice_in_dim(d, first, half, 0), w_qkv)

    attn_back_recv = swap(attn_back(other_first).astype(BF16))
    grad_attn_in = attn_back(own_first) + attn_back_recv.astype(F32)
    attn_sum = rest_of_halving(
        jnp.concatenate(
            [
                first_halving(halving_rows(attn_in, bits), d),
                first_halving(halving_rows(grad_attn_all, bits), heads_out),
            ],
            axis=1,
        ),
        bits,
    )
    norm_one, inv_one = layer_norm(tokens_float)
    scale_one_own = per_token(member_own, scale_one)
    grad_tokens = (
        grad_resid + norm_back(grad_attn_in * (1.0 + scale_one_own), norm_one, inv_one)
    ).astype(BF16)
    part_mod = jnp.concatenate(
        [per_item(member_own, grad_attn_in), per_item(member_own, grad_attn_in * norm_one), early],
        axis=1,
    )
    gains = jnp.pad(gain_parts[:2].reshape(1, 2 * LANES), ((0, 0), (0, 6 * width - 2 * LANES)))
    part_small = jnp.concatenate([part_mod, gains]).astype(BF16)
    small = part_small.astype(F32) + swap(part_small).astype(F32)
    small_all = lax.all_gather(small.astype(BF16), "dp", axis=0, tiled=False)
    grad_mod_all = small_all[:, :items].reshape(dp * items, 6 * width)
    gain_sums = jnp.sum(small_all[:, items, : 2 * LANES].astype(F32), axis=0).reshape(2, LANES)
    cond_parts = lax.all_to_all(
        dot_t(grad_mod_all, mod_weight).reshape(dp, items, owned),
        "dp",
        split_axis=0,
        concat_axis=0,
        tiled=True,
    )

    grad_mod_weight = t_dot(mod_in_own, grad_mod_all)
    grad_mod_in = cond_parts.transpose(1, 0, 2).reshape(items, dp * owned)
    grad_conditions = silu_grad(conditions.astype(F32)) * grad_mod_in
    grad_q, grad_k, grad_v, grad_proj = (
        attn_sum[:, which * inner : (which + 1) * inner] for which in range(4)
    )
    return (
        block_out,
        grad_tokens,
        grad_conditions,
        grad_mod_weight,
        grad_q,
        grad_k,
        grad_v,
        grad_proj.T,
        gain_sums[0, :HD],
        gain_sums[1, :HD],
        grad_gate,
        grad_up,
        grad_down,
    )


def solution(mesh):
    tokens = P(("dp", "tensor"), None)
    rows = P("dp", None)
    columns = P(None, "tensor")
    inner = P("tensor", None)
    both = P("dp", "tensor")
    turned = P("tensor", "dp")
    in_kernels = mesh.shape["dp"] == 16
    return jax.shard_map(
        shards_in_kernels if in_kernels else shards,
        mesh=mesh,
        in_specs=(
            tokens,
            rows,
            rows,
            rows,
            columns,
            columns,
            columns,
            inner,
            P(),
            P(),
            columns,
            columns,
            inner,
            tokens,
        ),
        out_specs=(
            tokens,
            tokens,
            rows,
            rows,
            both,
            both,
            both,
            turned,
            P(),
            P(),
            both,
            both,
            turned,
        ),
        check_vma=False,
    )
```

```python
import functools

import jax
import jax.numpy as jnp
import numpy as np
from jax import lax
from jax.experimental import pallas as pl
from jax.experimental.pallas import tpu as pltpu
from jax.sharding import PartitionSpec as P

HD = 72
QUARTER = HD // 4
LANES = 128
SPAN = 256
TILE = 256
UNROLL = 8
STEP = 16
EPSILON = 1e-06
F32 = jnp.float32
BF16 = jnp.bfloat16
HIGH = lax.Precision.HIGHEST


def silu_grad(values):
    sigma = jax.nn.sigmoid(values)
    return sigma * (1.0 + values * (1.0 - sigma))


def dot(left, right):
    return jnp.dot(left, right, preferred_element_type=F32)


def dot_t(left, right):
    return lax.dot_general(left, right, (((1,), (1,)), ((), ())), preferred_element_type=F32)


def t_dot(left, right):
    return lax.dot_general(left, right, (((0,), (0,)), ((), ())), preferred_element_type=F32)


def geometry(row_grids, length):
    heights = row_grids[:, 0]
    widths = row_grids[:, 1]
    count = row_grids.shape[0]
    sizes = heights * widths
    ends = [sizes[0]]
    for item in range(1, count):
        ends.append(ends[-1] + sizes[item])
    starts = [ends[item] - sizes[item] for item in range(count)]
    positions = jnp.arange(length, dtype=jnp.int32)
    member = jnp.stack(
        [(positions >= starts[item]) & (positions < ends[item]) for item in range(count)], axis=1
    )
    origin = sum(jnp.where(member[:, item], starts[item], 0) for item in range(count))
    width = jnp.maximum(
        sum(jnp.where(member[:, item], widths[item], 0) for item in range(count)), 1
    )
    local = positions - origin
    return member.astype(F32), local // width, local % width


def rope_tables(row_pos, col_pos):
    lane = jnp.arange(LANES)
    frequency = 10000.0 ** (-(lane % QUARTER).astype(F32) / QUARTER)
    along = jnp.where(lane[None, :] < 2 * QUARTER, row_pos[:, None], col_pos[:, None])
    angles = along.astype(F32) * frequency[None, :]
    valid = lane[None, :] < HD
    return jnp.where(valid, jnp.cos(angles), 0.0), jnp.where(valid, jnp.sin(angles), 0.0)


def turn(values):
    lane = lax.broadcasted_iota(jnp.int32, values.shape, 1)
    return jnp.where(
        lane % (2 * QUARTER) < QUARTER,
        -pltpu.roll(values, LANES - QUARTER, 1),
        pltpu.roll(values, QUARTER, 1),
    )


def only_head(values):
    lane = lax.broadcasted_iota(jnp.int32, values.shape, 1)
    return jnp.where(lane < HD, values, jnp.zeros_like(values))


def split_heads(wide, store, heads):
    rows = wide.shape[0]
    wide = jnp.concatenate([wide, jnp.zeros((rows, LANES), wide.dtype)], axis=1)
    for head in range(heads):
        store(head, only_head(wide[:, head * HD : head * HD + LANES]))


def item_spans(grids, items):
    spans = []
    start = 0
    for item in range(items):
        size = grids[item, 0] * grids[item, 1]
        spans.append((start, size))
        start = start + size
    return spans


def item_of(grids, items, first):
    which = 0
    for start, size in item_spans(grids, items):
        which = which + jnp.where(first >= start + size, 1, 0)
    return which


def mod_values(item, mod_ref, kind):
    width = mod_ref.shape[1] // 6
    return mod_ref[pl.ds(item, 1), kind * width : (kind + 1) * width]


def add_rows(sums_ref, item, items, values, lanes=slice(None)):
    row = jnp.sum(values, axis=0, keepdims=True)
    for which in range(items):
        sums_ref[which : which + 1, lanes] += jnp.where(item == which, row, 0.0)


def padded_gain(gain_ref):
    return jnp.concatenate([gain_ref[...], jnp.zeros((1, LANES - HD), F32)], axis=1)


def attend_kernel(
    heads,
    items,
    grids,
    tokens_ref,
    mod_ref,
    wq_ref,
    wk_ref,
    wv_ref,
    gq_ref,
    gk_ref,
    cos_ref,
    sin_ref,
    x_ref,
    out_ref,
    qpre_ref,
    kpre_ref,
    q_ref,
    k_ref,
    v_ref,
    probs_ref,
    qraw,
    kraw,
    vraw,
    oraw,
    wide,
):
    length = x_ref.shape[0]
    head = pl.program_id(0)

    @pl.when(head == 0)
    def _():
        def norm(index, carry):
            first = pl.multiple_of(index * STEP, STEP)
            rows = pl.ds(first, STEP)
            item = item_of(grids, items, first)
            normed, _ = layer_norm(tokens_ref[rows, :].astype(F32))
            x_ref[rows, :] = (
                normed * (1.0 + mod_values(item, mod_ref, 1)) + mod_values(item, mod_ref, 0)
            ).astype(BF16)
            return carry

        lax.fori_loop(0, length // STEP, norm, 0, unroll=UNROLL)
        for first in range(0, length, TILE):
            rows = pl.ds(first, TILE)
            x = x_ref[rows, :]
            for w_ref, raw in ((wq_ref, qraw), (wk_ref, kraw), (wv_ref, vraw)):

                def store(h, part, raw=raw):
                    raw[h, rows, :] = part.astype(raw.dtype)

                split_heads(dot_t(x, w_ref[...]), store, heads)

    for raw, pre_ref, low_ref, gain_ref in (
        (qraw, qpre_ref, q_ref, gq_ref),
        (kraw, kpre_ref, k_ref, gk_ref),
    ):
        for first in range(0, length, TILE):
            rows = pl.ds(first, TILE)
            pre = raw[head, rows, :]
            pre_ref[0, rows, :] = pre
            inv = lax.rsqrt(jnp.sum(pre * pre, axis=1, keepdims=True) / HD + EPSILON)
            normed = pre * inv * padded_gain(gain_ref)
            low_ref[0, rows, :] = (
                normed * cos_ref[rows, :] + turn(normed) * sin_ref[rows, :]
            ).astype(BF16)
    v_ref[0] = vraw[head]
    oraw[head] = vraw[head].astype(F32)
    row = lax.broadcasted_iota(jnp.int32, (SPAN, SPAN), 0)
    col = lax.broadcasted_iota(jnp.int32, (SPAN, SPAN), 1)
    row_out = lax.broadcasted_iota(jnp.int32, (SPAN, LANES), 0)
    for item, (start, size) in enumerate(item_spans(grids, items)):
        rows = pl.ds(pl.multiple_of(start, 16), SPAN)
        scores = dot_t(q_ref[0, rows, :], k_ref[0, rows, :]) * HD**-0.5
        scores = jnp.where(col < size, scores, -1e30)
        top = jnp.max(scores, axis=1, keepdims=True)
        weights = jnp.exp(scores - top)
        total = jnp.sum(weights, axis=1, keepdims=True)
        probs = jnp.where(row < size, weights / total, 0.0).astype(BF16)
        probs_ref[0, item] = probs
        mixed = dot(probs, v_ref[0, rows, :])
        oraw[head, rows, :] = jnp.where(row_out < size, mixed, oraw[head, rows, :])

    @pl.when(head == heads - 1)
    def _():
        for h in range(heads):
            wide[:, h * HD : h * HD + HD] = oraw[h][:, :HD]
        out_ref[...] = wide[...].astype(BF16)


def attend_back_kernel(
    heads,
    items,
    grids,
    grad_ref,
    qpre_ref,
    kpre_ref,
    q_ref,
    k_ref,
    v_ref,
    probs_ref,
    gq_ref,
    gk_ref,
    cos_ref,
    sin_ref,
    dq_ref,
    dk_ref,
    dv_ref,
    gain_ref,
    graw,
    dqraw,
    dkraw,
    dvraw,
    wide,
):
    length = grad_ref.shape[0]
    head = pl.program_id(0)

    @pl.when(head == 0)
    def _():
        gain_ref[...] = jnp.zeros_like(gain_ref)
        for first in range(0, length, TILE):
            rows = pl.ds(first, TILE)

            def store(h, part):
                graw[h, rows, :] = part.astype(BF16)

            split_heads(grad_ref[rows, :].astype(F32), store, heads)

    dqraw[head] = jnp.zeros((length, LANES), F32)
    dkraw[head] = jnp.zeros((length, LANES), F32)
    row_all = lax.broadcasted_iota(jnp.int32, (length, LANES), 0)
    used = sum(item_spans(grids, items)[-1])
    dvraw[head] = jnp.where(row_all >= used, graw[head].astype(F32), 0.0)
    for item, (start, _) in enumerate(item_spans(grids, items)):
        rows = pl.ds(pl.multiple_of(start, 16), SPAN)
        probs_low = probs_ref[0, item]
        probs = probs_low.astype(F32)
        grad = graw[head, rows, :]
        grad_probs = dot_t(grad, v_ref[0, rows, :])
        inner = jnp.sum(probs * grad_probs, axis=1, keepdims=True) / jnp.maximum(
            jnp.sum(probs, axis=1, keepdims=True), 0.5
        )
        grad_scores = (probs * (grad_probs - inner)).astype(BF16)
        dqraw[head, rows, :] += dot(grad_scores, k_ref[0, rows, :])
        dkraw[head, rows, :] += t_dot(grad_scores, q_ref[0, rows, :])
        dvraw[head, rows, :] += t_dot(probs_low, grad)

    for raw, pre_ref, g_ref, which in (
        (dqraw, qpre_ref, gq_ref, 0),
        (dkraw, kpre_ref, gk_ref, 1),
    ):
        for first in range(0, length, TILE):
            rows = pl.ds(first, TILE)
            turned = raw[head, rows, :] * HD**-0.5
            normed = turned * cos_ref[rows, :] - turn(turned * sin_ref[rows, :])
            pre = pre_ref[0, rows, :]
            inv = lax.rsqrt(jnp.sum(pre * pre, axis=1, keepdims=True) / HD + EPSILON)
            unit = pre * inv
            gain_ref[which : which + 1, :] += jnp.sum(normed * unit, axis=0, keepdims=True)
            scaled = normed * padded_gain(g_ref)
            along = jnp.sum(scaled * unit, axis=1, keepdims=True) / HD
            raw[head, rows, :] = inv * (scaled - unit * along)

    @pl.when(head == heads - 1)
    def _():
        for raw, o_ref in ((dqraw, dq_ref), (dkraw, dk_ref), (dvraw, dv_ref)):
            for h in range(heads):
                wide[:, h * HD : h * HD + HD] = raw[h][:, :HD]
            o_ref[...] = wide[...].astype(BF16)


def whole(shape):
    return pl.BlockSpec(shape, lambda h, grids: (0,) * len(shape))


def per_head(shape):
    return pl.BlockSpec((1,) + shape, lambda h, grids: (h,) + (0,) * len(shape))


def attend(grids, tokens, mod, wq, wk, wv, gain_q, gain_k, cosine, sine):
    length, width = tokens.shape
    heads = wq.shape[0] // HD
    items = grids.shape[0]
    head_f32 = jax.ShapeDtypeStruct((heads, length, LANES), F32)
    head_low = jax.ShapeDtypeStruct((heads, length, LANES), BF16)
    return pl.pallas_call(
        functools.partial(attend_kernel, heads, items),
        grid_spec=pltpu.PrefetchScalarGridSpec(
            num_scalar_prefetch=1,
            grid=(heads,),
            in_specs=[
                whole(tokens.shape),
                whole(mod.shape),
                whole(wq.shape),
                whole(wk.shape),
                whole(wv.shape),
                whole((1, HD)),
                whole((1, HD)),
                whole((length, LANES)),
                whole((length, LANES)),
            ],
            out_specs=[
                whole((length, width)),
                whole((length, heads * HD)),
                per_head((length, LANES)),
                per_head((length, LANES)),
                per_head((length, LANES)),
                per_head((length, LANES)),
                per_head((length, LANES)),
                per_head((items, SPAN, SPAN)),
            ],
            scratch_shapes=[
                pltpu.VMEM((heads, length, LANES), F32),
                pltpu.VMEM((heads, length, LANES), F32),
                pltpu.VMEM((heads, length, LANES), BF16),
                pltpu.VMEM((heads, length, LANES), F32),
                pltpu.VMEM((length, heads * HD), F32),
            ],
        ),
        out_shape=[
            jax.ShapeDtypeStruct((length, width), BF16),
            jax.ShapeDtypeStruct((length, heads * HD), BF16),
            head_f32,
            head_f32,
            head_low,
            head_low,
            head_low,
            jax.ShapeDtypeStruct((heads, items, SPAN, SPAN), BF16),
        ],
        compiler_params=pltpu.CompilerParams(vmem_limit_bytes=62 * 2**20),
        cost_estimate=pl.CostEstimate(
            flops=2 * length * width * heads * HD * 3 + 4 * heads * items * SPAN * SPAN * LANES,
            bytes_accessed=24 * 2**20,
            transcendentals=heads * items * SPAN * SPAN,
        ),
        name="attend",
    )(grids, tokens, mod, wq, wk, wv, gain_q, gain_k, cosine, sine)


def attend_back(grids, grad, saved, gain_q, gain_k, cosine, sine):
    length, width = grad.shape
    heads = width // HD
    items = grids.shape[0]
    out = jax.ShapeDtypeStruct((length, width), BF16)
    return pl.pallas_call(
        functools.partial(attend_back_kernel, heads, items),
        grid_spec=pltpu.PrefetchScalarGridSpec(
            num_scalar_prefetch=1,
            grid=(heads,),
            in_specs=[
                whole(grad.shape),
                per_head((length, LANES)),
                per_head((length, LANES)),
                per_head((length, LANES)),
                per_head((length, LANES)),
                per_head((length, LANES)),
                per_head((items, SPAN, SPAN)),
                whole((1, HD)),
                whole((1, HD)),
                whole((length, LANES)),
                whole((length, LANES)),
            ],
            out_specs=[
                whole((length, width)),
                whole((length, width)),
                whole((length, width)),
                whole((8, LANES)),
            ],
            scratch_shapes=[
                pltpu.VMEM((heads, length, LANES), BF16),
                pltpu.VMEM((heads, length, LANES), F32),
                pltpu.VMEM((heads, length, LANES), F32),
                pltpu.VMEM((heads, length, LANES), F32),
                pltpu.VMEM((length, width), F32),
            ],
        ),
        out_shape=[out, out, out, jax.ShapeDtypeStruct((8, LANES), F32)],
        compiler_params=pltpu.CompilerParams(vmem_limit_bytes=62 * 2**20),
        cost_estimate=pl.CostEstimate(
            flops=8 * heads * items * SPAN * SPAN * LANES,
            bytes_accessed=24 * 2**20,
            transcendentals=0,
        ),
        name="attend_back",
    )(grids, grad, *saved, gain_q, gain_k, cosine, sine)


def layer_norm(values):
    centred = values - jnp.mean(values, axis=1, keepdims=True)
    inv_std = lax.rsqrt(jnp.mean(centred * centred, axis=1, keepdims=True) + EPSILON)
    return (centred * inv_std, inv_std)


def norm_back(grad_norm, normed, inv_std):
    return inv_std * (
        grad_norm
        - jnp.mean(grad_norm, axis=1, keepdims=True)
        - normed * jnp.mean(grad_norm * normed, axis=1, keepdims=True)
    )


def per_token(member, rows):
    return sum(member[:, item, None] * rows[item][None, :] for item in range(rows.shape[0]))


def per_item(member, values):
    return jnp.stack(
        [jnp.sum(member[:, item, None] * values, axis=0) for item in range(member.shape[1])]
    )


def swap(values):
    return lax.ppermute(values, "tensor", [(0, 1), (1, 0)])


def in_order(own, other, second):
    return jnp.concatenate([jnp.where(second, other, own), jnp.where(second, own, other)])


def halving_rows(values, bits):
    dp = 2**bits
    depth = values.shape[1] // dp
    blocks = values.T.reshape((2,) * bits + (depth, values.shape[0]))
    me = lax.axis_index("dp")
    for bit in range(bits):
        axis = bits - 1 - bit
        blocks = jnp.where((me >> bit) & 1 == 1, jnp.flip(blocks, axis), blocks)
    blocks = blocks.transpose(tuple(range(bits - 1, -1, -1)) + (bits, bits + 1))
    return blocks.reshape(dp * depth, values.shape[0])


def first_halving(rows, grads):
    half = rows.shape[0] // 2
    sent = lax.ppermute(dot(rows[half:], grads).astype(BF16), "dp", partners(0))
    return (dot(rows[:half], grads) + sent.astype(F32)).astype(BF16)


def partners(bit):
    return [(i, i ^ (1 << bit)) for i in range(lax.axis_size("dp"))]


def rest_of_halving(part, bits):
    for bit in range(1, bits):
        half = part.shape[0] // 2
        sent = lax.ppermute(part[half:], "dp", partners(bit))
        part = part[:half].astype(F32) + sent.astype(F32)
        if bit < bits - 1:
            part = part.astype(BF16)
    return part.astype(F32)


def remote(src, dst, send, recv, device):
    return pltpu.make_async_remote_copy(
        src_ref=src,
        dst_ref=dst,
        send_sem=send,
        recv_sem=recv,
        device_id=device,
        device_id_type=pl.DeviceIdType.MESH,
    )


def block_at(position, me, order):
    block = 0
    for level, bit in enumerate(order):
        mine = (me // (1 << bit)) % 2
        there = (position >> (len(order) - 1 - level)) & 1
        block = block + (1 << bit) * (1 - mine if there else mine)
    return block


def across(me, bit):
    return me + (1 << bit) - 2 * (1 << bit) * ((me // (1 << bit)) % 2)


def group_rows(count):
    return -(-count // 16) * 16


def pack_rows(rows_ref, items, sources):
    span = rows_ref.shape[0] // items
    rows_ref[...] = jnp.zeros_like(rows_ref)
    for item in range(items):
        row = item * span
        for source, part in sources:
            width = rows_ref.shape[1]
            groups = source.shape[1] // width if part is None else source.shape[1] // width // 3
            for group in range(groups):
                lane = ((part or 0) * groups + group) * width
                rows_ref[row : row + 1, :] = source[item : item + 1, lane : lane + width]
                row += 1


def greet(peers):
    barrier = pltpu.get_barrier_semaphore()
    for peer in peers:
        pl.semaphore_signal(
            barrier, inc=1, device_id=peer, device_id_type=pl.DeviceIdType.MESH
        )
    pl.semaphore_wait(barrier, len(peers))


def tail_kernel(
    dp,
    items,
    dq_ref,
    dk_ref,
    dv_ref,
    attn_in_ref,
    grad_attn_ref,
    heads_ref,
    paired_keep_ref,
    paired_in_ref,
    early_ref,
    gain_ref,
    mod_ref,
    cond_ref,
    grids,
    wq_hbm,
    wk_hbm,
    wv_hbm,
    tokens_hbm,
    own_grad_hbm,
    grad_resid_hbm,
    resid_hbm,
    mlp_own_hbm,
    mlp_in_hbm,
    mod_weight_hbm,
    grad_tokens_ref,
    block_out_ref,
    sums_ref,
    all_ref,
    gains_ref,
    grad_cond_ref,
    wq_ref,
    wk_ref,
    wv_ref,
    tokens_ref,
    own_grad_ref,
    grad_resid_ref,
    resid_ref,
    mlp_own_ref,
    mlp_in_ref,
    mod_weight_ref,
    part,
    y_out,
    y_in,
    back,
    core_out,
    core_in,
    core_keep,
    x_out,
    x_in,
    x_keep,
    z_out,
    z_in,
    z_keep,
    w_out,
    w_in,
    gate_sums,
    early_all,
    late_rows,
    late_out,
    late_in,
    late_all,
    flat,
    cond_out,
    cond_in,
    load_sems,
    y_sems,
    halving_sems,
    early_sems,
    late_sems,
    cond_send,
    cond_recv,
):
    bits = dp.bit_length() - 1
    me = lax.axis_index("dp")
    ten = lax.axis_index("tensor")
    half, width = grad_tokens_ref.shape
    depth = width // dp
    inner = dq_ref.shape[1]
    pieces, _, piece = core_out.shape
    paired = paired_keep_ref.shape[0]
    groups = width // LANES
    early_span = early_ref.shape[0] // items
    late_span = late_out.shape[0] // items
    y_peer = (me, 1 - ten)
    dp_peers = [((me + step) % dp, ten) for step in range(1, dp)]
    loads = [
        pltpu.make_async_copy(source, there, load_sems.at[which])
        for which, (source, there) in enumerate(
            (
                (wq_hbm, wq_ref),
                (wk_hbm, wk_ref),
                (wv_hbm, wv_ref),
                (own_grad_hbm, own_grad_ref),
                (resid_hbm, resid_ref),
                (mlp_own_hbm, mlp_own_ref),
                (mlp_in_hbm, mlp_in_ref),
                (tokens_hbm, tokens_ref),
                (grad_resid_hbm, grad_resid_ref),
                (mod_weight_hbm, mod_weight_ref),
            )
        )
    ]
    for load in loads:
        load.start()
    greet([y_peer] + dp_peers)

    def y_copy(which, src, dst):
        return remote(src, dst, y_sems.at[0, which], y_sems.at[1, which], y_peer)

    order = (0, 1, 2, 3)
    gather_order = (1, 2, 3, 0)
    late_order = (2, 3, 0, 1)

    def halving(level, which, src, dst):
        return remote(
            src,
            dst,
            halving_sems.at[0, level, which],
            halving_sems.at[1, level, which],
            (across(me, order[level]), ten),
        )

    def doubling(level, slots, sems, order):
        count = 1 << level
        return remote(
            slots.at[pl.ds(0, count)],
            slots.at[pl.ds(count, count)],
            sems.at[0, level],
            sems.at[1, level],
            (across(me, order[level]), ten),
        )

    def in_steps(body):
        def one(index, carry):
            body(pl.multiple_of(index * STEP, STEP))
            return carry

        lax.fori_loop(0, half // STEP, one, 0, unroll=UNROLL)

    last_copies = {}

    def last_level(p, total):
        w_out[p, depth:, :] = jnp.zeros((w_out.shape[1] - depth, piece), BF16)
        w_out[p, :depth, :] = total[depth:].astype(BF16)
        last_copies[p] = halving(3, p, w_out.at[p], w_in.at[p])
        last_copies[p].start()
        sums_ref[p] = total[:depth]

    def paired_sum(p, rows):
        return paired_keep_ref[p, rows, :].astype(F32) + paired_in_ref[p, rows, :].astype(F32)

    early_all[0] = early_ref[...]
    early_copies = [doubling(level, early_all, early_sems, gather_order) for level in range(bits)]
    early_copies[0].start()

    for load in loads[:3]:
        load.wait()

    def attn_back(first):
        rows = pl.ds(pl.multiple_of(first, half), half)
        return (
            dot(dq_ref[rows, :], wq_ref[...])
            + dot(dk_ref[rows, :], wk_ref[...])
            + dot(dv_ref[rows, :], wv_ref[...])
        )

    y_out[...] = attn_back((1 - ten) * half).astype(BF16)
    back_copy = y_copy(1, y_out, y_in)
    back_copy.start()
    early_copies[0].wait_recv()
    early_copies[1].start()
    z_copies = []
    for p in range(paired):
        z_out[p] = paired_sum(p, pl.ds(2 * depth, 2 * depth)).astype(BF16)
        z_copies.append(halving(2, p, z_out.at[p], z_in.at[p]))
        z_copies[p].start()

    def weight_grad(which, left, right):
        columns = slice(which * inner, (which + 1) * inner)
        for first in range(0, width, LANES):
            rows = pl.ds(first, LANES)
            part[rows, columns] = t_dot(left[:, rows], right[...])

    core_copies = []

    def send_core(p):
        columns = pl.ds(p * piece, piece)

        def packed(position):
            def rows_of(at):
                block = block_at(at, me, order)
                return part[pl.ds(pl.multiple_of(block * depth, 8), depth), columns]

            return jnp.concatenate([rows_of(position), rows_of(position + 1)]).astype(BF16)

        for position in range(0, dp // 2, 2):
            core_out[p, pl.ds(position * depth, 2 * depth), :] = packed(dp // 2 + position)
        core_copies.append(halving(0, paired + p, core_out.at[p], core_in.at[p]))
        core_copies[p].start()
        for position in range(0, dp // 2, 2):
            core_keep[p, pl.ds(position * depth, 2 * depth), :] = packed(position)

    x_copies = []

    def cross(p):
        core_copies[p].wait_recv()
        for rows, there in (
            (pl.ds(4 * depth, 4 * depth), x_out),
            (pl.ds(0, 4 * depth), x_keep),
        ):
            there[p] = (core_keep[p, rows, :].astype(F32) + core_in[p, rows, :].astype(F32)).astype(
                BF16
            )
        x_copies.append(halving(1, paired + p, x_out.at[p], x_in.at[p]))
        x_copies[p].start()

    descents = {}

    def descend(p):
        there = paired + p
        x_copies[p].wait_recv()
        for rows, target in (
            (pl.ds(2 * depth, 2 * depth), z_out),
            (pl.ds(0, 2 * depth), z_keep),
        ):
            total = x_keep[p, rows, :].astype(F32) + x_in[p, rows, :].astype(F32)
            target[there if target is z_out else p] = total.astype(BF16)
        descents[p] = halving(2, there, z_out.at[there], z_in.at[there])
        descents[p].start()

    def finish_halving(p):
        descents[p].wait_recv()
        last_level(paired + p, z_keep[p].astype(F32) + z_in[paired + p].astype(F32))

    weight_grad(0, attn_in_ref, dq_ref)
    weight_grad(1, attn_in_ref, dk_ref)
    send_core(0)
    early_copies[1].wait_recv()
    early_copies[2].start()
    cross(0)
    weight_grad(2, attn_in_ref, dv_ref)
    send_core(1)
    for p in range(paired):
        z_copies[p].wait_recv()
        last_level(p, paired_sum(p, pl.ds(0, 2 * depth)) + z_in[p].astype(F32))
    cross(1)
    weight_grad(3, grad_attn_ref, heads_ref)
    send_core(2)

    for load in loads[3:7]:
        load.wait()
    gate_sums[...] = jnp.zeros_like(gate_sums)

    def finish_block(first):
        rows = pl.ds(first, STEP)
        item = item_of(grids, items, ten * half + first)
        mlp_out = mlp_own_ref[rows, :] + mlp_in_ref[rows, :].astype(F32)
        block_out_ref[rows, :] = (
            resid_ref[rows, :] + mod_values(item, mod_ref, 5) * mlp_out
        ).astype(BF16)
        add_rows(gate_sums, item, items, own_grad_ref[rows, :].astype(F32) * mlp_out)

    in_steps(finish_block)

    back[...] = attn_back(ten * half)
    cross(2)
    descend(0)

    count = dp * items

    def unpack(all_here, span, order, places):
        rows = items * span
        for slot in range(dp):
            source = block_at(slot, me, order[::-1])
            there = pl.multiple_of(source * rows, 16)
            flat[pl.ds(there, rows), :] = all_here[slot].astype(F32)
        for group, place in enumerate(places):
            lanes = pl.ds(place * LANES, LANES)
            all_ref[:, lanes] = flat[pl.ds(group, count, stride=span), :].astype(BF16)

    for load in loads[7:]:
        load.wait()
    back_copy.wait_recv()
    grad_cond_ref[...] = jnp.zeros_like(grad_cond_ref)
    gains_ref[...] = jnp.zeros_like(gains_ref)

    def norm_grad(first):
        rows = pl.ds(first, STEP)
        item = item_of(grids, items, ten * half + first)
        normed, inv = layer_norm(tokens_ref[rows, :].astype(F32))
        grad = back[rows, :] + y_in[rows, :].astype(F32)
        n = grad * (1.0 + mod_values(item, mod_ref, 1))
        grad_tokens_ref[rows, :] = (grad_resid_ref[rows, :] + norm_back(n, normed, inv)).astype(BF16)
        add_rows(grad_cond_ref, item, items, grad)
        add_rows(gains_ref, item, items, grad * normed)

    in_steps(norm_grad)
    pack_rows(late_rows, items, [(grad_cond_ref, None), (gains_ref, None), (gate_sums, None)])
    late_rows[3 * groups : 3 * groups + 2, :] = gain_ref[:2, :]
    late_out[...] = late_rows[...].astype(BF16)
    late_copy = y_copy(2, late_out, late_in)
    late_copy.start()
    early_copies[2].wait_recv()
    early_copies[3].start()
    late_copy.wait_recv()
    late_all[0] = (late_out[...].astype(F32) + late_in[...].astype(F32)).astype(BF16)
    late_copies = [doubling(level, late_all, late_sems, late_order) for level in range(bits)]
    late_copies[0].start()
    early_copies[3].wait_recv()
    unpack(early_all, early_span, gather_order, range(2 * groups, 5 * groups))
    late_copies[0].wait_recv()
    late_copies[1].start()
    descend(1)
    late_copies[1].wait_recv()
    late_copies[2].start()
    finish_halving(0)
    late_copies[2].wait_recv()
    late_copies[3].start()
    descend(2)
    late_copies[3].wait_recv()
    unpack(late_all, late_span, late_order, [*range(2 * groups), *range(5 * groups, 6 * groups)])
    gains = jnp.zeros((2, LANES), F32)
    for source in range(dp):
        row = source * items * late_span + 3 * groups
        gains += flat[row : row + 2, :]
    gains_ref[:2, :LANES] = gains
    flat[:count, :depth] = dot_t(all_ref[...], mod_weight_ref[...])
    cond_out[...] = jnp.zeros_like(cond_out)
    for dest in range(dp):
        cond_out[dest, :items, :depth] = flat[pl.ds(dest * items, items), :depth]
    cond_in[me] = cond_out[me]
    cond_copies = []
    for step, peer in enumerate(dp_peers):
        cond_copies.append(
            remote(cond_out.at[peer[0]], cond_in.at[me], cond_send.at[step], cond_recv.at[me], peer)
        )
        cond_copies[-1].start()
    finish_halving(1)
    finish_halving(2)
    for step in range(1, dp):
        source = (me + dp - step) % dp
        remote(
            cond_out.at[0], cond_in.at[source], cond_send.at[0], cond_recv.at[source], y_peer
        ).wait_recv()
    for source in range(dp):
        grad_cond_ref[:, source * depth : (source + 1) * depth] = cond_in[source, :, :depth]
    values = cond_ref[...].astype(F32)
    grad_cond_ref[:items, :] = grad_cond_ref[:items, :] * silu_grad(values)
    for p in last_copies:
        last_copies[p].wait_recv()
        sums_ref[p] += w_in[p, :depth, :].astype(F32)
    for copy in (
        [back_copy, late_copy]
        + early_copies
        + late_copies
        + cond_copies
        + core_copies
        + x_copies
        + z_copies
        + list(descents.values())
        + list(last_copies.values())
    ):
        copy.wait_send()


def tail(
    dp,
    d,
    attn_in,
    grad_attn,
    heads_out,
    paired_keep,
    paired_in,
    early,
    gains,
    mod,
    conditions,
    grids,
    weights,
    tokens,
    own_grad,
    grad_resid,
    resid,
    mlp_own,
    mlp_in,
    mod_weight,
):
    half, width = tokens.shape
    items = grids.shape[0]
    length = 2 * half
    inner = d[0].shape[1]
    depth = width // dp
    pieces = 3
    piece = 4 * inner // pieces
    groups = width // LANES
    early_rows = early.shape[0]
    late_rows = items * group_rows(3 * groups + 2)
    count = dp * items
    paired = paired_keep.shape[0]
    total = pieces + paired
    columns = mod_weight.shape[1]
    vmem = pltpu.VMEM
    dma = pltpu.SemaphoreType.DMA
    anywhere = pl.BlockSpec(memory_space=pl.ANY)
    in_vmem = pl.BlockSpec(memory_space=pltpu.VMEM)
    later = (*weights, tokens, own_grad, grad_resid, resid, mlp_own, mlp_in, mod_weight)
    return pl.pallas_call(
        functools.partial(tail_kernel, dp, items),
        out_shape=[
            jax.ShapeDtypeStruct((half, width), BF16),
            jax.ShapeDtypeStruct((half, width), BF16),
            jax.ShapeDtypeStruct((total, depth, piece), F32),
            jax.ShapeDtypeStruct((count, columns), BF16),
            jax.ShapeDtypeStruct((8, width), F32),
            jax.ShapeDtypeStruct((8, width), F32),
        ],
        in_specs=[in_vmem] * 12
        + [pl.BlockSpec(memory_space=pltpu.SMEM)]
        + [anywhere] * len(later),
        out_specs=[in_vmem] * 6,
        scratch_shapes=[
            *[vmem(array.shape, array.dtype) for array in later],
            vmem((width, 4 * inner), F32),
            vmem((half, width), BF16),
            vmem((half, width), BF16),
            vmem((half, width), F32),
            vmem((pieces, width // 2, piece), BF16),
            vmem((pieces, width // 2, piece), BF16),
            vmem((pieces, width // 2, piece), BF16),
            vmem((pieces, width // 4, piece), BF16),
            vmem((pieces, width // 4, piece), BF16),
            vmem((pieces, width // 4, piece), BF16),
            vmem((total, width // 8, piece), BF16),
            vmem((total, width // 8, piece), BF16),
            vmem((pieces, width // 8, piece), BF16),
            vmem((total, group_rows(depth), piece), BF16),
            vmem((total, group_rows(depth), piece), BF16),
            vmem((8, width), F32),
            vmem((dp, early_rows, LANES), BF16),
            vmem((late_rows, LANES), F32),
            vmem((late_rows, LANES), BF16),
            vmem((late_rows, LANES), BF16),
            vmem((dp, late_rows, LANES), BF16),
            vmem((dp * max(early_rows, late_rows) + LANES, LANES), F32),
            vmem((dp, 8, LANES), F32),
            vmem((dp, 8, LANES), F32),
            dma((len(later),)),
            dma((2, 3)),
            dma((2, 4, total)),
            dma((2, 4)),
            dma((2, 4)),
            dma((dp,)),
            dma((dp,)),
        ],
        compiler_params=pltpu.CompilerParams(
            collective_id=1, has_side_effects=True, vmem_limit_bytes=62 * 2**20
        ),
        cost_estimate=pl.CostEstimate(
            flops=4 * length * width * 4 * inner, bytes_accessed=20 * 2**20, transcendentals=0
        ),
        name="tail",
    )(
        *d,
        attn_in,
        grad_attn,
        heads_out,
        paired_keep,
        paired_in,
        early,
        gains,
        mod,
        conditions,
        grids,
        *later,
    )


def head_kernel(
    dp,
    cond_ref,
    mod_weight_ref,
    tokens_ref,
    grids,
    frequency_ref,
    mod_ref,
    mod_in_ref,
    tokens_all_ref,
    cos_ref,
    sin_ref,
    cond_out,
    cond_in,
    gathered,
    flat,
    out_0,
    in_0,
    out_1,
    in_1,
    keep_1,
    out_2,
    in_2,
    keep_2,
    out_3,
    in_3,
    halves,
    cond_send,
    cond_recv,
    halving_sems,
    y_sems,
):
    bits = dp.bit_length() - 1
    me = lax.axis_index("dp")
    ten = lax.axis_index("tensor")
    items = cond_ref.shape[0]
    half, width = tokens_ref.shape
    depth = width // dp
    count = dp * items
    groups = mod_weight_ref.shape[1] // LANES // 2
    span = flat.shape[0] // (count + 1)
    block = items * span
    y_peer = (me, 1 - ten)
    dp_peers = [((me + step) % dp, ten) for step in range(1, dp)]

    cond_out[...] = jnp.zeros_like(cond_out)
    values = cond_ref[...].astype(F32)
    for dest in range(dp):
        cond_out[dest, :items, :depth] = values[:, dest * depth : (dest + 1) * depth]
    greet([y_peer] + dp_peers)
    cond_in[me] = cond_out[me]
    cond_copies = []
    for step, peer in enumerate(dp_peers):
        cond_copies.append(
            remote(cond_out.at[peer[0]], cond_in.at[me], cond_send.at[step], cond_recv.at[me], peer)
        )
        cond_copies[-1].start()
    own_rows = pl.ds(pl.multiple_of(ten * half, half), half)
    tokens_copy = remote(
        tokens_ref, tokens_all_ref.at[own_rows, :], y_sems.at[0, 0], y_sems.at[1, 0], y_peer
    )
    tokens_copy.start()
    tokens_all_ref[own_rows, :] = tokens_ref[...]
    for step in range(1, dp):
        source = (me + dp - step) % dp
        remote(
            cond_out.at[0], cond_in.at[source], cond_send.at[0], cond_recv.at[source], y_peer
        ).wait_recv()
    for source in range(dp):
        gathered[pl.ds(source * items, items), :] = cond_in[source, :items, :]
    raw = gathered[...]
    mod_in = (raw / (1.0 + jnp.exp(-raw))).astype(BF16)
    mod_in_ref[...] = mod_in

    for group in range(groups):
        lanes = pl.ds(pl.multiple_of((ten * groups + group) * LANES, LANES), LANES)
        flat[pl.ds(group, count, stride=span), :] = dot(mod_in[:, :depth], mod_weight_ref[:, lanes])

    def rows_of(position):
        return pl.ds(pl.multiple_of(block_at(position, me, range(bits)) * block, 8), block)

    def at(position):
        return pl.ds(position * block, block)

    def halving(bit, src, dst):
        copy = remote(
            src, dst, halving_sems.at[0, bit], halving_sems.at[1, bit], (across(me, bit), ten)
        )
        copy.start()
        return copy

    for position in range(dp // 2):
        out_0[at(position), :] = flat[rows_of(dp // 2 + position), :]
    copies = [halving(0, out_0, in_0)]

    lane = lax.broadcasted_iota(jnp.int32, (STEP, LANES), 1)

    def tables(first, last):
        def one(index, carry):
            first = pl.multiple_of(index * STEP, STEP)
            rows = pl.ds(first, STEP)
            position = lax.broadcasted_iota(jnp.int32, (STEP, LANES), 0) + first
            origin = jnp.zeros((STEP, LANES), jnp.int32)
            breadth = jnp.ones((STEP, LANES), jnp.int32)
            for item, (start, size) in enumerate(item_spans(grids, items)):
                inside = (position >= start) & (position < start + size)
                origin = jnp.where(inside, start, origin)
                breadth = jnp.where(inside, grids[item, 1], breadth)
            local = (position - origin).astype(F32)
            breadth = breadth.astype(F32)
            down = jnp.floor((local + 0.5) / breadth)
            angles = jnp.where(lane < 2 * QUARTER, down, local - down * breadth) * frequency_ref[...]
            cos_ref[rows, :] = jnp.where(lane < HD, jnp.cos(angles), 0.0)
            sin_ref[rows, :] = jnp.where(lane < HD, jnp.sin(angles), 0.0)
            return carry

        lax.fori_loop(first, last, one, 0)

    steps = 2 * half // STEP
    tables(0, steps // 3)
    copies[0].wait_recv()
    for position in range(dp // 4):
        out_1[at(position), :] = flat[rows_of(dp // 4 + position), :] + in_0[at(dp // 4 + position), :]
    copies.append(halving(1, out_1, in_1))
    for position in range(dp // 4):
        keep_1[at(position), :] = flat[rows_of(position), :] + in_0[at(position), :]
    tables(steps // 3, 2 * steps // 3)
    copies[1].wait_recv()
    for position in range(dp // 8):
        later = at(dp // 8 + position)
        out_2[at(position), :] = keep_1[later, :] + in_1[later, :]
    copies.append(halving(2, out_2, in_2))
    for position in range(dp // 8):
        keep_2[at(position), :] = keep_1[at(position), :] + in_1[at(position), :]
    tables(2 * steps // 3, steps)
    copies[2].wait_recv()
    out_3[...] = keep_2[at(1), :] + in_2[at(1), :]
    copies.append(halving(3, out_3, in_3))
    copies[3].wait_recv()
    halves[ten] = keep_2[at(0), :] + in_2[at(0), :] + in_3[...]
    mod_copy = remote(halves.at[ten], halves.at[ten], y_sems.at[0, 1], y_sems.at[1, 1], y_peer)
    mod_copy.start()
    mod_ref[...] = jnp.zeros_like(mod_ref)
    remote(
        halves.at[1 - ten], halves.at[1 - ten], y_sems.at[0, 1], y_sems.at[1, 1], y_peer
    ).wait_recv()
    for side in range(2):
        for item in range(items):
            for group in range(groups):
                first = (side * groups + group) * LANES
                row = item * span + group
                mod_ref[item : item + 1, first : first + LANES] = halves[side, row : row + 1, :]
    tokens_copy.wait_recv()
    for copy in cond_copies + copies + [tokens_copy, mod_copy]:
        copy.wait_send()


def head(dp, conditions, mod_weight, tokens, grids, frequency):
    half, width = tokens.shape
    items = conditions.shape[0]
    count = dp * items
    groups = mod_weight.shape[1] // LANES // 2
    span = -(-groups // 8) * 8
    block = items * span
    vmem = pltpu.VMEM
    dma = pltpu.SemaphoreType.DMA
    in_vmem = pl.BlockSpec(memory_space=pltpu.VMEM)
    return pl.pallas_call(
        functools.partial(head_kernel, dp),
        out_shape=[
            jax.ShapeDtypeStruct((8, 6 * width), F32),
            jax.ShapeDtypeStruct((count, LANES), BF16),
            jax.ShapeDtypeStruct((2 * half, width), BF16),
            jax.ShapeDtypeStruct((2 * half, LANES), F32),
            jax.ShapeDtypeStruct((2 * half, LANES), F32),
        ],
        in_specs=[in_vmem] * 3 + [pl.BlockSpec(memory_space=pltpu.SMEM), in_vmem],
        out_specs=[in_vmem] * 5,
        scratch_shapes=[
            vmem((dp, 8, LANES), F32),
            vmem((dp, 8, LANES), F32),
            vmem((count, LANES), F32),
            vmem(((count + 1) * span, LANES), F32),
            vmem((dp // 2 * block, LANES), F32),
            vmem((dp // 2 * block, LANES), F32),
            vmem((dp // 4 * block, LANES), F32),
            vmem((dp // 4 * block, LANES), F32),
            vmem((dp // 4 * block, LANES), F32),
            vmem((dp // 8 * block, LANES), F32),
            vmem((dp // 8 * block, LANES), F32),
            vmem((dp // 8 * block, LANES), F32),
            vmem((block, LANES), F32),
            vmem((block, LANES), F32),
            vmem((2, block, LANES), F32),
            dma((dp,)),
            dma((dp,)),
            dma((2, 4)),
            dma((2, 2)),
        ],
        compiler_params=pltpu.CompilerParams(
            collective_id=3, has_side_effects=True, vmem_limit_bytes=62 * 2**20
        ),
        cost_estimate=pl.CostEstimate(
            flops=2 * count * width // dp * 6 * width, bytes_accessed=8 * 2**20, transcendentals=0
        ),
        name="head",
    )(conditions, mod_weight, tokens, grids, frequency)


def middle_kernel(
    items,
    chunk,
    step,
    heads_ref,
    proj_ref,
    tokens_ref,
    own_grad_ref,
    other_grad_ref,
    grids,
    mod_ref,
    gate_hbm,
    up_hbm,
    down_hbm,
    grad_heads_ref,
    grad_attn_ref,
    grad_resid_ref,
    resid_ref,
    early_sum_ref,
    mlp_other_ref,
    mlp_own_ref,
    last_keep_ref,
    last_out_ref,
    paired_keep_ref,
    paired_out_ref,
    gate_ref,
    up_ref,
    down_ref,
    attn,
    grad_mlp,
    mlp_in,
    hidden,
    grad_gate,
    grad_up,
    y_out,
    y_in,
    part,
    core_out,
    core_keep,
    core_in,
    x_out,
    x_in,
    x_keep,
    z_in,
    early_ref,
    early_rows,
    early_out,
    early_in,
    y_sems,
    core_sems,
    x_sems,
    z_sems,
    load_sems,
):
    dp = lax.axis_size("dp")
    bits = dp.bit_length() - 1
    me = lax.axis_index("dp")
    ten = lax.axis_index("tensor")
    half, width = tokens_ref.shape
    depth = width // dp
    units = gate_ref.shape[1]
    piece = part.shape[1]
    per_weight = units // piece
    chunks = half // chunk
    y_peer = (me, 1 - ten)
    core_peer = (across(me, 0), ten)
    x_peer = (across(me, 1), ten)
    z_peer = (across(me, 2), ten)
    loads = [
        pltpu.make_async_copy(source, there, load_sems.at[which])
        for which, (source, there) in enumerate(
            ((gate_hbm, gate_ref), (up_hbm, up_ref), (down_hbm, down_ref))
        )
    ]
    for load in loads:
        load.start()
    greet([y_peer, core_peer, x_peer, z_peer])

    def rows_at(first, count=chunk):
        return pl.ds(pl.multiple_of(first, 16), count)

    def y_copy(kind, c, src, dst):
        return remote(
            src, dst, y_sems.at[0, kind, c], y_sems.at[1, kind, c], y_peer
        )

    def item_at(first_token, rows):
        return item_of(grids, items, first_token + rows.start)

    def in_steps(c, body):
        def one(index, carry):
            body(pl.ds(pl.multiple_of(c * chunk + index * step, step), step))
            return carry

        lax.fori_loop(0, chunk // step, one, 0, unroll=UNROLL)

    proj_copies = []
    for c in range(chunks):
        rows = pl.ds(c * chunk, chunk)
        y_out[rows, :] = dot(
            heads_ref[rows_at((1 - ten) * half + c * chunk), :], proj_ref[...]
        ).astype(BF16)
        proj_copies.append(y_copy(0, c, y_out.at[rows, :], y_in.at[rows, :]))
        proj_copies[c].start()
    for c in range(chunks):
        attn[pl.ds(c * chunk, chunk), :] = dot(
            heads_ref[rows_at(ten * half + c * chunk), :], proj_ref[...]
        )
    for c in range(chunks):

        def scale_grads(rows):
            later = pl.ds(pl.multiple_of(rows.start + half, step), step)
            grad_mlp[rows, :] = (
                mod_values(item_at(ten * half, rows), mod_ref, 5) * own_grad_ref[rows, :].astype(F32)
            ).astype(BF16)
            grad_mlp[later, :] = (
                mod_values(item_at((1 - ten) * half, rows), mod_ref, 5)
                * other_grad_ref[rows, :].astype(F32)
            ).astype(BF16)

        in_steps(c, scale_grads)

    for load in loads:
        load.wait()

    def mlp(c):
        rows = pl.ds(c * chunk, chunk)
        for first in range(0, units, 256):
            columns = pl.ds(first, 256)
            gate = dot(mlp_in[rows, :], gate_ref[:, columns])
            up = dot(mlp_in[rows, :], up_ref[:, columns])
            grad = dot_t(grad_mlp[rows, :], down_ref[columns, :])
            sigma = 1.0 / (1.0 + jnp.exp(-gate))
            silu = gate * sigma
            hidden[rows, columns] = (silu * up).astype(BF16)
            grad_gate[rows, columns] = (
                grad * up * (sigma * (1.0 + gate * (1.0 - sigma)))
            ).astype(BF16)
            grad_up[rows, columns] = (grad * silu).astype(BF16)

    mlp_copies = []
    for c in range(chunks):
        proj_copies[c].wait_recv()

        def norm(rows):
            mixed = attn[rows, :] + y_in[rows, :].astype(F32)
            attn[rows, :] = mixed
            item = item_at(ten * half, rows)
            resid = tokens_ref[rows, :].astype(F32) + mod_values(item, mod_ref, 2) * mixed
            resid_ref[rows, :] = resid
            normed, _ = layer_norm(resid)
            mlp_in[rows, :] = (
                normed * (1.0 + mod_values(item, mod_ref, 4)) + mod_values(item, mod_ref, 3)
            ).astype(BF16)

        in_steps(c, norm)
        mlp_copies.append(
            y_copy(
                1, c, mlp_in.at[pl.ds(c * chunk, chunk), :], mlp_in.at[pl.ds(half + c * chunk, chunk), :]
            )
        )
        mlp_copies[c].start()
    for c in range(chunks):
        mlp(c)

    def back(first):
        rows = pl.ds(first, chunk)
        return dot_t(grad_gate[rows, :], gate_ref[...]) + dot_t(grad_up[rows, :], up_ref[...])

    back_copies = []
    for c in range(chunks):
        mlp_copies[c].wait_recv()
        mlp(chunks + c)
        rows = pl.ds(c * chunk, chunk)
        proj_copies[c].wait_send()
        y_out[rows, :] = back(half + c * chunk).astype(BF16)
        back_copies.append(y_copy(2, c, y_out.at[rows, :], y_in.at[rows, :]))
        back_copies[c].start()

    orders = [(0, 2, 1, 3) if p % 2 and p < 2 * per_weight else (0, 1, 2, 3) for p in range(6)]

    def packed(position, order):
        def rows_of(p):
            return part[pl.ds(pl.multiple_of(block_at(p, me, order) * depth, 8), depth), :]

        return jnp.concatenate([rows_of(position), rows_of(position + 1)]).astype(BF16)

    core_copies = []
    x_copies = []

    def weight_grad(p):
        which, column = divmod(p, per_weight)
        columns = pl.ds(column * piece, piece)
        left, right = ((grad_mlp, hidden), (mlp_in, grad_gate), (mlp_in, grad_up))[which]
        slot = p % 2
        for first in range(0, width, LANES):
            rows = pl.ds(first, LANES)
            part[rows, :] = t_dot(left[:, rows], right[:, columns])
        if p >= 2:
            core_copies[p - 2].wait_send()
        for position in range(0, dp // 2, 2):
            rows = pl.ds(position * depth, 2 * depth)
            core_out[slot, rows, :] = packed(dp // 2 + position, orders[p])
        core_copies.append(
            remote(
                core_out.at[slot], core_in.at[p], core_sems.at[0, p], core_sems.at[1, p], core_peer
            )
        )
        core_copies[p].start()
        for position in range(0, dp // 2, 2):
            rows = pl.ds(position * depth, 2 * depth)
            core_keep[slot, rows, :] = packed(position, orders[p])

    quarter = width // 4

    def cross(p):
        slot = p % 2
        core_copies[p].wait_recv()

        def total(rows):
            return (core_keep[slot, rows, :].astype(F32) + core_in[p, rows, :].astype(F32)).astype(
                BF16
            )

        if p < 2 * per_weight:
            x_out[p] = total(pl.ds(quarter, quarter))
            x_copies.append(
                remote(
                    x_out.at[p],
                    x_in.at[p],
                    x_sems.at[0, p],
                    x_sems.at[1, p],
                    (across(me, orders[p][1]), ten),
                )
            )
            x_copies[p].start()
            x_keep[p] = total(pl.ds(0, quarter))
        else:
            paired_keep_ref[p - 2 * per_weight] = total(pl.ds(0, quarter))
            paired_out_ref[p - 2 * per_weight] = total(pl.ds(quarter, quarter))

    eighth = width // 8
    z_copies = []

    def ascend(p):
        x_copies[p].wait_recv()
        x_copies[p].wait_send()
        rows = pl.ds(eighth, eighth)
        z_out = x_out.at[p, pl.ds(0, eighth), :]
        x_out[p, :eighth, :] = (
            x_keep[p, rows, :].astype(F32) + x_in[p, rows, :].astype(F32)
        ).astype(BF16)
        next_peer = (across(me, orders[p][2]), ten)
        z_copies.append(remote(z_out, z_in.at[p], z_sems.at[0, p], z_sems.at[1, p], next_peer))
        z_copies[p].start()

    pieces = 3 * per_weight
    weight_grad(0)
    weight_grad(1)
    cross(0)
    for c in range(chunks):
        grad_resid_ref[pl.ds(c * chunk, chunk), :] = back(c * chunk)

    early_ref[...] = jnp.zeros_like(early_ref)
    grad_copies = []
    for c in range(chunks):
        back_copies[c].wait_recv()

        def norm_grad(rows):
            grad = grad_resid_ref[rows, :] + y_in[rows, :].astype(F32)
            normed, inv = layer_norm(resid_ref[rows, :])
            item = item_at(ten * half, rows)
            n = grad * (1.0 + mod_values(item, mod_ref, 4))
            grad_resid = own_grad_ref[rows, :].astype(F32) + norm_back(n, normed, inv)
            grad_resid_ref[rows, :] = grad_resid
            there = pl.ds(pl.multiple_of(rows.start + ten * half, step), step)
            grad_attn_ref[there, :] = (mod_values(item, mod_ref, 2) * grad_resid).astype(BF16)
            for kind, values in enumerate((grad_resid * attn[rows, :], grad, grad * normed)):
                lanes = slice(kind * width, (kind + 1) * width)
                add_rows(early_ref, item, items, values, lanes)

        in_steps(c, norm_grad)
        rows = rows_at(ten * half + c * chunk)
        grad_copies.append(y_copy(3, c, grad_attn_ref.at[rows, :], grad_attn_ref.at[rows, :]))
        grad_copies[c].start()
        weight_grad(2 + c)
        cross(1 + c)

    pack_rows(early_rows, items, [(early_ref, 0), (early_ref, 1), (early_ref, 2)])
    early_out[...] = early_rows[...].astype(BF16)
    early_copy = y_copy(4, 0, early_out, early_in)
    early_copy.start()

    weight_grad(4)
    cross(3)
    ascend(0)
    weight_grad(5)
    cross(4)
    ascend(1)
    for c in range(chunks):
        rows = pl.ds(c * chunk, chunk)
        mlp_other_ref[rows, :] = dot(
            hidden[pl.ds(half + c * chunk, chunk), :], down_ref[...]
        ).astype(BF16)
        mlp_own_ref[rows, :] = dot(hidden[rows, :], down_ref[...])
        own_rows = rows_at(ten * half + c * chunk)
        grad_heads_ref[own_rows, :] = dot_t(grad_attn_ref[own_rows, :], proj_ref[...]).astype(BF16)
    cross(5)
    ascend(2)
    for c in range(chunks):
        rows = rows_at((1 - ten) * half + c * chunk)
        y_copy(3, c, grad_attn_ref.at[rows, :], grad_attn_ref.at[rows, :]).wait_recv()
        grad_heads_ref[rows, :] = dot_t(grad_attn_ref[rows, :], proj_ref[...]).astype(BF16)
    early_copy.wait_recv()
    early_sum_ref[...] = (early_out[...].astype(F32) + early_in[...].astype(F32)).astype(BF16)
    ascend(3)
    for p in range(2 * per_weight):
        z_copies[p].wait_recv()
        total = (
            x_keep[p, :eighth, :].astype(F32)
            + x_in[p, :eighth, :].astype(F32)
            + z_in[p].astype(F32)
        )
        last_keep_ref[p] = total[:depth].astype(BF16)
        last_out_ref[p] = total[depth:].astype(BF16)
    for copy in mlp_copies + back_copies + grad_copies + core_copies[-2:] + z_copies + [early_copy]:
        copy.wait_send()


def middle(heads_out, proj, tokens, own_grad, other_grad, grids, mod, gate, up, down):
    half, width = tokens.shape
    length = 2 * half
    units = gate.shape[1]
    inner = heads_out.shape[1]
    items = grids.shape[0]
    dp = lax.axis_size("dp")
    early_rows = items * group_rows(3 * width // LANES)
    chunk = half // 2
    chunks = half // chunk
    piece = units // 2
    pieces = 6
    vmem = pltpu.VMEM
    dma = pltpu.SemaphoreType.DMA
    anywhere = pl.BlockSpec(memory_space=pl.ANY)
    return pl.pallas_call(
        functools.partial(middle_kernel, items, chunk, STEP),
        out_shape=[
            jax.ShapeDtypeStruct((length, inner), BF16),
            jax.ShapeDtypeStruct((length, width), BF16),
            jax.ShapeDtypeStruct((half, width), F32),
            jax.ShapeDtypeStruct((half, width), F32),
            jax.ShapeDtypeStruct((early_rows, LANES), BF16),
            jax.ShapeDtypeStruct((half, width), BF16),
            jax.ShapeDtypeStruct((half, width), F32),
            jax.ShapeDtypeStruct((4, width // dp, piece), BF16),
            jax.ShapeDtypeStruct((4, width // dp, piece), BF16),
            jax.ShapeDtypeStruct((2, width // 4, piece), BF16),
            jax.ShapeDtypeStruct((2, width // 4, piece), BF16),
        ],
        in_specs=[pl.BlockSpec(memory_space=pltpu.VMEM)] * 5
        + [pl.BlockSpec(memory_space=pltpu.SMEM), pl.BlockSpec(memory_space=pltpu.VMEM)]
        + [anywhere] * 3,
        out_specs=[pl.BlockSpec(memory_space=pltpu.VMEM)] * 11,
        scratch_shapes=[
            vmem((width, units), BF16),
            vmem((width, units), BF16),
            vmem((units, width), BF16),
            vmem((half, width), F32),
            vmem((length, width), BF16),
            vmem((length, width), BF16),
            vmem((length, units), BF16),
            vmem((length, units), BF16),
            vmem((length, units), BF16),
            vmem((half, width), BF16),
            vmem((half, width), BF16),
            vmem((width, piece), F32),
            vmem((2, width // 2, piece), BF16),
            vmem((2, width // 2, piece), BF16),
            vmem((pieces, width // 2, piece), BF16),
            vmem((4, width // 4, piece), BF16),
            vmem((4, width // 4, piece), BF16),
            vmem((4, width // 4, piece), BF16),
            vmem((4, width // 8, piece), BF16),
            vmem((8, 3 * width), F32),
            vmem((early_rows, LANES), F32),
            vmem((early_rows, LANES), BF16),
            vmem((early_rows, LANES), BF16),
            dma((2, 5, chunks)),
            dma((2, pieces)),
            dma((2, 4)),
            dma((2, 4)),
            dma((3,)),
        ],
        compiler_params=pltpu.CompilerParams(
            collective_id=2, has_side_effects=True, vmem_limit_bytes=62 * 2**20
        ),
        cost_estimate=pl.CostEstimate(
            flops=18 * length * width * units, bytes_accessed=30 * 2**20, transcendentals=0
        ),
        name="middle",
    )(heads_out, proj, tokens, own_grad, other_grad, grids, mod, gate, up, down)


def shards_in_kernels(
    tokens,
    conditions,
    item_grids,
    mod_weight,
    query_weight,
    key_weight,
    value_weight,
    proj_weight,
    query_gain,
    key_gain,
    gate_weight,
    up_weight,
    down_weight,
    out_grad,
):
    half, width = tokens.shape
    dp = lax.axis_size("dp")
    items = conditions.shape[0]
    owned = mod_weight.shape[0]
    grids = item_grids
    lane = np.arange(LANES)
    frequency = jnp.asarray(
        (10000.0 ** (-(lane % QUARTER) / QUARTER)).astype(np.float32)[None, :]
    )
    mod, mod_in_own, tokens_all, cosine, sine = head(
        dp, conditions, mod_weight, tokens, grids, frequency
    )
    out_grad_later, mod = lax.optimization_barrier((out_grad, mod))
    out_grad_other = swap(out_grad_later)
    gain_q = query_gain[None, :]
    gain_k = key_gain[None, :]
    weights = (query_weight.T, key_weight.T, value_weight.T)
    attn_in, heads_out, *saved = attend(
        grids, tokens_all, mod, *weights, gain_q, gain_k, cosine, sine
    )
    (
        grad_heads,
        grad_attn_all,
        grad_resid,
        resid,
        early,
        mlp_other,
        mlp_own,
        last_keep,
        last_out,
        paired_keep,
        paired_out,
    ) = middle(
        heads_out,
        proj_weight,
        tokens,
        out_grad,
        out_grad_other,
        grids,
        mod,
        gate_weight,
        up_weight,
        down_weight,
    )
    mlp_recv = swap(mlp_other)
    last_in = lax.ppermute(last_out, "dp", partners(3))
    paired_in = lax.ppermute(paired_out, "dp", partners(1))
    *d, gain_parts = attend_back(grids, grad_heads, saved, gain_q, gain_k, cosine, sine)
    grad_tokens, block_out, sums, grad_mod_all, gain_sums, grad_cond = tail(
        dp,
        d,
        attn_in,
        grad_attn_all,
        heads_out,
        paired_keep,
        paired_in,
        early,
        gain_parts,
        mod,
        conditions,
        grids,
        weights,
        tokens,
        out_grad,
        grad_resid,
        resid,
        mlp_own,
        mlp_recv,
        mod_weight,
    )
    last = last_keep.astype(F32) + last_in.astype(F32)
    grad_mod_weight = t_dot(mod_in_own[:, :owned], grad_mod_all)
    attn_sum = jnp.concatenate(list(sums[2:]), axis=1)
    inner = heads_out.shape[1]
    grad_q, grad_k, grad_v, grad_proj = (
        attn_sum[:, which * inner : (which + 1) * inner] for which in range(4)
    )
    return (
        block_out,
        grad_tokens,
        grad_cond[:items],
        grad_mod_weight,
        grad_q,
        grad_k,
        grad_v,
        grad_proj.T,
        gain_sums[0, :HD],
        gain_sums[1, :HD],
        jnp.concatenate([last[2], last[3]], axis=1),
        jnp.concatenate(list(sums[:2]), axis=1),
        jnp.concatenate([last[0], last[1]], axis=1).T,
    )


def shards(
    tokens,
    conditions,
    item_grids,
    mod_weight,
    query_weight,
    key_weight,
    value_weight,
    proj_weight,
    query_gain,
    key_gain,
    gate_weight,
    up_weight,
    down_weight,
    out_grad,
):
    half, width = tokens.shape
    length = 2 * half
    dp = lax.axis_size("dp")
    bits = dp.bit_length() - 1
    me = lax.axis_index("dp")
    second = lax.axis_index("tensor") == 1
    own_first = lax.axis_index("tensor") * half
    other_first = half - own_first
    items = conditions.shape[0]
    owned = mod_weight.shape[0]

    tokens_other = swap(tokens)
    out_grad_other = swap(out_grad)

    member, row_pos, col_pos = geometry(item_grids, length)
    cosine, sine = rope_tables(row_pos, col_pos)
    gain_q = query_gain[None, :]
    gain_k = key_gain[None, :]
    member_own = lax.dynamic_slice_in_dim(member, own_first, half, 0)
    member_other = lax.dynamic_slice_in_dim(member, other_first, half, 0)

    cond_all = lax.all_gather(conditions, "dp", axis=0, tiled=True)
    mod_in_all = jax.nn.silu(cond_all.astype(F32)).astype(BF16)
    mod_in_own = lax.dynamic_slice_in_dim(mod_in_all, me * owned, owned, 1)
    mod_part = dot(mod_in_own, mod_weight)
    mod_parts = lax.all_to_all(
        mod_part.reshape(dp, items, 6 * width), "dp", split_axis=0, concat_axis=0, tiled=True
    )
    modulation = jnp.sum(mod_parts.astype(F32), axis=0)
    shift_one, scale_one, gate_one, shift_two, scale_two, gate_two = jnp.split(
        modulation, 6, axis=1
    )

    tokens_float = tokens.astype(F32)
    tokens_all = in_order(tokens, tokens_other, second)

    w_qkv = jnp.concatenate([query_weight, key_weight, value_weight], axis=1)
    mod = jnp.pad(modulation, ((0, 8 - items), (0, 0)))
    attn_in, heads_out, *saved = attend(
        item_grids,
        tokens_all,
        mod,
        query_weight.T,
        key_weight.T,
        value_weight.T,
        gain_q,
        gain_k,
        cosine,
        sine,
    )
    inner = heads_out.shape[1]
    grad_out = out_grad.astype(F32)
    gate_two_own = per_token(member_own, gate_two)

    heads_other = lax.dynamic_slice_in_dim(heads_out, other_first, half, 0)
    heads_own = lax.dynamic_slice_in_dim(heads_out, own_first, half, 0)
    attn_recv = swap(dot(heads_other, proj_weight).astype(BF16))
    attn_out = dot(heads_own, proj_weight) + attn_recv.astype(F32)

    gate_one_own = per_token(member_own, gate_one)
    scale_two_own = per_token(member_own, scale_two)
    resid = tokens_float + gate_one_own * attn_out
    norm_two, inv_two = layer_norm(resid)
    mlp_in = (norm_two * (1.0 + scale_two_own) + per_token(member_own, shift_two)).astype(BF16)
    mlp_in_all = jnp.concatenate([mlp_in, swap(mlp_in)])

    grad_mlp_all = jnp.concatenate(
        [
            (gate_two_own * grad_out).astype(BF16),
            (per_token(member_other, gate_two) * out_grad_other.astype(F32)).astype(BF16),
        ]
    )
    grad_hidden = dot_t(grad_mlp_all, down_weight)

    gate_pre = dot(mlp_in_all, gate_weight)
    up_pre = dot(mlp_in_all, up_weight)
    silu_gate = jax.nn.silu(gate_pre)
    hidden = (silu_gate * up_pre).astype(BF16)
    grad_gate_pre = (grad_hidden * up_pre * silu_grad(gate_pre)).astype(BF16)
    grad_up_pre = (grad_hidden * silu_gate).astype(BF16)

    back_other = dot_t(grad_gate_pre[half:], gate_weight) + dot_t(grad_up_pre[half:], up_weight)
    back_recv = swap(back_other.astype(BF16))
    mlp_recv = swap(dot(hidden[half:], down_weight).astype(BF16))
    grad_mlp_in = (
        dot_t(grad_gate_pre[:half], gate_weight)
        + dot_t(grad_up_pre[:half], up_weight)
        + back_recv.astype(F32)
    )

    grad_mlp_rows = halving_rows(grad_mlp_all, bits)
    mlp_in_rows = halving_rows(mlp_in_all, bits)
    down_part = first_halving(grad_mlp_rows, hidden)
    gate_part = first_halving(mlp_in_rows, grad_gate_pre)
    up_part = first_halving(mlp_in_rows, grad_up_pre)

    mlp_out = dot(hidden[:half], down_weight) + mlp_recv.astype(F32)
    block_out = (resid + gate_two_own * mlp_out).astype(BF16)

    grad_resid = grad_out + norm_back(grad_mlp_in * (1.0 + scale_two_own), norm_two, inv_two)
    grad_attn = (gate_one_own * grad_resid).astype(BF16)
    grad_attn_all = in_order(grad_attn, swap(grad_attn), second)
    grad_heads = dot_t(grad_attn_all, proj_weight).astype(BF16)
    grad_heads, down_part, gate_part, up_part = lax.optimization_barrier(
        (grad_heads, down_part, gate_part, up_part)
    )
    grad_down = rest_of_halving(down_part, bits).T
    grad_gate = rest_of_halving(gate_part, bits)
    grad_up = rest_of_halving(up_part, bits)
    *d, gain_parts = attend_back(item_grids, grad_heads, saved, gain_q, gain_k, cosine, sine)

    d = jnp.concatenate(d, axis=1)
    early = jnp.concatenate(
        [
            per_item(member_own, grad_resid * attn_out),
            per_item(member_own, grad_mlp_in),
            per_item(member_own, grad_mlp_in * norm_two),
            per_item(member_own, grad_out * mlp_out),
        ],
        axis=1,
    )
    def attn_back(first):
        return dot_t(lax.dynamic_slice_in_dim(d, first, half, 0), w_qkv)

    attn_back_recv = swap(attn_back(other_first).astype(BF16))
    grad_attn_in = attn_back(own_first) + attn_back_recv.astype(F32)
    attn_sum = rest_of_halving(
        jnp.concatenate(
            [
                first_halving(halving_rows(attn_in, bits), d),
                first_halving(halving_rows(grad_attn_all, bits), heads_out),
            ],
            axis=1,
        ),
        bits,
    )
    norm_one, inv_one = layer_norm(tokens_float)
    scale_one_own = per_token(member_own, scale_one)
    grad_tokens = (
        grad_resid + norm_back(grad_attn_in * (1.0 + scale_one_own), norm_one, inv_one)
    ).astype(BF16)
    part_mod = jnp.concatenate(
        [per_item(member_own, grad_attn_in), per_item(member_own, grad_attn_in * norm_one), early],
        axis=1,
    )
    gains = jnp.pad(gain_parts[:2].reshape(1, 2 * LANES), ((0, 0), (0, 6 * width - 2 * LANES)))
    part_small = jnp.concatenate([part_mod, gains]).astype(BF16)
    small = part_small.astype(F32) + swap(part_small).astype(F32)
    small_all = lax.all_gather(small.astype(BF16), "dp", axis=0, tiled=False)
    grad_mod_all = small_all[:, :items].reshape(dp * items, 6 * width)
    gain_sums = jnp.sum(small_all[:, items, : 2 * LANES].astype(F32), axis=0).reshape(2, LANES)
    cond_parts = lax.all_to_all(
        dot_t(grad_mod_all, mod_weight).reshape(dp, items, owned),
        "dp",
        split_axis=0,
        concat_axis=0,
        tiled=True,
    )

    grad_mod_weight = t_dot(mod_in_own, grad_mod_all)
    grad_mod_in = cond_parts.transpose(1, 0, 2).reshape(items, dp * owned)
    grad_conditions = silu_grad(conditions.astype(F32)) * grad_mod_in
    grad_q, grad_k, grad_v, grad_proj = (
        attn_sum[:, which * inner : (which + 1) * inner] for which in range(4)
    )
    return (
        block_out,
        grad_tokens,
        grad_conditions,
        grad_mod_weight,
        grad_q,
        grad_k,
        grad_v,
        grad_proj.T,
        gain_sums[0, :HD],
        gain_sums[1, :HD],
        grad_gate,
        grad_up,
        grad_down,
    )


def solution(mesh):
    tokens = P(("dp", "tensor"), None)
    rows = P("dp", None)
    columns = P(None, "tensor")
    inner = P("tensor", None)
    both = P("dp", "tensor")
    turned = P("tensor", "dp")
    in_kernels = mesh.shape["dp"] == 16
    return jax.shard_map(
        shards_in_kernels if in_kernels else shards,
        mesh=mesh,
        in_specs=(
            tokens,
            rows,
            rows,
            rows,
            columns,
            columns,
            columns,
            inner,
            P(),
            P(),
            columns,
            columns,
            inner,
            tokens,
        ),
        out_specs=(
            tokens,
            tokens,
            rows,
            rows,
            both,
            both,
            both,
            turned,
            P(),
            P(),
            both,
            both,
            turned,
        ),
        check_vma=False,
    )
```
